128 devices in a mesh: gx: 16 (over y_hi, z, core), gy: 8 (over y_lo, x).
Axes of the slice: x: 4, y: 4 (y_hi: 2, y_lo: 2; y = y_hi * 2 + y_lo), z: 4, core: 2. Of those that a mesh axis runs over, the one named last changes fastest.
Arguments:
- flow_pops: float32 [19, 512, 16384], P(None, 'gx', 'gy'), may hold values from 0 to 1, as said below
- heat_pops: float32 [7, 512, 16384], P(None, 'gx', 'gy'), may hold values from 0 to 1, as said below
- solid_flag: int32 [512, 16384], P('gx', 'gy'), may hold values 0 or 1
- brick_temp: float32 [256, 512], P(('gx', 'gy')), may hold values from 2 to 6
- brick_ids: int32 [256], replicated, may hold values from 0 to 255, each once
- brick_links: int32 [256, 6], replicated, may hold values from -1 to 255, as said below
- face_cell: int32 [131072], replicated, may hold values from 0 to 65535
- face_owner: int32 [131072, 1], replicated, may hold values from 0 to 127; in each aligned block of 1024 rows (0 to 1023, 1024 to 2047, ...) at most 16 rows name the same one
- face_spot: int32 [131072], replicated, may hold values from 0 to 1023
Outputs:
- flow_out: float32 [19, 512, 16384], P(None, 'gx', 'gy')
- heat_out: float32 [7, 512, 16384], P(None, 'gx', 'gy')
- brick_out: float32 [256, 512], P(('gx', 'gy'))
The draws below stay inside these ranges and needn't reach their ends.
Inputs may be any that keep to these rules, and one draw needn't show every extreme that they name: `flow_pops`: each population f_i is its lattice weight times a factor within 0.55 to 1.45. `heat_pops`: each population g_j is its lattice weight times a factor within 0.3 to 1.7. `brick_ids`: A permutation of the brick numbers. `brick_links`: -1 marks a side with no neighbour; links are mutual: if a names b on side s, b names a on the other side of that axis. `face_owner`: among the 1024 faces of one fluid device, no device is named more than 16 times.
All inputs are finite; a program needn't handle non-finite values. No bound on the sum of `solid_flag` on one device may be relied on, other than what follows from the above.
Results may differ from the reference program's by a relative error of at most 0.0003.
Values sent between devices are 32-bit elements; how exact they have to be, the bound alone decides.
A program may use at most 192 MiB of HBM per device.

```python
import math
import jax
import jax.numpy as jnp
import numpy as np

CX = 32
CY = 64
NZ = 32
STEPS = 2
BPD = 2
BE = 8
W = 1024
CAP = 16
NX = 512
NY = 512
BRICKS = 256
FACES = 131072
N_GY = 8
DEVICES = 128


WEIGHTS_FLOW = [1.0 / 3.0] + [1.0 / 18.0] * 6 + [1.0 / 36.0] * 12


WEIGHTS_HEAT = [0.25] + [0.125] * 6


def draw_flow_pops(key, part):
    key = jax.random.fold_in(key, 5)
    weights = jnp.array(WEIGHTS_FLOW, jnp.float32).reshape(19, 1, 1)
    factor = jax.random.uniform(key, (19, NX, NY * NZ), jnp.float32, 0.7, 1.3)
    return weights * factor


def draw_heat_pops(key, part):
    key = jax.random.fold_in(key, 7)
    weights = jnp.array(WEIGHTS_HEAT, jnp.float32).reshape(7, 1, 1)
    factor = jax.random.uniform(key, (7, NX, NY * NZ), jnp.float32, 0.5, 1.5)
    return weights * factor


def draw_brick_links(key, part):
    key = jax.random.fold_in(key, 11)
    layers = BRICKS // 16
    present = jax.random.randint(key, (BRICKS, 3), 0, 4) < 3
    present = present.at[:, 2].set(True)
    index = jnp.arange(BRICKS, dtype=jnp.int32)
    coords = [index // 16, index // 4 % 4, index % 4]
    strides = [16, 4, 1]
    limits = [layers, 4, 4]
    columns = []
    for d in range(3):
        low_ok = coords[d] > 0
        low_id = jnp.where(low_ok, index - strides[d], 0)
        low_side = jnp.where(low_ok & present[low_id, d], low_id, -1)
        high_ok = coords[d] < limits[d] - 1
        high_side = jnp.where(high_ok & present[:, d], index + strides[d], -1)
        columns.append(low_side)
        columns.append(high_side)
    return jnp.stack(columns, axis=1).astype(jnp.int32)


def plant(result, rng, low, high):
    longest = result.shape.index(max(result.shape))
    spots = []
    for shift in (0, 1):
        where = [jax.random.randint(jax.random.fold_in(rng, axis), (), 0, length) for axis, length in enumerate(result.shape)]
        where[longest] = (where[longest] + shift) % result.shape[longest]
        spots.append(tuple(where))
    return result.at[spots[0]].set(low).at[spots[1]].set(high)


def level_of(stream_key, extent, pieces, low, largest):
    loudness, own = 1.0, jax.random.fold_in(stream_key, 6)
    for axis_at, blocks in pieces:
        draws = jnp.exp(jax.random.uniform(jax.random.fold_in(own, axis_at), (blocks,), jnp.float32, low / len(pieces), largest / len(pieces)))
        loudness = loudness * jnp.repeat(draws, extent[axis_at] // blocks).reshape([-1 if axis == axis_at else 1 for axis in range(len(extent))])
    return loudness


def shared_out(rng, own, number, rows, number_of, top, limit, slope):
    ranking = jax.random.permutation(rng, number_of)
    packed, usual = load_shares(number_of, rows * top, limit, slope, True), load_shares(number_of, rows * top, limit, slope, False)
    places = jnp.arange(number_of)

    def named(lengths, rotation):
        used = int((lengths > 0).sum())
        fixed = max(1, used // 4)
        passed = fixed + (places - fixed + rotation * (used - fixed)) % max(1, number_of - fixed)
        return jnp.zeros((number_of,), jnp.int32).at[ranking[jnp.where(places < fixed, places, passed)]].set(jnp.asarray(lengths, jnp.int32))

    lengths = jnp.where(number % 4 == 0, named(packed, number // 4), named(usual, number - number // 4 - 1))
    mixed = jax.random.permutation(jax.random.fold_in(own, 3), number_of)
    donor, receiver = mixed[0:number_of // 2 * 2:2], mixed[1:number_of // 2 * 2:2]
    room = jnp.minimum(lengths[donor] - 1, limit - lengths[receiver]) // 2
    room = jnp.where((donor == ranking[0]) | (receiver == ranking[0]) | (lengths[receiver] == 0), 0, jnp.maximum(room, 0))
    passed = jax.random.randint(jax.random.fold_in(own, 4), (number_of // 2,), 0, 1 << 20) % (room + 1)
    lengths = lengths.at[donor].add(-passed).at[receiver].add(passed)
    members = jnp.searchsorted(jnp.cumsum(lengths), jnp.arange(rows * top), side="right").astype(jnp.int32)
    listing = members.reshape(top, rows).T
    listing = listing[jax.random.permutation(jax.random.fold_in(own, 1), rows)]
    rotation = jax.random.randint(jax.random.fold_in(own, 2), (rows, 1), 0, top)
    return jnp.take_along_axis(listing, (jnp.arange(top)[None, :] + rotation) % top, axis=1)


def load_shares(count, total, reach, lean, full):
    portions = [(1 << 20) // math.isqrt(standing ** lean) + 1 for standing in range(1, count + 1)]
    largest = reach if full else min(reach, max(-(-total // count), total * portions[0] // sum(portions)))
    least = 1 if total - largest >= count - 1 else 0
    counts, rest = [largest] + [least] * (count - 1), total - largest - least * (count - 1)
    while rest > 0:
        candidates = [i for i in range(1, count) if counts[i] < largest] or [i for i in range(1, count) if counts[i] < reach]
        whole, remaining = sum([portions[i] for i in candidates]), rest
        for i in candidates:
            addition = min(reach - counts[i], max(1, remaining * portions[i] // whole), rest)
            counts[i] = counts[i] + addition
            rest = rest - addition
    return np.array(counts)


def setup_inputs(seed: int = 0) -> dict:
    streams_of = jax.random.split(jax.random.key(seed), 10)
    flow_pops = draw_flow_pops(jax.random.fold_in(streams_of[9], 71), 0)
    heat_pops = draw_heat_pops(jax.random.fold_in(streams_of[9], 71), 0)
    solid_flag = plant((jax.random.randint(streams_of[2], (NX, NY * NZ), 0, 4) < 1).astype(jnp.int32), jax.random.fold_in(streams_of[2], 1), 0, 1)
    brick_temp = jnp.clip(2.0 + 4.0 * jax.random.uniform(streams_of[3], (BRICKS, BE * BE * BE), jnp.float32) ** level_of(streams_of[3], (BRICKS, BE * BE * BE), ((0, 128),), -0.2, 0.2), 2.0, 6.0)
    brick_ids = jax.random.permutation(streams_of[4], BRICKS).astype(jnp.int32)
    brick_links = draw_brick_links(jax.random.fold_in(streams_of[9], 71), 0)
    face_cell = plant(jax.random.randint(streams_of[6], (FACES,), 0, CX * CY * NZ), jax.random.fold_in(streams_of[6], 1), 0, (CX * CY * NZ) - 1).astype(jnp.int32)
    face_owner_keys = jax.random.split(jax.random.fold_in(streams_of[7], 1), FACES // W)
    face_owner_turns = jax.random.permutation(jax.random.fold_in(streams_of[7], 3), FACES // W)
    face_owner = jax.vmap(lambda own, number: shared_out(jax.random.fold_in(streams_of[7], 2), own, number, W, DEVICES, 1, CAP, 2))(face_owner_keys, face_owner_turns).reshape((FACES, 1))
    face_spot = plant(jax.random.randint(streams_of[8], (FACES,), 0, BPD * BE * BE * BE), jax.random.fold_in(streams_of[8], 1), 0, (BPD * BE * BE * BE) - 1).astype(jnp.int32)
    return {"flow_pops": flow_pops, "heat_pops": heat_pops, "solid_flag": solid_flag, "brick_temp": brick_temp, "brick_ids": brick_ids, "brick_links": brick_links, "face_cell": face_cell, "face_owner": face_owner, "face_spot": face_spot}


VELOCITY = [(0, 0, 0), (1, 0, 0), (-1, 0, 0), (0, 1, 0), (0, -1, 0), (0, 0, 1), (0, 0, -1),
            (1, 1, 0), (-1, -1, 0), (1, -1, 0), (-1, 1, 0), (1, 0, 1), (-1, 0, -1), (1, 0, -1),
            (-1, 0, 1), (0, 1, 1), (0, -1, -1), (0, 1, -1), (0, -1, 1)]
OPPOSITE = [0, 2, 1, 4, 3, 6, 5, 8, 7, 10, 9, 12, 11, 14, 13, 16, 15, 18, 17]
WEIGHTS_FLOW = [1.0 / 3.0] + [1.0 / 18.0] * 6 + [1.0 / 36.0] * 12
WEIGHTS_HEAT = [0.25] + [0.125] * 6
SIDE_SWAP = [1, 0, 3, 2, 5, 4]
TAU_FLOW = 0.8
TAU_HEAT = 0.9
BUOYANCY = 0.002
HEAT_REF = 1.0
WALL_COEF = 0.1
BRICK_LOSS = 0.5
COND_BASE = 0.04
COND_SLOPE = 0.1
LATENT = 2.0
MELT = 4.0
MELT_WIDTH = 0.5


def dotted(vector, velocity):
    terms = [velocity[a] * vector[a] for a in range(3) if velocity[a] != 0]
    if not terms:
        return jnp.zeros_like(vector[0])
    return sum(terms[1:], terms[0])


def collide(flow_pops, heat_pops, solid_mask):
    density = jnp.sum(flow_pops, axis=0)
    momentum = [sum(VELOCITY[i][a] * flow_pops[i] for i in range(19) if VELOCITY[i][a] != 0) for a in range(3)]
    velocity = [m / density for m in momentum]
    fluid_temp = jnp.sum(heat_pops, axis=0)
    forcing = BUOYANCY * (fluid_temp - HEAT_REF)
    shifted = [velocity[0], velocity[1], velocity[2] + TAU_FLOW * forcing / density]
    speed_sq = shifted[0] * shifted[0] + shifted[1] * shifted[1] + shifted[2] * shifted[2]
    relaxed_flow = []
    for i in range(19):
        along = dotted(shifted, VELOCITY[i])
        equilibrium = WEIGHTS_FLOW[i] * density * (1.0 + 3.0 * along + 4.5 * along * along - 1.5 * speed_sq)
        relaxed = flow_pops[i] - (flow_pops[i] - equilibrium) / TAU_FLOW
        relaxed_flow.append(jnp.where(solid_mask, flow_pops[OPPOSITE[i]], relaxed))
    relaxed_heat = []
    for j in range(7):
        along = dotted(velocity, VELOCITY[j])
        equilibrium = WEIGHTS_HEAT[j] * fluid_temp * (1.0 + 4.0 * along)
        relaxed = heat_pops[j] - (heat_pops[j] - equilibrium) / TAU_HEAT
        relaxed_heat.append(jnp.where(solid_mask, heat_pops[OPPOSITE[j]], relaxed))
    return jnp.stack(relaxed_flow), jnp.stack(relaxed_heat), fluid_temp


def propagate(padded, velocities):
    row_count = padded.shape[1] - 2
    col_count = padded.shape[2] - 2
    deep = jnp.pad(padded, ((0, 0), (0, 0), (0, 0), (1, 1)))
    layer_count = deep.shape[3] - 2
    return jnp.stack([deep[i, 1 - v[0]:1 - v[0] + row_count, 1 - v[1]:1 - v[1] + col_count,
                           1 - v[2]:1 - v[2] + layer_count] for i, v in enumerate(velocities)])


def brick_faces(bricks):
    count = bricks.shape[0]
    cube = bricks.reshape(count, BE, BE, BE)
    layers = [cube[:, 0], cube[:, -1], cube[:, :, 0], cube[:, :, -1], cube[:, :, :, 0], cube[:, :, :, -1]]
    return jnp.stack(layers, axis=1).reshape(count, 6, BE * BE)


def fill_ghosts(every_face, own_faces, link_slot, linked):
    swap = jnp.array(SIDE_SWAP, jnp.int32)
    remote = every_face[link_slot, swap[None, :]]
    return jnp.where(linked[:, :, None], remote, own_faces)


def conduct(bricks, ghost, loss):
    count = bricks.shape[0]
    cube = bricks.reshape(count, BE, BE, BE)
    sides = ghost.reshape(count, 6, BE, BE)
    beside = [
        jnp.concatenate([sides[:, 0][:, None], cube[:, :-1]], axis=1),
        jnp.concatenate([cube[:, 1:], sides[:, 1][:, None]], axis=1),
        jnp.concatenate([sides[:, 2][:, :, None], cube[:, :, :-1]], axis=2),
        jnp.concatenate([cube[:, :, 1:], sides[:, 3][:, :, None]], axis=2),
        jnp.concatenate([sides[:, 4][..., None], cube[..., :-1]], axis=3),
        jnp.concatenate([cube[..., 1:], sides[:, 5][..., None]], axis=3),
    ]
    conduct_here = COND_BASE * (1.0 + COND_SLOPE * cube)
    spread = sum(0.5 * (conduct_here + COND_BASE * (1.0 + COND_SLOPE * other)) * (other - cube) for other in beside)
    phase = jax.nn.sigmoid((cube - MELT) / MELT_WIDTH)
    capacity = 1.0 + LATENT * phase * (1.0 - phase) / MELT_WIDTH
    updated = cube + (spread - BRICK_LOSS * loss.reshape(cube.shape)) / capacity
    return updated.reshape(count, BE * BE * BE)


def reference(flow_pops, heat_pops, solid_flag, brick_temp, brick_ids, brick_links, face_cell, face_owner, face_spot):
    flow_now = flow_pops.reshape(19, NX, NY, NZ)
    heat_now = heat_pops.reshape(7, NX, NY, NZ)
    solid_mask = (solid_flag == 1).reshape(NX, NY, NZ)
    brick_now = brick_temp
    cells_brick = BE * BE * BE
    all_bricks = brick_ids.shape[0]
    slot_of = jnp.zeros((all_bricks,), jnp.int32).at[brick_ids].set(jnp.arange(all_bricks, dtype=jnp.int32))
    own_links = brick_links[brick_ids]
    link_slot = slot_of[jnp.maximum(own_links, 0)]
    linked = own_links >= 0
    face_count = face_cell.shape[0]
    device_of = jnp.arange(face_count, dtype=jnp.int32) // W
    x_index = (device_of // N_GY) * CX + face_cell // (CY * NZ)
    y_index = (device_of % N_GY) * CY + (face_cell // NZ) % CY
    z_index = face_cell % NZ
    brick_slot = face_owner[:, 0] * BPD + face_spot // cells_brick
    brick_cell = face_spot % cells_brick
    weights_heat = jnp.array(WEIGHTS_HEAT, jnp.float32).reshape(7, 1, 1, 1)
    for step_index in range(STEPS):
        relaxed_flow, relaxed_heat, fluid_temp = collide(flow_now, heat_now, solid_mask)
        face_temp = fluid_temp[x_index, y_index, z_index]
        wall_flux = WALL_COEF * (brick_now[brick_slot, brick_cell] - face_temp)
        heat_gain = jnp.zeros_like(fluid_temp).at[x_index, y_index, z_index].add(wall_flux)
        brick_loss = jnp.zeros_like(brick_now).at[brick_slot, brick_cell].add(wall_flux)
        relaxed_heat = relaxed_heat + weights_heat * heat_gain[None]
        pad_widths = ((0, 0), (1, 1), (1, 1), (0, 0))
        flow_now = propagate(jnp.pad(relaxed_flow, pad_widths), VELOCITY)
        heat_now = propagate(jnp.pad(relaxed_heat, pad_widths), VELOCITY[:7])
        own_faces = brick_faces(brick_now)
        ghost = fill_ghosts(own_faces, own_faces, link_slot, linked)
        brick_now = conduct(brick_now, ghost, brick_loss)
    return flow_now.reshape(19, NX, NY * NZ), heat_now.reshape(7, NX, NY * NZ), brick_now
```

```python
import jax
import jax.numpy as jnp
from jax import lax
from jax.sharding import PartitionSpec as P

NZ = 32
STEPS = 2
BE = 8


VELOCITY = [
    (0, 0, 0),
    (1, 0, 0),
    (-1, 0, 0),
    (0, 1, 0),
    (0, -1, 0),
    (0, 0, 1),
    (0, 0, -1),
    (1, 1, 0),
    (-1, -1, 0),
    (1, -1, 0),
    (-1, 1, 0),
    (1, 0, 1),
    (-1, 0, -1),
    (1, 0, -1),
    (-1, 0, 1),
    (0, 1, 1),
    (0, -1, -1),
    (0, 1, -1),
    (0, -1, 1),
]
OPPOSITE = [0, 2, 1, 4, 3, 6, 5, 8, 7, 10, 9, 12, 11, 14, 13, 16, 15, 18, 17]
WEIGHTS_FLOW = [1.0 / 3.0] + [1.0 / 18.0] * 6 + [1.0 / 36.0] * 12
WEIGHTS_HEAT = [0.25] + [0.125] * 6
SIDE_SWAP = [1, 0, 3, 2, 5, 4]
TAU_FLOW = 0.8
TAU_HEAT = 0.9
BUOYANCY = 0.002
HEAT_REF = 1.0
WALL_COEF = 0.1
BRICK_LOSS = 0.5
COND_BASE = 0.04
COND_SLOPE = 0.1
LATENT = 2.0
MELT = 4.0
MELT_WIDTH = 0.5
EXACT = lax.Precision.HIGHEST


def with_halo(block, sides, width):
    for axis, dim in sides:
        count = lax.axis_size(axis)
        forward = [(i, i + 1) for i in range(count - 1)]
        backward = [(target, source) for source, target in forward]
        low = lax.ppermute(
            lax.slice_in_dim(block, block.shape[dim] - width, None, axis=dim), axis, forward
        )
        high = lax.ppermute(lax.slice_in_dim(block, 0, width, axis=dim), axis, backward)
        block = jnp.concatenate([low, block, high], axis=dim)
    return block


def dotted(vector, velocity):
    terms = [velocity[a] * vector[a] for a in range(3) if velocity[a] != 0]
    if not terms:
        return jnp.zeros_like(vector[0])
    return sum(terms[1:], terms[0])


def collide(flow_pops, heat_pops, solid_mask):
    density = jnp.sum(flow_pops, axis=0)
    momentum = [
        sum((VELOCITY[i][a] * flow_pops[i] for i in range(19) if VELOCITY[i][a] != 0))
        for a in range(3)
    ]
    velocity = [m / density for m in momentum]
    fluid_temp = jnp.sum(heat_pops, axis=0)
    forcing = BUOYANCY * (fluid_temp - HEAT_REF)
    shifted = [velocity[0], velocity[1], velocity[2] + TAU_FLOW * forcing / density]
    speed_sq = shifted[0] * shifted[0] + shifted[1] * shifted[1] + shifted[2] * shifted[2]
    relaxed_flow = []
    for i in range(19):
        along = dotted(shifted, VELOCITY[i])
        equilibrium = (
            WEIGHTS_FLOW[i] * density * (1.0 + 3.0 * along + 4.5 * along * along - 1.5 * speed_sq)
        )
        relaxed = flow_pops[i] - (flow_pops[i] - equilibrium) / TAU_FLOW
        relaxed_flow.append(jnp.where(solid_mask, flow_pops[OPPOSITE[i]], relaxed))
    relaxed_heat = []
    for j in range(7):
        along = dotted(velocity, VELOCITY[j])
        equilibrium = WEIGHTS_HEAT[j] * fluid_temp * (1.0 + 4.0 * along)
        relaxed = heat_pops[j] - (heat_pops[j] - equilibrium) / TAU_HEAT
        relaxed_heat.append(jnp.where(solid_mask, heat_pops[OPPOSITE[j]], relaxed))
    return (jnp.stack(relaxed_flow), jnp.stack(relaxed_heat), fluid_temp)


def propagate_flat(extended, velocities, row_count, flat_width):
    depth_pos = lax.broadcasted_iota(jnp.int32, (row_count, flat_width), 1) % NZ
    moved = []
    for i, v in enumerate(velocities):
        start = (1 - v[1]) * NZ
        piece = extended[i, 1 - v[0] : 1 - v[0] + row_count, start : start + flat_width]
        if v[2] == 1:
            piece = jnp.where(depth_pos == 0, 0.0, jnp.roll(piece, 1, axis=1))
        elif v[2] == -1:
            piece = jnp.where(depth_pos == NZ - 1, 0.0, jnp.roll(piece, -1, axis=1))
        moved.append(piece)
    return jnp.stack(moved)


def brick_faces(bricks):
    count = bricks.shape[0]
    cube = bricks.reshape(count, BE, BE, BE)
    layers = [
        cube[:, 0],
        cube[:, -1],
        cube[:, :, 0],
        cube[:, :, -1],
        cube[:, :, :, 0],
        cube[:, :, :, -1],
    ]
    return jnp.stack(layers, axis=1).reshape(count, 6, BE * BE)


def fill_ghosts(every_face, own_faces, link_slot, linked):
    swap = jnp.array(SIDE_SWAP, jnp.int32)
    remote = every_face[link_slot, swap[None, :]]
    return jnp.where(linked[:, :, None], remote, own_faces)


def conduct(bricks, ghost, loss):
    count = bricks.shape[0]
    cube = bricks.reshape(count, BE, BE, BE)
    sides = ghost.reshape(count, 6, BE, BE)
    beside = [
        jnp.concatenate([sides[:, 0][:, None], cube[:, :-1]], axis=1),
        jnp.concatenate([cube[:, 1:], sides[:, 1][:, None]], axis=1),
        jnp.concatenate([sides[:, 2][:, :, None], cube[:, :, :-1]], axis=2),
        jnp.concatenate([cube[:, :, 1:], sides[:, 3][:, :, None]], axis=2),
        jnp.concatenate([sides[:, 4][..., None], cube[..., :-1]], axis=3),
        jnp.concatenate([cube[..., 1:], sides[:, 5][..., None]], axis=3),
    ]
    conduct_here = COND_BASE * (1.0 + COND_SLOPE * cube)
    spread = sum(
        (
            0.5 * (conduct_here + COND_BASE * (1.0 + COND_SLOPE * other)) * (other - cube)
            for other in beside
        )
    )
    phase = jax.nn.sigmoid((cube - MELT) / MELT_WIDTH)
    capacity = 1.0 + LATENT * phase * (1.0 - phase) / MELT_WIDTH
    updated = cube + (spread - BRICK_LOSS * loss.reshape(cube.shape)) / capacity
    return updated.reshape(count, BE * BE * BE)


def body(
    flow_pops,
    heat_pops,
    solid_flag,
    brick_temp,
    brick_ids,
    brick_links,
    face_cell,
    face_owner,
    face_spot,
):
    grid_rows = lax.axis_size("gx")
    grid_cols = lax.axis_size("gy")
    devices = grid_rows * grid_cols
    device_id = lax.axis_index("gx") * grid_cols + lax.axis_index("gy")
    block_rows = flow_pops.shape[1]
    flat_width = flow_pops.shape[2]
    cell_count = block_rows * flat_width
    flow_now = flow_pops
    heat_now = heat_pops
    solid_mask = solid_flag == 1
    per_device = face_cell.shape[0] // devices
    capacity = max(2, 2 * per_device // devices)
    owners = face_owner[:, 0]
    own_cell = lax.dynamic_slice_in_dim(face_cell, device_id * per_device, per_device)
    own_owner = lax.dynamic_slice_in_dim(owners, device_id * per_device, per_device)
    targets = jnp.arange(devices, dtype=jnp.int32)
    onehot = (own_owner[:, None] == targets[None, :]).astype(jnp.int32)
    own_rank = jnp.sum(jnp.cumsum(onehot, axis=0) * onehot, axis=1) - 1
    send_slot = own_owner * capacity + own_rank
    slot_table = (
        send_slot[:, None] == jnp.arange(devices * capacity, dtype=jnp.int32)[None, :]
    ).astype(jnp.float32)
    mine = (owners == device_id).astype(jnp.int32).reshape(devices, per_device)
    recv_rank = jnp.where(mine == 1, jnp.cumsum(mine, axis=1) - 1, capacity)
    ranks = jnp.arange(capacity, dtype=jnp.int32)[None, :, None]
    chosen = recv_rank[:, None, :] == ranks
    spots = face_spot.reshape(devices, 1, per_device)
    recv_spot = jnp.sum(jnp.where(chosen, spots, 0), axis=2)
    recv_live = jnp.sum(jnp.where(chosen, 1.0, 0.0), axis=2)
    cell_row = own_cell // flat_width
    cell_col = own_cell % flat_width
    row_table = (cell_row[:, None] == jnp.arange(block_rows, dtype=jnp.int32)[None, :]).astype(
        jnp.float32
    )
    col_table = (cell_col[:, None] == jnp.arange(flat_width, dtype=jnp.int32)[None, :]).astype(
        jnp.float32
    )
    bricks_here = brick_temp.shape[0]
    brick_cells = bricks_here * brick_temp.shape[1]
    spot_table = (
        recv_spot.reshape(-1)[:, None] == jnp.arange(brick_cells, dtype=jnp.int32)[None, :]
    ).astype(jnp.float32)
    all_bricks = brick_ids.shape[0]
    slot_of = (
        jnp.zeros((all_bricks,), jnp.int32)
        .at[brick_ids]
        .set(jnp.arange(all_bricks, dtype=jnp.int32))
    )
    own_slots = device_id * bricks_here + jnp.arange(bricks_here, dtype=jnp.int32)
    own_links = brick_links[brick_ids[own_slots]]
    link_slot = slot_of[jnp.maximum(own_links, 0)]
    linked = own_links >= 0
    brick_now = brick_temp
    every_velocity = VELOCITY + VELOCITY[:7]
    weights_heat = jnp.array(WEIGHTS_HEAT, jnp.float32).reshape(7, 1, 1)
    for step_index in range(STEPS):
        relaxed_flow, relaxed_heat, fluid_temp = collide(flow_now, heat_now, solid_mask)
        face_temp = fluid_temp.reshape(cell_count)[own_cell]
        outgoing = jnp.dot(face_temp, slot_table, precision=EXACT).reshape(devices, capacity)
        arrived = lax.all_to_all(outgoing, ("gx", "gy"), split_axis=0, concat_axis=0, tiled=True)
        flat_brick = brick_now.reshape(-1)
        wall_flux = WALL_COEF * (flat_brick[recv_spot] - arrived) * recv_live
        brick_loss = jnp.dot(wall_flux.reshape(-1), spot_table, precision=EXACT).reshape(
            brick_now.shape
        )
        returned = lax.all_to_all(wall_flux, ("gx", "gy"), split_axis=0, concat_axis=0, tiled=True)
        face_flux = jnp.dot(slot_table, returned.reshape(-1), precision=EXACT)
        heat_gain = jnp.dot((row_table * face_flux[:, None]).T, col_table, precision=EXACT)
        relaxed_heat = relaxed_heat + weights_heat * heat_gain[None]
        combined = jnp.concatenate([relaxed_flow, relaxed_heat], axis=0)
        widened = with_halo(combined, (("gx", 1),), 1)
        extended = with_halo(widened, (("gy", 2),), NZ)
        moved = propagate_flat(extended, every_velocity, block_rows, flat_width)
        flow_now = moved[:19]
        heat_now = moved[19:]
        faces_here = brick_faces(brick_now)
        own_copy = faces_here.reshape(1, bricks_here * 6 * BE * BE)
        every_face = lax.all_to_all(
            jnp.broadcast_to(own_copy, (devices, own_copy.shape[1])),
            ("gx", "gy"),
            split_axis=0,
            concat_axis=0,
            tiled=True,
        ).reshape(all_bricks, 6, BE * BE)
        ghost = fill_ghosts(every_face, faces_here, link_slot, linked)
        brick_now = conduct(brick_now, ghost, brick_loss)
    return (flow_now, heat_now, brick_now)


def solution(mesh):
    return jax.shard_map(
        body,
        mesh=mesh,
        in_specs=(
            P(None, "gx", "gy"),
            P(None, "gx", "gy"),
            P("gx", "gy"),
            P(("gx", "gy"), None),
            P(),
            P(),
            P(),
            P(),
            P(),
        ),
        out_specs=(P(None, "gx", "gy"), P(None, "gx", "gy"), P(("gx", "gy"), None)),
        check_vma=False,
    )
```

```python
import functools

import jax
import jax.numpy as jnp
from jax import lax
from jax.experimental import pallas as pl
from jax.experimental.pallas import tpu as pltpu
from jax.sharding import PartitionSpec as P

MESH = pl.DeviceIdType.MESH
F32, BF16, I32 = jnp.float32, jnp.bfloat16, jnp.int32

VELOCITY = [
    (0, 0, 0),
    (1, 0, 0),
    (-1, 0, 0),
    (0, 1, 0),
    (0, -1, 0),
    (0, 0, 1),
    (0, 0, -1),
    (1, 1, 0),
    (-1, -1, 0),
    (1, -1, 0),
    (-1, 1, 0),
    (1, 0, 1),
    (-1, 0, -1),
    (1, 0, -1),
    (-1, 0, 1),
    (0, 1, 1),
    (0, -1, -1),
    (0, 1, -1),
    (0, -1, 1),
]
SIDE_SWAP = [1, 0, 3, 2, 5, 4]
WEIGHTS_HEAT = [0.25] + [0.125] * 6
TAU_FLOW, TAU_HEAT = 0.8, 0.9
BUOYANCY = 0.002
WALL_COEF = 0.1
BRICK_LOSS = 0.5
COND_BASE, COND_SLOPE = 0.04, 0.1
LATENT, MELT, MELT_WIDTH = 2.0, 4.0, 0.5

GX, GY = 16, 8
DEV = GX * GY
CAP = 16
ROWS, TILES, NZ = 32, 16, 32
PITCH = 48
TALL = (TILES + 2) * PITCH
SLOTS = CAP * DEV

ORDER = [9, 1, 11, 13, 20, 7, 3, 15, 17, 22, 10, 2, 12, 14, 21, 8, 4, 16, 18, 23]
ORDER += [0, 5, 6, 19, 24, 25]
PLACE = {pop: at for at, pop in enumerate(ORDER)}
ALL_VELOCITY = VELOCITY + VELOCITY[:7]
XP, YP, XM, YM = ORDER[0:6], ORDER[5:11], ORDER[10:16], ORDER[15:20] + [9]
CORNERS = [(7, 1, 1), (8, -1, -1), (9, 1, -1), (10, -1, 1)]


def iota(shape, dim):
    return lax.broadcasted_iota(I32, shape, dim)


def lane_pick(rows, index):
    return jnp.take_along_axis(rows, index, axis=1, mode="promise_in_bounds")


def tables_kernel(
    owners,
    spots,
    cells,
    id_col,
    links,
    id_row,
    arow_ref,
    lrow_ref,
    lcol_ref,
    oh_cell,
    brow_ref,
    blrow_ref,
    blcol_ref,
    oh_brick,
    pick_ref,
    key,
    val,
    packed,
    by_slot,
):
    x, y = lax.axis_index("gx"), lax.axis_index("gy")
    me = x * GY + y
    square = (128, 128)
    lane = iota(square, 1)
    wide_row, wide_lane = iota((128, 256), 0), iota((128, 256), 1)
    prefix = jnp.where((wide_row <= wide_lane), 1.0, 0.0).astype(BF16)

    def compact(get):
        before = jnp.zeros(square, F32)
        for b in range(8):
            mask, value = get(b)
            counts = jnp.dot(
                jnp.where(mask, 1.0, 0.0).astype(BF16), prefix, preferred_element_type=F32
            )
            key[b] = jnp.where(mask, counts[:, :128] + before, 0.0)
            val[b] = value
            before = before + counts[:, 128:]

        @pl.loop(0, 16)
        def _(c):
            rows = pl.ds(pl.multiple_of(c * 8, 8), 8)
            keys = [key[b, rows, :] for b in range(8)]
            vals = [val[b, rows, :] for b in range(8)]
            at = iota((8, 128), 1)
            out = jnp.zeros((8, 128), F32)
            for r in range(CAP):
                hit = jnp.zeros((8, 128), F32)
                for b in range(8):
                    hit = jnp.where(keys[b] == float(r + 1), vals[b], hit)
                out = jnp.where(at == r, jnp.sum(hit, axis=1, keepdims=True), out)
            packed[rows, :] = out

        return packed[...]

    own_rows = pl.ds(pl.multiple_of(me * 8, 8), 8)
    own_owner = owners[own_rows, :]
    own_cell = cells[own_rows, :].astype(F32) + 1.0
    row_index = iota(square, 0)
    table = compact(
        lambda b: (
            row_index == own_owner[b : b + 1, :],
            jnp.broadcast_to(own_cell[b : b + 1, :], square),
        )
    )

    def split_cell(c):
        c = c.astype(I32) - 1
        live = c >= 0
        a = ((c >> 7) & 15) * ROWS + (c >> 11)
        return jnp.where(live, a, -1), c & 127, live

    a, low, live = split_cell(table)
    lcol_ref[...] = jnp.where(live, low, -1)
    a, low, live = split_cell(jnp.transpose(table)[:CAP, :])
    arow_ref[...] = a
    lrow_ref[...] = jnp.where(live, low, 0)
    for r in range(CAP):
        for q in range(4):
            part = iota(square, 0) + q * 128 == a[r : r + 1, :]
            oh_cell[q * 128 : (q + 1) * 128, r * 128 : (r + 1) * 128] = jnp.where(
                part, 1.0, 0.0
            ).astype(BF16)

    def from_device(b):
        rows = pl.ds(b, 128, stride=8)
        return owners[rows, :] == me, spots[rows, :].astype(F32) + 1.0

    table = compact(from_device)

    def split_spot(c):
        c = c.astype(I32) - 1
        live = c >= 0
        return jnp.where(live, c >> 6, -1), c & 63, live

    a, low, live = split_spot(table)
    blcol_ref[...] = jnp.where(live, low, -1)
    a, low, live = split_spot(jnp.transpose(table)[:CAP, :])
    brow_ref[...] = a
    blrow_ref[...] = jnp.where(live, low, 0)
    for r in range(CAP):
        part = iota((16, 128), 0) == a[r : r + 1, :]
        oh_brick[:, r * 128 : (r + 1) * 128] = jnp.where(part, 1.0, 0.0).astype(BF16)

    chosen = jnp.where(id_col[...] == iota((256, 256), 1), 1.0, 0.0).astype(BF16)
    by_slot[...] = jnp.dot(
        chosen, links[...].astype(F32).astype(BF16), preferred_element_type=F32
    )
    at = iota((16, 128), 1)
    to_x = iota((16, 128), 0)
    ids = id_row[...].astype(F32)
    for b in range(2):
        named = by_slot[pl.ds(2 * y + b, 16, stride=16), :]
        for s in range(6):
            j = s * 2 + b
            n = named[:, s : s + 1]
            side = (at & 15) >> 1
            remote = (n == ids) & (side == SIDE_SWAP[s])
            own = (n < 0.0) & (to_x == x) & (at == y * 16 + j)
            pick_ref[j * 16 : (j + 1) * 16, :] = jnp.where(remote | own, 1.0, 0.0).astype(BF16)


def collide(f, g, solid):
    pairs = [(1, 2), (3, 4), (5, 6), (7, 8), (9, 10), (11, 12), (13, 14), (15, 16), (17, 18)]
    total = {a: f[a] + f[b] for a, b in pairs}
    diff = {a: f[a] - f[b] for a, b in pairs}
    density = f[0] + (
        (total[1] + total[3])
        + (total[5] + total[7])
        + (total[9] + total[11])
        + (total[13] + total[15])
        + total[17]
    )
    inverse = 1.0 / density
    ux = (diff[1] + diff[7] + diff[9] + diff[11] + diff[13]) * inverse
    uy = (diff[3] + diff[7] - diff[9] + diff[15] + diff[17]) * inverse
    uz = (diff[5] + diff[11] - diff[13] + diff[15] - diff[17]) * inverse
    temp = g[0] + ((g[1] + g[2]) + (g[3] + g[4]) + (g[5] + g[6]))
    sz = uz + (TAU_FLOW * BUOYANCY) * (temp - 1.0) * inverse
    base = 1.0 - 1.5 * (ux * ux + uy * uy + sz * sz)
    keep = 1.0 - 1.0 / TAU_FLOW
    along_of = {1: ux, 3: uy, 5: sz, 7: ux + uy, 9: ux - uy}
    along_of.update({11: ux + sz, 13: ux - sz, 15: uy + sz, 17: uy - sz})
    out_f = [None] * 19
    k0 = density * (1.0 / 3.0 / TAU_FLOW)
    out_f[0] = jnp.where(solid, f[0], keep * f[0] + k0 * base)
    scale = {1: density * (1.0 / 18.0 / TAU_FLOW), 7: density * (1.0 / 36.0 / TAU_FLOW)}
    for a, b in pairs:
        k = scale[1 if a < 7 else 7]
        along = along_of[a]
        even = k * (base + 4.5 * (along * along))
        odd = (3.0 * k) * along
        out_f[a] = jnp.where(solid, f[b], (even + odd) + keep * f[a])
        out_f[b] = jnp.where(solid, f[a], (even - odd) + keep * f[b])
    keep = 1.0 - 1.0 / TAU_HEAT
    out_g = [None] * 7
    out_g[0] = jnp.where(solid, g[0], keep * g[0] + (0.25 / TAU_HEAT) * temp)
    k = (0.125 / TAU_HEAT) * temp
    for a, u in ((1, ux), (3, uy), (5, uz)):
        odd = (4.0 * k) * u
        out_g[a] = jnp.where(solid, g[a + 1], (k + odd) + keep * g[a])
        out_g[a + 1] = jnp.where(solid, g[a], (k - odd) + keep * g[a + 1])
    return out_f, out_g


def pull(store, pop, t, xb, lane):
    cx, cy, cz = ALL_VELOCITY[pop]
    at = PLACE[pop]

    def tile(step):
        return store[at, pl.ds((t + 1 + step) * PITCH + 8 + xb * 8 - cx, 8), :]

    here = tile(0)
    if cy == 1:
        here = jnp.where(lane >= 128 - NZ, tile(-1), here)
    if cy == -1:
        here = jnp.where(lane < NZ, tile(1), here)
    shift = (cy * NZ + cz) % 128
    if shift:
        here = pltpu.roll(here, shift, 1)
    if cz == 1:
        here = jnp.where(lane % NZ == 0, 0.0, here)
    if cz == -1:
        here = jnp.where(lane % NZ == NZ - 1, 0.0, here)
    return here


def own_rows(t, xb):
    return pl.ds((t + 1) * PITCH + 8 + xb * 8, 8)


def natural(t, xb):
    return pl.ds(xb * 8, 8), pl.ds(pl.multiple_of(t * 128, 128), 128)


def temp_rows(t, xb):
    return pl.ds(pl.multiple_of(t * ROWS + xb * 8, 8), 8)


def halves(value):
    high = value.astype(BF16)
    return high, (value - high.astype(F32)).astype(BF16)


def scatter(onehot, columns, flux, spread):
    high, low = halves(flux)
    high, low = high.astype(F32), low.astype(F32)
    at = iota((128, 128), 1)
    for r in range(CAP):
        hit = at == columns[:, r : r + 1]
        rows = slice(r * 128, (r + 1) * 128)
        spread[rows, 0:128] = jnp.where(hit, high[:, r : r + 1], 0.0).astype(BF16)
        spread[rows, 128:256] = jnp.where(hit, low[:, r : r + 1], 0.0).astype(BF16)
    both = jnp.dot(onehot[...], spread[...], preferred_element_type=F32)
    return both[:, :128] + both[:, 128:]


def brick_lookup(brick, brow, blrow):
    out = jnp.zeros((CAP, 128), F32)
    for a in range(16):
        row = jnp.broadcast_to(brick[a : a + 1, :], (CAP, 128))
        out = jnp.where(brow == a, lane_pick(row, blrow), out)
    return out


def store_faces(brick, faces):
    at, row = iota((16, 128), 1), iota((16, 128), 0)
    mine = ((at >> 3) & 7) == (row & 7)
    wanted = {
        2: at & 7,
        3: 56 + (at & 7),
        4: (at & 7) * 8,
        5: (at & 7) * 8 + 7,
    }
    faces[12:16, :] = jnp.zeros((4, 128), F32)
    for b in range(2):
        faces[b : b + 1, :] = brick[b * 8 : b * 8 + 1, :]
        faces[2 + b : 3 + b, :] = brick[b * 8 + 7 : b * 8 + 8, :]
    for s, index in wanted.items():
        got = jnp.where(mine, lane_pick(brick, index), 0.0)
        for b in range(2):
            faces[s * 2 + b : s * 2 + b + 1, :] = jnp.sum(
                got[b * 8 : b * 8 + 8], axis=0, keepdims=True
            )


def conduct(brick, ghost, loss):
    at, row = iota((16, 128), 1), iota((16, 128), 0)
    x = row & 7

    def ghost_rows(s):
        return jnp.where(row < 8, ghost[s * 2 : s * 2 + 1, :], ghost[s * 2 + 1 : s * 2 + 2, :])

    over_z = x * 8 + (at & 7)
    over_y = x * 8 + ((at >> 3) & 7)
    beside = [
        jnp.where(x == 0, ghost_rows(0), pltpu.roll(brick, 1, 0)),
        jnp.where(x == 7, ghost_rows(1), pltpu.roll(brick, 15, 0)),
        jnp.where(at < 8, lane_pick(ghost_rows(2), over_z), pltpu.roll(brick, 8, 1)),
        jnp.where(at >= 56, lane_pick(ghost_rows(3), over_z), pltpu.roll(brick, 120, 1)),
        jnp.where((at & 7) == 0, lane_pick(ghost_rows(4), over_y), pltpu.roll(brick, 1, 1)),
        jnp.where((at & 7) == 7, lane_pick(ghost_rows(5), over_y), pltpu.roll(brick, 127, 1)),
    ]
    here = COND_BASE * (1.0 + COND_SLOPE * brick)
    spread = jnp.zeros((16, 128), F32)
    for other in beside:
        spread += 0.5 * (here + COND_BASE * (1.0 + COND_SLOPE * other)) * (other - brick)
    phase = 1.0 / (1.0 + jnp.exp(-(brick - MELT) / MELT_WIDTH))
    capacity = 1.0 + LATENT * phase * (1.0 - phase) / MELT_WIDTH
    return jnp.where(at < 64, brick + (spread - BRICK_LOSS * loss) / capacity, 0.0)


def steps_kernel(
    flow,
    heat,
    solid,
    brick_in,
    arow_ref,
    lrow_ref,
    lcol_ref,
    oh_cell,
    brow_ref,
    blrow_ref,
    blcol_ref,
    oh_brick,
    pick_ref,
    second,
    brick_out,
    first,
    temps,
    gain,
    spread,
    msg,
    faces,
    s1,
    r1,
    s2,
    r2,
    xs,
    xr,
    ys,
    yr,
    cs,
    cr,
    s1_send,
    s1_recv,
    s2_send,
    s2_recv,
    halo_send,
    halo_recv,
):
    x, y = lax.axis_index("gx"), lax.axis_index("gy")

    def xn(k):
        return lax.rem(x + (k + GX), GX)

    def yn(k):
        return lax.rem(y + (k + GY), GY)

    barrier = pltpu.get_barrier_semaphore()
    peers = [(x, yn(k)) for k in range(1, GY)] + [(xn(k), y) for k in range(1, GX)]
    peers += [(xn(a), yn(b)) for a in (-1, 1) for b in (-1, 1)]
    for peer in peers:
        pl.semaphore_signal(barrier, inc=1, device_id=peer, device_id_type=MESH)

    lane = iota((8, 128), 1)

    def look_up_faces(brick):
        a, low = arow_ref[...], lrow_ref[...]

        def body(i, out):
            for u in range(8):
                row = i * 8 + u
                line = jnp.broadcast_to(temps[pl.ds(row, 1), :], (CAP, 128))
                out = jnp.where(a == row, lane_pick(line, low), out)
            return out

        found = lax.fori_loop(0, TILES * ROWS // 8, body, jnp.zeros((CAP, 128), F32))
        asked = brick_lookup(brick, brow_ref[...], blrow_ref[...])
        rest = jnp.zeros((128 - 2 * CAP, 128), F32)
        msg[...] = jnp.transpose(jnp.concatenate([found, asked, rest], axis=0))
        store_faces(brick, faces)

    def phase_one(step):
        for k in range(GY):
            s1[step, k * 32 : k * 32 + 16, :] = msg[pl.ds(k, 16, stride=8), :]
            s1[step, k * 32 + 16 : k * 32 + 32, :] = faces[...]
        copies = []
        for k in range(1, GY):
            to = yn(k)
            copies.append(
                pltpu.make_async_remote_copy(
                    src_ref=s1.at[step, pl.ds(pl.multiple_of(to * 32, 32), 32), :],
                    dst_ref=r1.at[step, pl.ds(pl.multiple_of(y * 32, 32), 32), :],
                    send_sem=s1_send.at[step, k],
                    recv_sem=s1_recv.at[step, y],
                    device_id=(x, to),
                    device_id_type=MESH,
                )
            )
            copies[-1].start()
        own = pl.ds(pl.multiple_of(y * 32, 32), 32)
        r1[step, own, :] = s1[step, own, :]
        return copies

    def end_one(step, copies):
        for k in range(1, GY):
            copies[k - 1].wait_send()
            came = yn(k)
            rows = pl.ds(pl.multiple_of(came * 32, 32), 32)
            pltpu.make_async_remote_copy(
                src_ref=s1.at[step, rows, :],
                dst_ref=r1.at[step, rows, :],
                send_sem=s1_send.at[step, k],
                recv_sem=s1_recv.at[step, came],
                device_id=(x, came),
                device_id_type=MESH,
            ).wait_recv()

    def phase_two(step):
        every = jnp.concatenate(
            [r1[step, k * 32 + 16 : k * 32 + 32, :] for k in range(GY)], axis=0
        )
        high = every.astype(BF16)
        low = every - high.astype(F32)
        at = iota((128, 128), 1)
        both = jnp.where(at < 64, high.astype(F32), pltpu.roll(low, 64, 1)).astype(BF16)
        picked = jnp.dot(pick_ref[...], both, preferred_element_type=F32)
        picked = picked + pltpu.roll(picked, 64, 1)
        for j in range(12):
            s2[step, pl.ds(8 + j, 16, stride=24), :] = picked[j * 16 : (j + 1) * 16, :]
        for j in range(12, 16):
            s2[step, pl.ds(8 + j, 16, stride=24), :] = jnp.zeros((16, 128), F32)
        for k in range(GX):
            s2[step, k * 24 : k * 24 + 8, :] = r1[step, pl.ds(k, 8, stride=32), :]
        copies = []
        for k in range(1, GX):
            to = xn(k)
            copies.append(
                pltpu.make_async_remote_copy(
                    src_ref=s2.at[step, pl.ds(pl.multiple_of(to * 24, 8), 24), :],
                    dst_ref=r2.at[step, pl.ds(pl.multiple_of(x * 24, 8), 24), :],
                    send_sem=s2_send.at[step, k],
                    recv_sem=s2_recv.at[step, x],
                    device_id=(to, y),
                    device_id_type=MESH,
                )
            )
            copies[-1].start()
        own = pl.ds(pl.multiple_of(x * 24, 8), 24)
        r2[step, own, :] = s2[step, own, :]
        return copies

    def end_two(step, copies):
        for k in range(1, GX):
            copies[k - 1].wait_send()
            came = xn(k)
            rows = pl.ds(pl.multiple_of(came * 24, 8), 24)
            pltpu.make_async_remote_copy(
                src_ref=s2.at[step, rows, :],
                dst_ref=r2.at[step, rows, :],
                send_sem=s2_send.at[step, k],
                recv_sem=s2_recv.at[step, came],
                device_id=(came, y),
                device_id_type=MESH,
            ).wait_recv()

    def couple(step, brick, store):
        came = jnp.concatenate([r2[step, k * 24 : k * 24 + 8, :] for k in range(GX)], axis=0)
        ghost = r2[step, 8:24, :]
        for k in range(1, GX):
            ghost = ghost + r2[step, k * 24 + 8 : k * 24 + 24, :]
        mine = msg[...]
        to_fluid = WALL_COEF * (pltpu.roll(came, 128 - CAP, 1) - mine)
        gain[...] = scatter(oh_cell, lcol_ref[...], to_fluid, spread)
        lost = WALL_COEF * (pltpu.roll(mine, 128 - CAP, 1) - came)
        loss = scatter(oh_brick, blcol_ref[...], lost, spread)

        @pl.loop(0, TILES)
        def _(t):
            for xb in range(4):
                more = gain[temp_rows(t, xb), :]
                for j in range(7):
                    rows = own_rows(t, xb)
                    at = PLACE[19 + j]
                    store[at, rows, :] = store[at, rows, :] + WEIGHTS_HEAT[j] * more

        return conduct(brick, ghost, loss)

    def send_halo(step, store):
        for side, (group, row) in enumerate(((XP, 39), (XM, 8))):
            for k, pop in enumerate(group):
                xs[step, side, k * 16 : (k + 1) * 16, :] = store[
                    PLACE[pop], pl.ds(PITCH + row, 16, stride=PITCH), :
                ]
        wide = iota((32, 128), 1)
        for side, (group, t, lanes) in enumerate(((YP, TILES, 96), (YM, 1, 0))):
            parts = []
            for k, pop in enumerate(group):
                part = store[PLACE[pop], t * PITCH + 8 : t * PITCH + 40, :]
                turn = ((k % 4) * 32 - lanes) % 128
                parts.append(pltpu.roll(part, turn, 1) if turn else part)
            for q in range(2):
                tile = parts[q * 4]
                for k in range(1, len(parts[q * 4 : q * 4 + 4])):
                    tile = jnp.where(wide >= k * 32, parts[q * 4 + k], tile)
                ys[step, side, q * 32 : (q + 1) * 32, :] = tile
        for c, (pop, dx, dy) in enumerate(CORNERS):
            t, row = (TILES if dy == 1 else 1), (39 if dx == 1 else 8)
            cs[step, c] = jnp.broadcast_to(
                store[PLACE[pop], t * PITCH + row : t * PITCH + row + 1, :], (8, 128)
            )
        plan = [(xs.at[step, 0], xr.at[step, 0], (xn(1), y))]
        plan.append((xs.at[step, 1], xr.at[step, 1], (xn(-1), y)))
        plan.append((ys.at[step, 0], yr.at[step, 0], (x, yn(1))))
        plan.append((ys.at[step, 1], yr.at[step, 1], (x, yn(-1))))
        for c, (_, dx, dy) in enumerate(CORNERS):
            plan.append((cs.at[step, c], cr.at[step, c], (xn(dx), yn(dy))))
        copies = []
        for n, (source, target, peer) in enumerate(plan):
            copies.append(
                pltpu.make_async_remote_copy(
                    src_ref=source,
                    dst_ref=target,
                    send_sem=halo_send.at[step, n],
                    recv_sem=halo_recv.at[step, n],
                    device_id=peer,
                    device_id_type=MESH,
                )
            )
            copies[-1].start()
        return copies

    def end_halo(step, store, copies):
        for copy in copies:
            copy.wait()
        inside = {(1, 0): x > 0, (-1, 0): x < GX - 1, (0, 1): y > 0, (0, -1): y < GY - 1}
        for side, (group, row, way) in enumerate(((XP, 7, 1), (XM, 40, -1))):
            for k, pop in enumerate(group):
                store[PLACE[pop], pl.ds(PITCH + row, 16, stride=PITCH), :] = jnp.where(
                    inside[(way, 0)], xr[step, side, k * 16 : (k + 1) * 16, :], 0.0
                )
        for side, (group, t, lanes, way) in enumerate(((YP, 0, 96, 1), (YM, TILES + 1, 0, -1))):
            for k, pop in enumerate(group):
                part = yr[step, side, (k // 4) * 32 : (k // 4 + 1) * 32, :]
                turn = (lanes - (k % 4) * 32) % 128
                part = pltpu.roll(part, turn, 1) if turn else part
                store[PLACE[pop], t * PITCH + 8 : t * PITCH + 40, :] = jnp.where(
                    inside[(0, way)], part, 0.0
                )
        for c, (pop, dx, dy) in enumerate(CORNERS):
            t, row = (0 if dy == 1 else TILES + 1), (7 if dx == 1 else 40)
            known = inside[(dx, 0)] & inside[(0, dy)]
            store[PLACE[pop], t * PITCH + row : t * PITCH + row + 1, :] = jnp.where(
                known, cr[step, c, 0:1, :], 0.0
            )

    def store_relaxed(store, t, xb, f, g):
        out_f, out_g = collide(f, g, solid[natural(t, xb)] == 1)
        rows = own_rows(t, xb)
        for i in range(19):
            store[PLACE[i], rows, :] = out_f[i]
        for j in range(7):
            store[PLACE[19 + j], rows, :] = out_g[j]

    @pl.loop(0, TILES)
    def _(t):
        for xb in range(4):
            rows, lanes = natural(t, xb)
            g = [heat[j, rows, lanes] for j in range(7)]
            temps[temp_rows(t, xb), :] = g[0] + (
                (g[1] + g[2]) + (g[3] + g[4]) + (g[5] + g[6])
            )

    brick = brick_in[...]
    look_up_faces(brick)
    pl.semaphore_wait(barrier, len(peers))
    copies = phase_one(0)

    def relax_first(low, high):
        @pl.loop(low * 4, high * 4)
        def _(n):
            t, xb = n // 4, n % 4
            rows, lanes = pl.ds(pl.multiple_of(xb * 8, 8), 8), natural(t, 0)[1]
            f = [flow[i, rows, lanes] for i in range(19)]
            g = [heat[j, rows, lanes] for j in range(7)]
            store_relaxed(first, t, xb, f, g)

    relax_first(0, TILES // 2)
    end_one(0, copies)
    copies = phase_two(0)
    relax_first(TILES // 2, TILES)
    end_two(0, copies)
    brick = couple(0, brick, first)
    copies = send_halo(0, first)
    brick_out[...] = brick
    end_halo(0, first, copies)

    @pl.loop(0, TILES)
    def _(t):
        for xb in range(4):
            g = [pull(first, 19 + j, t, xb, lane) for j in range(7)]
            temps[temp_rows(t, xb), :] = g[0] + (
                (g[1] + g[2]) + (g[3] + g[4]) + (g[5] + g[6])
            )

    brick = brick_out[...]
    look_up_faces(brick)
    copies = phase_one(1)

    def relax_second(low, high):
        @pl.loop(low * 4, high * 4)
        def _(n):
            t, xb = n // 4, n % 4
            f = [pull(first, i, t, xb, lane) for i in range(19)]
            g = [pull(first, 19 + j, t, xb, lane) for j in range(7)]
            store_relaxed(second, t, xb, f, g)

    relax_second(0, TILES // 2)
    end_one(1, copies)
    copies = phase_two(1)
    relax_second(TILES // 2, TILES)
    end_two(1, copies)
    brick = couple(1, brick, second)
    copies = send_halo(1, second)
    brick_out[...] = brick
    end_halo(1, second, copies)


def spread_kernel(second, flow_out, heat_out, flow_now, heat_now, sems):
    lane = iota((8, 128), 1)
    copies = []
    for pop in range(26):
        now, out, at = (flow_now, flow_out, pop) if pop < 19 else (heat_now, heat_out, pop - 19)

        @pl.loop(0, TILES)
        def _(t):
            for xb in range(4):
                rows, lanes = natural(t, xb)
                now[at, rows, lanes] = pull(second, pop, t, xb, lane)

        copies.append(pltpu.make_async_copy(now.at[at], out.at[at], sems.at[pop]))
        copies[-1].start()
    for copy in copies:
        copy.wait()


def vmem(count):
    return [pl.BlockSpec(memory_space=pltpu.VMEM)] * count


def body(
    flow_pops,
    heat_pops,
    solid_flag,
    brick_temp,
    brick_ids,
    brick_links,
    face_cell,
    face_owner,
    face_spot,
):
    gx = lax.axis_index("gx")
    shape = jax.ShapeDtypeStruct
    ids = lax.dynamic_slice_in_dim(brick_ids, gx * GY * 2, GY * 2).reshape(GY, 1, 2)
    id_row = jnp.broadcast_to(ids, (GY, 8, 2)).reshape(1, 128)
    tables = pl.pallas_call(
        tables_kernel,
        out_shape=[
            shape((CAP, 128), I32),
            shape((CAP, 128), I32),
            shape((128, 128), I32),
            shape((TILES * ROWS, SLOTS), BF16),
            shape((CAP, 128), I32),
            shape((CAP, 128), I32),
            shape((128, 128), I32),
            shape((16, SLOTS), BF16),
            shape((192, 128), BF16),
        ],
        in_specs=vmem(6),
        out_specs=vmem(9),
        scratch_shapes=[
            pltpu.VMEM((8, 128, 128), F32),
            pltpu.VMEM((8, 128, 128), F32),
            pltpu.VMEM((128, 128), F32),
            pltpu.VMEM((256, 128), F32),
        ],
        compiler_params=pltpu.CompilerParams(vmem_limit_bytes=16 << 20),
    )(
        face_owner.reshape(1024, 128),
        face_spot.reshape(1024, 128),
        face_cell.reshape(1024, 128),
        brick_ids.reshape(256, 1),
        jnp.pad(brick_links, ((0, 0), (0, 122))),
        id_row,
    )
    brick = jnp.pad(brick_temp.reshape(16, 64), ((0, 0), (0, 64)))
    dma = pltpu.SemaphoreType.DMA
    second, brick = pl.pallas_call(
        steps_kernel,
        out_shape=[pltpu.VMEM((26, TALL, 128), F32), shape((16, 128), F32)],
        in_specs=vmem(13),
        out_specs=vmem(2),
        scratch_shapes=[
            pltpu.VMEM((26, TALL, 128), F32),
            pltpu.VMEM((TILES * ROWS, 128), F32),
            pltpu.VMEM((TILES * ROWS, 128), F32),
            pltpu.VMEM((SLOTS, 256), BF16),
            pltpu.VMEM((128, 128), F32),
            pltpu.VMEM((16, 128), F32),
            pltpu.VMEM((2, GY * 32, 128), F32),
            pltpu.VMEM((2, GY * 32, 128), F32),
            pltpu.VMEM((2, GX * 24, 128), F32),
            pltpu.VMEM((2, GX * 24, 128), F32),
            pltpu.VMEM((2, 2, 96, 128), F32),
            pltpu.VMEM((2, 2, 96, 128), F32),
            pltpu.VMEM((2, 2, 64, 128), F32),
            pltpu.VMEM((2, 2, 64, 128), F32),
            pltpu.VMEM((2, 4, 8, 128), F32),
            pltpu.VMEM((2, 4, 8, 128), F32),
            dma((2, GY)),
            dma((2, GY)),
            dma((2, GX)),
            dma((2, GX)),
            dma((2, 8)),
            dma((2, 8)),
        ],
        compiler_params=pltpu.CompilerParams(
            collective_id=0, has_side_effects=True, vmem_limit_bytes=40 << 20
        ),
    )(flow_pops, heat_pops, solid_flag, brick, *tables)
    flow, heat = pl.pallas_call(
        spread_kernel,
        out_shape=[shape(flow_pops.shape, F32), shape(heat_pops.shape, F32)],
        in_specs=vmem(1),
        out_specs=[pl.BlockSpec(memory_space=pl.ANY)] * 2,
        scratch_shapes=[
            pltpu.VMEM(flow_pops.shape, F32),
            pltpu.VMEM(heat_pops.shape, F32),
            dma((26,)),
        ],
        compiler_params=pltpu.CompilerParams(vmem_limit_bytes=24 << 20),
    )(second)
    return flow, heat, brick[:, :64].reshape(brick_temp.shape)


def solution(mesh):
    return jax.shard_map(
        body,
        mesh=mesh,
        in_specs=(
            P(None, "gx", "gy"),
            P(None, "gx", "gy"),
            P("gx", "gy"),
            P(("gx", "gy"), None),
            P(),
            P(),
            P(),
            P(),
            P(),
        ),
        out_specs=(P(None, "gx", "gy"), P(None, "gx", "gy"), P(("gx", "gy"), None)),
        check_vma=False,
    )
```

```python
import functools

import jax
import jax.numpy as jnp
from jax import lax
from jax.experimental import pallas as pl
from jax.experimental.pallas import tpu as pltpu
from jax.sharding import PartitionSpec as P

MESH = pl.DeviceIdType.MESH
F32, BF16, I32 = jnp.float32, jnp.bfloat16, jnp.int32

VELOCITY = [
    (0, 0, 0),
    (1, 0, 0),
    (-1, 0, 0),
    (0, 1, 0),
    (0, -1, 0),
    (0, 0, 1),
    (0, 0, -1),
    (1, 1, 0),
    (-1, -1, 0),
    (1, -1, 0),
    (-1, 1, 0),
    (1, 0, 1),
    (-1, 0, -1),
    (1, 0, -1),
    (-1, 0, 1),
    (0, 1, 1),
    (0, -1, -1),
    (0, 1, -1),
    (0, -1, 1),
]
SIDE_SWAP = [1, 0, 3, 2, 5, 4]
WEIGHTS_HEAT = [0.25] + [0.125] * 6
TAU_FLOW, TAU_HEAT = 0.8, 0.9
BUOYANCY = 0.002
WALL_COEF = 0.1
BRICK_LOSS = 0.5
COND_BASE, COND_SLOPE = 0.04, 0.1
LATENT, MELT, MELT_WIDTH = 2.0, 4.0, 0.5

GX, GY = 16, 8
DEV = GX * GY
CAP = 16
ROWS, TILES, NZ = 32, 16, 32
PITCH = 48
TALL = (TILES + 2) * PITCH
SLOTS = CAP * DEV

ALL_VELOCITY = VELOCITY + VELOCITY[:7]
SIDES = [([9, 1, 11, 13, 7], 20), ([10, 2, 12, 14, 8], 21)]
SIDES += [([7, 3, 15, 17, 10], 22), ([8, 4, 16, 18, 9], 23)]
CORNERS = [(7, 1, 1), (8, -1, -1), (9, 1, -1), (10, -1, 1)]


def iota(shape, dim):
    return lax.broadcasted_iota(I32, shape, dim)


def lane_pick(rows, index):
    return jnp.take_along_axis(rows, index, axis=1, mode="promise_in_bounds")


def compact(get, key, val, packed):
    square = (128, 128)
    wide_row, wide_lane = iota((128, 256), 0), iota((128, 256), 1)
    prefix = jnp.where(wide_row <= wide_lane, 1.0, 0.0).astype(BF16)
    before = jnp.zeros(square, F32)
    for b in range(8):
        mask, value = get(b)
        counts = jnp.dot(
            jnp.where(mask, 1.0, 0.0).astype(BF16), prefix, preferred_element_type=F32
        )
        key[b] = jnp.where(mask, counts[:, :128] + before, 0.0)
        val[b] = value
        before = before + counts[:, 128:]

    @pl.loop(0, 4)
    def _(c):
        for u in range(4):
            rows = pl.ds(pl.multiple_of(c * 32 + u * 8, 8), 8)
            keys = [key[b, rows, :] for b in range(8)]
            vals = [val[b, rows, :] for b in range(8)]
            at = iota((8, 128), 1)
            out = jnp.zeros((8, 128), F32)
            for r in range(CAP):
                hit = jnp.zeros((8, 128), F32)
                for b in range(8):
                    hit = jnp.where(keys[b] == float(r + 1), vals[b], hit)
                out = jnp.where(at == r, jnp.sum(hit, axis=1, keepdims=True), out)
            packed[rows, :] = out

    return packed[...]


def split_cell(c):
    c = c.astype(I32) - 1
    live = c >= 0
    a = ((c >> 7) & 15) * ROWS + (c >> 11)
    return jnp.where(live, a, -1), c & 127, live


def split_spot(c):
    c = c.astype(I32) - 1
    live = c >= 0
    return jnp.where(live, c >> 6, -1), c & 63, live


def fill_onehots(row, onehot):
    count = onehot.shape[0]
    for r in range(CAP):
        for q in range(0, count, 128):
            size = min(128, count)
            part = iota((size, 128), 0) + q == row[r : r + 1, :]
            onehot[q : q + size, r * 128 : (r + 1) * 128] = jnp.where(part, 1.0, 0.0).astype(BF16)


def fill_pick(x, y, ids, links, wide, by_slot, pick):
    order = jnp.concatenate([ids[0:1, :], ids[1:2, :]], axis=1)
    chosen = jnp.where(iota((256, 256), 0) == order, 1.0, 0.0).astype(BF16)
    wide[...] = jnp.zeros((128, 256), F32)
    wide[0:6, :] = jnp.dot(
        links.astype(F32).astype(BF16), chosen, preferred_element_type=F32
    )
    by_slot[0:128, :] = jnp.transpose(wide[:, 0:128])
    by_slot[128:256, :] = jnp.transpose(wide[:, 128:256])
    at, to_x = iota((16, 128), 1), iota((16, 128), 0)
    half = jnp.where(x >= GX // 2, ids[1:2, :], ids[0:1, :])
    column = lax.rem(x, GX // 2) * 16 + (at >> 4) * 2 + (at & 1)
    here = lane_pick(jnp.broadcast_to(half.astype(F32), (16, 128)), column)
    side = (at & 15) >> 1
    for b in range(2):
        named = by_slot[pl.ds(2 * y + b, 16, stride=16), :]
        for s in range(6):
            j = s * 2 + b
            n = named[:, s : s + 1]
            remote = (n == here) & (side == SIDE_SWAP[s])
            own = (n < 0.0) & (to_x == x) & (at == y * 16 + j)
            pick[j * 16 : (j + 1) * 16, :] = jnp.where(remote | own, 1.0, 0.0).astype(BF16)


def to_rows(brick):
    at = iota((1, 128), 1)
    rows = []
    for b in range(2):
        for x in range(8):
            part = brick[b : b + 1, (x // 2) * 128 : (x // 2 + 1) * 128]
            part = pltpu.roll(part, 64, 1) if x % 2 else part
            rows.append(jnp.where(at < 64, part, 0.0))
    return jnp.concatenate(rows, axis=0)


def from_rows(rows, out):
    turned = pltpu.roll(rows, 64, 1)
    at = iota((1, 128), 1)
    for b in range(2):
        for q in range(4):
            r = b * 8 + q * 2
            out[b : b + 1, q * 128 : (q + 1) * 128] = jnp.where(
                at < 64, rows[r : r + 1, :], turned[r + 1 : r + 2, :]
            )


def collide(f, g, solid):
    pairs = [(1, 2), (3, 4), (5, 6), (7, 8), (9, 10), (11, 12), (13, 14), (15, 16), (17, 18)]
    total = {a: f[a] + f[b] for a, b in pairs}
    diff = {a: f[a] - f[b] for a, b in pairs}
    density = f[0] + (
        (total[1] + total[3])
        + (total[5] + total[7])
        + (total[9] + total[11])
        + (total[13] + total[15])
        + total[17]
    )
    inverse = 1.0 / density
    ux = (diff[1] + diff[7] + diff[9] + diff[11] + diff[13]) * inverse
    uy = (diff[3] + diff[7] - diff[9] + diff[15] + diff[17]) * inverse
    uz = (diff[5] + diff[11] - diff[13] + diff[15] - diff[17]) * inverse
    temp = g[0] + ((g[1] + g[2]) + (g[3] + g[4]) + (g[5] + g[6]))
    sz = uz + (TAU_FLOW * BUOYANCY) * (temp - 1.0) * inverse
    base = 1.0 - 1.5 * (ux * ux + uy * uy + sz * sz)
    keep = 1.0 - 1.0 / TAU_FLOW
    along_of = {1: ux, 3: uy, 5: sz, 7: ux + uy, 9: ux - uy}
    along_of.update({11: ux + sz, 13: ux - sz, 15: uy + sz, 17: uy - sz})
    out_f = [None] * 19
    k0 = density * (1.0 / 3.0 / TAU_FLOW)
    out_f[0] = jnp.where(solid, f[0], keep * f[0] + k0 * base)
    scale = {1: density * (1.0 / 18.0 / TAU_FLOW), 7: density * (1.0 / 36.0 / TAU_FLOW)}
    for a, b in pairs:
        k = scale[1 if a < 7 else 7]
        along = along_of[a]
        even = k * (base + 4.5 * (along * along))
        odd = (3.0 * k) * along
        out_f[a] = jnp.where(solid, f[b], (even + odd) + keep * f[a])
        out_f[b] = jnp.where(solid, f[a], (even - odd) + keep * f[b])
    keep = 1.0 - 1.0 / TAU_HEAT
    out_g = [None] * 7
    out_g[0] = jnp.where(solid, g[0], keep * g[0] + (0.25 / TAU_HEAT) * temp)
    k = (0.125 / TAU_HEAT) * temp
    for a, u in ((1, ux), (3, uy), (5, uz)):
        odd = (4.0 * k) * u
        out_g[a] = jnp.where(solid, g[a + 1], (k + odd) + keep * g[a])
        out_g[a + 1] = jnp.where(solid, g[a], (k - odd) + keep * g[a + 1])
    return out_f, out_g


def pull(store, pop, t, xb, lane):
    cx, cy, cz = ALL_VELOCITY[pop]
    at = pop

    def tile(step):
        return store[at, pl.ds((t + 1 + step) * PITCH + 8 + xb * 8 - cx, 8), :]

    here = tile(0)
    if cy == 1:
        here = jnp.where(lane >= 128 - NZ, tile(-1), here)
    if cy == -1:
        here = jnp.where(lane < NZ, tile(1), here)
    shift = (cy * NZ + cz) % 128
    if shift:
        here = pltpu.roll(here, shift, 1)
    if cz == 1:
        here = jnp.where(lane & (NZ - 1) == 0, 0.0, here)
    if cz == -1:
        here = jnp.where(lane & (NZ - 1) == NZ - 1, 0.0, here)
    return here


def own_rows(t, xb):
    return pl.ds((t + 1) * PITCH + 8 + xb * 8, 8)


def natural(t, xb):
    return pl.ds(xb * 8, 8), pl.ds(pl.multiple_of(t * 128, 128), 128)


def temp_rows(t, xb):
    return pl.ds(pl.multiple_of(t * ROWS + xb * 8, 8), 8)


def halves(value):
    high = value.astype(BF16)
    return high, (value - high.astype(F32)).astype(BF16)


def scatter(onehot, columns, flux, spread):
    high, low = halves(flux)
    high, low = high.astype(F32), low.astype(F32)
    at = iota((128, 128), 1)
    for r in range(CAP):
        hit = at == columns[:, r : r + 1]
        rows = slice(r * 128, (r + 1) * 128)
        spread[rows, 0:128] = jnp.where(hit, high[:, r : r + 1], 0.0).astype(BF16)
        spread[rows, 128:256] = jnp.where(hit, low[:, r : r + 1], 0.0).astype(BF16)
    both = jnp.dot(onehot[...], spread[...], preferred_element_type=F32)
    return both[:, :128] + both[:, 128:]


def brick_lookup(brick, brow, blrow):
    out = jnp.zeros((CAP, 128), F32)
    for a in range(16):
        row = jnp.broadcast_to(brick[a : a + 1, :], (CAP, 128))
        out = jnp.where(brow == a, lane_pick(row, blrow), out)
    return out


def store_faces(brick, faces):
    at, row = iota((16, 128), 1), iota((16, 128), 0)
    mine = ((at >> 3) & 7) == (row & 7)
    wanted = {
        2: at & 7,
        3: 56 + (at & 7),
        4: (at & 7) * 8,
        5: (at & 7) * 8 + 7,
    }
    faces[12:16, :] = jnp.zeros((4, 128), F32)
    for b in range(2):
        faces[b : b + 1, :] = brick[b * 8 : b * 8 + 1, :]
        faces[2 + b : 3 + b, :] = brick[b * 8 + 7 : b * 8 + 8, :]
    for s, index in wanted.items():
        got = jnp.where(mine, lane_pick(brick, index), 0.0)
        for b in range(2):
            faces[s * 2 + b : s * 2 + b + 1, :] = jnp.sum(
                got[b * 8 : b * 8 + 8], axis=0, keepdims=True
            )


def conduct(brick, ghost, loss):
    at, row = iota((16, 128), 1), iota((16, 128), 0)
    x = row & 7

    def ghost_rows(s):
        return jnp.where(row < 8, ghost[s * 2 : s * 2 + 1, :], ghost[s * 2 + 1 : s * 2 + 2, :])

    over_z = x * 8 + (at & 7)
    over_y = x * 8 + ((at >> 3) & 7)
    beside = [
        jnp.where(x == 0, ghost_rows(0), pltpu.roll(brick, 1, 0)),
        jnp.where(x == 7, ghost_rows(1), pltpu.roll(brick, 15, 0)),
        jnp.where(at < 8, lane_pick(ghost_rows(2), over_z), pltpu.roll(brick, 8, 1)),
        jnp.where(at >= 56, lane_pick(ghost_rows(3), over_z), pltpu.roll(brick, 120, 1)),
        jnp.where((at & 7) == 0, lane_pick(ghost_rows(4), over_y), pltpu.roll(brick, 1, 1)),
        jnp.where((at & 7) == 7, lane_pick(ghost_rows(5), over_y), pltpu.roll(brick, 127, 1)),
    ]
    here = COND_BASE * (1.0 + COND_SLOPE * brick)
    spread = jnp.zeros((16, 128), F32)
    for other in beside:
        spread += 0.5 * (here + COND_BASE * (1.0 + COND_SLOPE * other)) * (other - brick)
    phase = 1.0 / (1.0 + jnp.exp(-(brick - MELT) / MELT_WIDTH))
    capacity = 1.0 + LATENT * phase * (1.0 - phase) / MELT_WIDTH
    return jnp.where(at < 64, brick + (spread - BRICK_LOSS * loss) / capacity, 0.0)


def steps_kernel(
    flow_in,
    heat_in,
    solid_in,
    owners_in,
    spots_in,
    cells_in,
    brick_in,
    ids_in,
    links_in,
    second,
    brick_out,
    first,
    flow,
    heat,
    solid,
    owners,
    spots,
    cells,
    brick_flat,
    ids,
    links,
    key,
    val,
    packed,
    wide,
    by_slot,
    pick,
    oh_cell,
    oh_brick,
    arow,
    lrow,
    lcol,
    brow,
    blrow,
    blcol,
    temps,
    gain,
    spread,
    found,
    asked,
    msg,
    faces,
    brick,
    s1,
    r1,
    s2,
    r2,
    xf,
    xfr,
    yf,
    yfr,
    cf,
    cfr,
    xh,
    xhr,
    yh,
    yhr,
    load_sem,
    s1_send,
    s1_recv,
    s2_send,
    s2_recv,
    flow_send,
    flow_recv,
    heat_send,
    heat_recv,
):
    x, y = lax.axis_index("gx"), lax.axis_index("gy")
    me = x * GY + y

    def xn(k):
        return lax.rem(x + (k + GX), GX)

    def yn(k):
        return lax.rem(y + (k + GY), GY)

    own_faces = pl.ds(pl.multiple_of(me * 8, 8), 8)
    loads = {}
    for n, (name, source, target) in enumerate(
        (
            ("owners", owners_in, owners),
            ("cells", cells_in.at[own_faces, :], cells),
            ("spots", spots_in, spots),
            ("heat", heat_in, heat),
            ("brick", brick_in, brick_flat),
            ("ids", ids_in, ids),
            ("links", links_in, links),
            ("solid", solid_in, solid),
            ("flow", flow_in, flow),
        )
    ):
        loads[name] = pltpu.make_async_copy(source, target, load_sem.at[n])
        loads[name].start()

    barrier = pltpu.get_barrier_semaphore()
    peers = [(x, yn(k)) for k in range(1, GY)] + [(xn(k), y) for k in range(1, GX)]
    peers += [(xn(a), yn(b)) for a in (-1, 1) for b in (-1, 1)]
    for peer in peers:
        pl.semaphore_signal(barrier, inc=1, device_id=peer, device_id_type=MESH)

    lane = iota((8, 128), 1)


    def look_up_row(row, outs, u, a, low):
        line = jnp.broadcast_to(temps[pl.ds(row, 1), :], (CAP, 128))
        outs[u % 4] = jnp.where(a == row, lane_pick(line, low), outs[u % 4])

    def look_up_tiles(start, stop, top, bottom):
        a, low = arow[...], lrow[...]

        def tile(t, outs):
            outs = list(outs)
            for u, row in enumerate(range(top, bottom)):
                look_up_row(t * ROWS + row, outs, u, a, low)
            return tuple(outs)

        outs = lax.fori_loop(start, stop, tile, (jnp.zeros((CAP, 128), F32),) * 4)
        return (outs[0] + outs[1]) + (outs[2] + outs[3])

    def look_up_edges():
        a, low = arow[...], lrow[...]
        outs = [jnp.zeros((CAP, 128), F32)] * 4
        for u, t in enumerate(range(1, TILES - 1)):
            for row in (0, ROWS - 1):
                look_up_row(t * ROWS + row, outs, u, a, low)
        return (outs[0] + outs[1]) + (outs[2] + outs[3])

    def ask():
        now = brick[...]
        asked[...] = brick_lookup(now, brow[...], blrow[...])
        store_faces(now, faces)

    def fill_message():
        rest = jnp.zeros((128 - 2 * CAP, 128), F32)
        msg[...] = jnp.transpose(jnp.concatenate([found[...], asked[...], rest], axis=0))


    def one(step, k, to, slot):
        rows = pl.ds(pl.multiple_of(to * 32, 32), 32)
        place = pl.ds(pl.multiple_of(slot * 32, 32), 32)
        return pltpu.make_async_remote_copy(
            src_ref=s1.at[step, rows, :],
            dst_ref=r1.at[step, place, :],
            send_sem=s1_send.at[step, k],
            recv_sem=s1_recv.at[step, slot],
            device_id=(x, to),
            device_id_type=MESH,
        )

    def two(step, k, to, slot):
        rows = pl.ds(pl.multiple_of(to * 24, 8), 24)
        place = pl.ds(pl.multiple_of(slot * 24, 8), 24)
        return pltpu.make_async_remote_copy(
            src_ref=s2.at[step, rows, :],
            dst_ref=r2.at[step, place, :],
            send_sem=s2_send.at[step, k],
            recv_sem=s2_recv.at[step, slot],
            device_id=(to, y),
            device_id_type=MESH,
        )

    def start_one(step):
        for k in range(GY):
            s1[step, k * 32 : k * 32 + 16, :] = msg[pl.ds(k, 16, stride=8), :]
            s1[step, k * 32 + 16 : k * 32 + 32, :] = faces[...]
        for k in range(1, GY):
            one(step, k, yn(k), y).start()
        own = pl.ds(pl.multiple_of(y * 32, 32), 32)
        r1[step, own, :] = s1[step, own, :]

    def end_one(step):
        for k in range(1, GY):
            one(step, k, yn(k), y).wait_send()
        for k in range(1, GY):
            one(step, k, yn(k), yn(k)).wait_recv()

    def start_two(step):
        every = jnp.concatenate(
            [r1[step, k * 32 + 16 : k * 32 + 32, :] for k in range(GY)], axis=0
        )
        high = every.astype(BF16)
        low = every - high.astype(F32)
        at = iota((128, 128), 1)
        both = jnp.where(at < 64, high.astype(F32), pltpu.roll(low, 64, 1)).astype(BF16)
        picked = jnp.dot(pick[...], both, preferred_element_type=F32)
        picked = picked + pltpu.roll(picked, 64, 1)
        for j in range(12):
            s2[step, pl.ds(8 + j, 16, stride=24), :] = picked[j * 16 : (j + 1) * 16, :]
        for j in range(12, 16):
            s2[step, pl.ds(8 + j, 16, stride=24), :] = jnp.zeros((16, 128), F32)
        for k in range(GX):
            s2[step, k * 24 : k * 24 + 8, :] = r1[step, pl.ds(k, 8, stride=32), :]
        for k in range(1, GX):
            two(step, k, xn(k), x).start()
        own = pl.ds(pl.multiple_of(x * 24, 8), 24)
        r2[step, own, :] = s2[step, own, :]

    def end_two(step):
        for k in range(1, GX):
            two(step, k, xn(k), x).wait_send()
        for k in range(1, GX):
            two(step, k, xn(k), xn(k)).wait_recv()

    def arrived(step):
        return jnp.concatenate([r2[step, k * 24 : k * 24 + 8, :] for k in range(GX)], axis=0)

    def heat_faces(step, store):
        flux = WALL_COEF * (pltpu.roll(arrived(step), 128 - CAP, 1) - msg[...])
        gain[...] = scatter(oh_cell, lcol[...], flux, spread)

        @pl.loop(0, TILES)
        def _(t):
            for xb in range(4):
                more = gain[temp_rows(t, xb), :]
                rows = own_rows(t, xb)
                for j in range(7):
                    store[19 + j, rows, :] = store[19 + j, rows, :] + WEIGHTS_HEAT[j] * more

    def cool_bricks(step):
        flux = WALL_COEF * (pltpu.roll(msg[...], 128 - CAP, 1) - arrived(step))
        loss = scatter(oh_brick, blcol[...], flux, spread)
        ghost = r2[step, 8:24, :]
        for k in range(1, GX):
            ghost = ghost + r2[step, k * 24 + 8 : k * 24 + 24, :]
        brick[...] = conduct(brick[...], ghost, loss)


    ways = [(1, 0), (-1, 0), (0, 1), (0, -1)]
    inside = {(1, 0): x > 0, (-1, 0): x < GX - 1, (0, 1): y > 0, (0, -1): y < GY - 1}
    leave_row, leave_tile = (39, 8), (TILES, 1)
    enter_row, enter_tile = (7, 40), (0, TILES + 1)
    edge_lane = (128 - NZ, 0)

    def plan_copies(step, plan, send, recv):
        return [
            pltpu.make_async_remote_copy(
                src_ref=source,
                dst_ref=target,
                send_sem=send.at[step, n],
                recv_sem=recv.at[step, n],
                device_id=peer,
                device_id_type=MESH,
            )
            for n, (source, target, peer) in enumerate(plan)
        ]

    def flow_copies(step):
        plan = []
        for n, (dx, dy) in enumerate(ways):
            source, target = (xf, xfr) if n < 2 else (yf, yfr)
            plan.append((source.at[step, n % 2], target.at[step, n % 2], (xn(dx), yn(dy))))
        for c, (_, dx, dy) in enumerate(CORNERS):
            plan.append((cf.at[step, c], cfr.at[step, c], (xn(dx), yn(dy))))
        return plan_copies(step, plan, flow_send, flow_recv)

    def heat_copies(step):
        plan = []
        for n, (dx, dy) in enumerate(ways):
            source, target = (xh, xhr) if n < 2 else (yh, yhr)
            plan.append((source.at[step, n % 2], target.at[step, n % 2], (xn(dx), yn(dy))))
        return plan_copies(step, plan, heat_send, heat_recv)

    def send_flow_halo(step, store):
        for n in range(2):
            for k, pop in enumerate(SIDES[n][0]):
                rows = pl.ds(PITCH + leave_row[n], 16, stride=PITCH)
                xf[step, n, k * 16 : (k + 1) * 16, :] = store[pop, rows, :]
        at = iota((32, 128), 1)
        for n in range(2):
            top = leave_tile[n] * PITCH + 8
            parts = []
            for k, pop in enumerate(SIDES[2 + n][0]):
                turn = ((k % 4) * NZ - edge_lane[n]) % 128
                part = store[pop, top : top + 32, :]
                parts.append(pltpu.roll(part, turn, 1) if turn else part)
            for k in range(1, 4):
                parts[0] = jnp.where(at >= k * NZ, parts[k], parts[0])
            yf[step, n, 0:32, :] = parts[0]
            yf[step, n, 32:64, :] = parts[4]
        for c, (pop, dx, dy) in enumerate(CORNERS):
            row = leave_tile[dy < 0] * PITCH + leave_row[dx < 0]
            cf[step, c] = jnp.broadcast_to(store[pop, row : row + 1, :], (8, 128))
        for copy in flow_copies(step):
            copy.start()

    def end_flow_halo(step, store):
        for copy in flow_copies(step):
            copy.wait()
        for n in range(2):
            for k, pop in enumerate(SIDES[n][0]):
                rows = pl.ds(PITCH + enter_row[n], 16, stride=PITCH)
                store[pop, rows, :] = jnp.where(
                    inside[ways[n]], xfr[step, n, k * 16 : (k + 1) * 16, :], 0.0
                )
        for n in range(2):
            top = enter_tile[n] * PITCH + 8
            for k, pop in enumerate(SIDES[2 + n][0]):
                part = yfr[step, n, (k // 4) * 32 : (k // 4 + 1) * 32, :]
                turn = (edge_lane[n] - (k % 4) * NZ) % 128
                part = pltpu.roll(part, turn, 1) if turn else part
                store[pop, top : top + 32, :] = jnp.where(inside[ways[2 + n]], part, 0.0)
        for c, (pop, dx, dy) in enumerate(CORNERS):
            row = enter_tile[dy < 0] * PITCH + enter_row[dx < 0]
            known = inside[(dx, 0)] & inside[(0, dy)]
            store[pop, row : row + 1, :] = jnp.where(known, cfr[step, c, 0:1, :], 0.0)

    def send_heat_halo(step, store):
        for n in range(2):
            rows = pl.ds(PITCH + leave_row[n], 16, stride=PITCH)
            xh[step, n] = store[SIDES[n][1], rows, :]
            top = leave_tile[n] * PITCH + 8
            yh[step, n] = store[SIDES[2 + n][1], top : top + 32, :]
        for copy in heat_copies(step):
            copy.start()

    def end_heat_halo(step, store):
        for copy in heat_copies(step):
            copy.wait()
        for n in range(2):
            rows = pl.ds(PITCH + enter_row[n], 16, stride=PITCH)
            store[SIDES[n][1], rows, :] = jnp.where(inside[ways[n]], xhr[step, n], 0.0)
            top = enter_tile[n] * PITCH + 8
            store[SIDES[2 + n][1], top : top + 32, :] = jnp.where(
                inside[ways[2 + n]], yhr[step, n], 0.0
            )


    def store_relaxed(store, t, xb, f, g):
        out_f, out_g = collide(f, g, solid[natural(t, xb)] == 1)
        rows = own_rows(t, xb)
        for i, value in enumerate(out_f + out_g):
            store[i, rows, :] = value

    def relax_first(low, high):
        @pl.loop(low, high)
        def _(t):
            for xb in range(4):
                rows, lanes = natural(t, xb)
                f = [flow[i, rows, lanes] for i in range(19)]
                g = [heat[j, rows, lanes] for j in range(7)]
                store_relaxed(first, t, xb, f, g)

    def relax_second(low, high):
        @pl.loop(low, high)
        def _(t):
            for xb in range(4):
                f = [pull(first, i, t, xb, lane) for i in range(19)]
                g = [pull(first, 19 + j, t, xb, lane) for j in range(7)]
                store_relaxed(second, t, xb, f, g)

    def sum_heat(g):
        return g[0] + ((g[1] + g[2]) + (g[3] + g[4]) + (g[5] + g[6]))

    def pulled_temp(t, xb):
        temps[temp_rows(t, xb), :] = sum_heat([pull(first, 19 + j, t, xb, lane) for j in range(7)])


    square = (128, 128)
    loads["owners"].wait()
    loads["cells"].wait()
    row_index = iota(square, 0)
    own_owner = owners[own_faces, :]
    own_cell = cells[...].astype(F32) + 1.0
    table = compact(
        lambda b: (
            row_index == own_owner[b : b + 1, :],
            jnp.broadcast_to(own_cell[b : b + 1, :], square),
        ),
        key,
        val,
        packed,
    )
    _, low, live = split_cell(table)
    lcol[...] = jnp.where(live, low, -1)
    a, low, live = split_cell(jnp.transpose(table)[:CAP, :])
    arow[...] = a
    lrow[...] = jnp.where(live, low, 0)

    loads["spots"].wait()

    def from_device(b):
        rows = pl.ds(b, 128, stride=8)
        return owners[rows, :] == me, spots[rows, :].astype(F32) + 1.0

    table = compact(from_device, key, val, packed)
    _, low, live = split_spot(table)
    blcol[...] = jnp.where(live, low, -1)
    a, low, live = split_spot(jnp.transpose(table)[:CAP, :])
    brow[...] = a
    blrow[...] = jnp.where(live, low, 0)


    loads["heat"].wait()

    @pl.loop(0, TILES)
    def _(t):
        for xb in range(4):
            rows, lanes = natural(t, xb)
            temps[temp_rows(t, xb), :] = sum_heat([heat[j, rows, lanes] for j in range(7)])

    found[...] = look_up_tiles(0, TILES, 0, ROWS)
    loads["brick"].wait()
    brick[...] = to_rows(brick_flat[...])
    ask()
    fill_message()
    pl.semaphore_wait(barrier, len(peers))
    start_one(0)
    loads["ids"].wait()
    loads["links"].wait()
    fill_pick(x, y, ids[...], links[...], wide, by_slot, pick)
    fill_onehots(arow[...], oh_cell)
    fill_onehots(brow[...], oh_brick)
    loads["solid"].wait()
    loads["flow"].wait()
    relax_first(0, TILES // 4)
    end_one(0)
    start_two(0)
    relax_first(TILES // 4, TILES)
    send_flow_halo(0, first)
    end_two(0)
    heat_faces(0, first)
    send_heat_halo(0, first)
    cool_bricks(0)
    ask()


    @pl.loop(1, TILES - 1)
    def _(t):
        for xb in range(4):
            pulled_temp(t, xb)

    found[...] = look_up_tiles(1, TILES - 1, 1, ROWS - 1)
    end_heat_halo(0, first)

    @pl.loop(1, TILES - 1)
    def _(t):
        for xb in (0, 3):
            pulled_temp(t, xb)

    for t in (0, TILES - 1):
        for xb in range(4):
            pulled_temp(t, xb)
    found[...] = found[...] + (look_up_edges() + look_up_tiles(0, 1, 0, ROWS))
    found[...] = found[...] + look_up_tiles(TILES - 1, TILES, 0, ROWS)
    fill_message()
    start_one(1)
    end_flow_halo(0, first)
    relax_second(0, TILES // 2)
    end_one(1)
    start_two(1)
    relax_second(TILES // 2, TILES)
    send_flow_halo(1, second)
    end_two(1)
    heat_faces(1, second)
    send_heat_halo(1, second)
    cool_bricks(1)
    from_rows(brick[...], brick_out)
    end_flow_halo(1, second)
    end_heat_halo(1, second)


def spread_kernel(second, flow_out, heat_out):
    lane = iota((8, 128), 1)
    step = pl.program_id(0)
    width = flow_out.shape[2] // 128

    @pl.loop(0, width)
    def _(u):
        t = step * width + u
        for xb in range(4):
            rows, lanes = natural(u, xb)
            for i in range(19):
                flow_out[i, rows, lanes] = pull(second, i, t, xb, lane)
            for j in range(7):
                heat_out[j, rows, lanes] = pull(second, 19 + j, t, xb, lane)


def body(
    flow_pops,
    heat_pops,
    solid_flag,
    brick_temp,
    brick_ids,
    brick_links,
    face_cell,
    face_owner,
    face_spot,
):
    shape = jax.ShapeDtypeStruct
    dma = pltpu.SemaphoreType.DMA
    near = pl.BlockSpec(memory_space=pltpu.VMEM)
    far = pl.BlockSpec(memory_space=pltpu.HBM)
    grid = (TILES * ROWS, 128)
    inputs = (
        flow_pops,
        heat_pops,
        solid_flag,
        face_owner.reshape(1024, 128),
        face_spot.reshape(1024, 128),
        face_cell.reshape(1024, 128),
        brick_temp,
        brick_ids.reshape(2, 128),
        brick_links.T,
    )
    second, brick = pl.pallas_call(
        steps_kernel,
        out_shape=[pltpu.VMEM((26, TALL, 128), F32), shape((2, 512), F32)],
        in_specs=[far] * 9,
        out_specs=[near] * 2,
        scratch_shapes=[
            pltpu.VMEM((26, TALL, 128), F32),
            pltpu.VMEM(flow_pops.shape, F32),
            pltpu.VMEM(heat_pops.shape, F32),
            pltpu.VMEM(solid_flag.shape, I32),
            pltpu.VMEM((1024, 128), I32),
            pltpu.VMEM((1024, 128), I32),
            pltpu.VMEM((8, 128), I32),
            pltpu.VMEM((2, 512), F32),
            pltpu.VMEM((2, 128), I32),
            pltpu.VMEM((6, 256), I32),
            pltpu.VMEM((8, 128, 128), F32),
            pltpu.VMEM((8, 128, 128), F32),
            pltpu.VMEM((128, 128), F32),
            pltpu.VMEM((128, 256), F32),
            pltpu.VMEM((256, 128), F32),
            pltpu.VMEM((192, 128), BF16),
            pltpu.VMEM((TILES * ROWS, SLOTS), BF16),
            pltpu.VMEM((16, SLOTS), BF16),
            pltpu.VMEM((CAP, 128), I32),
            pltpu.VMEM((CAP, 128), I32),
            pltpu.VMEM((128, 128), I32),
            pltpu.VMEM((CAP, 128), I32),
            pltpu.VMEM((CAP, 128), I32),
            pltpu.VMEM((128, 128), I32),
            pltpu.VMEM(grid, F32),
            pltpu.VMEM(grid, F32),
            pltpu.VMEM((SLOTS, 256), BF16),
            pltpu.VMEM((CAP, 128), F32),
            pltpu.VMEM((CAP, 128), F32),
            pltpu.VMEM((128, 128), F32),
            pltpu.VMEM((16, 128), F32),
            pltpu.VMEM((16, 128), F32),
            pltpu.VMEM((2, GY * 32, 128), F32),
            pltpu.VMEM((2, GY * 32, 128), F32),
            pltpu.VMEM((2, GX * 24, 128), F32),
            pltpu.VMEM((2, GX * 24, 128), F32),
            pltpu.VMEM((2, 2, 80, 128), F32),
            pltpu.VMEM((2, 2, 80, 128), F32),
            pltpu.VMEM((2, 2, 64, 128), F32),
            pltpu.VMEM((2, 2, 64, 128), F32),
            pltpu.VMEM((2, 4, 8, 128), F32),
            pltpu.VMEM((2, 4, 8, 128), F32),
            pltpu.VMEM((2, 2, 16, 128), F32),
            pltpu.VMEM((2, 2, 16, 128), F32),
            pltpu.VMEM((2, 2, 32, 128), F32),
            pltpu.VMEM((2, 2, 32, 128), F32),
            dma((9,)),
            dma((2, GY)),
            dma((2, GY)),
            dma((2, GX)),
            dma((2, GX)),
            dma((2, 8)),
            dma((2, 8)),
            dma((2, 4)),
            dma((2, 4)),
        ],
        compiler_params=pltpu.CompilerParams(
            collective_id=0, has_side_effects=True, vmem_limit_bytes=40 << 20
        ),
    )(*(pltpu.with_memory_space_constraint(value, pltpu.HBM) for value in inputs))
    width = 256
    flow, heat = pl.pallas_call(
        spread_kernel,
        grid=(TILES * 128 // width,),
        out_shape=[shape(flow_pops.shape, F32), shape(heat_pops.shape, F32)],
        in_specs=[near],
        out_specs=[
            pl.BlockSpec((19, ROWS, width), lambda i: (0, 0, i)),
            pl.BlockSpec((7, ROWS, width), lambda i: (0, 0, i)),
        ],
        compiler_params=pltpu.CompilerParams(vmem_limit_bytes=16 << 20),
    )(second)
    return flow, heat, brick


def solution(mesh):
    return jax.shard_map(
        body,
        mesh=mesh,
        in_specs=(
            P(None, "gx", "gy"),
            P(None, "gx", "gy"),
            P("gx", "gy"),
            P(("gx", "gy"), None),
            P(),
            P(),
            P(),
            P(),
            P(),
        ),
        out_specs=(P(None, "gx", "gy"), P(None, "gx", "gy"), P(("gx", "gy"), None)),
        check_vma=False,
    )
```

```python
import functools

import jax
import jax.numpy as jnp
from jax import lax
from jax.experimental import pallas as pl
from jax.experimental.pallas import tpu as pltpu
from jax.sharding import PartitionSpec as P

MESH = pl.DeviceIdType.MESH
F32, BF16, I32 = jnp.float32, jnp.bfloat16, jnp.int32

VELOCITY = [
    (0, 0, 0),
    (1, 0, 0),
    (-1, 0, 0),
    (0, 1, 0),
    (0, -1, 0),
    (0, 0, 1),
    (0, 0, -1),
    (1, 1, 0),
    (-1, -1, 0),
    (1, -1, 0),
    (-1, 1, 0),
    (1, 0, 1),
    (-1, 0, -1),
    (1, 0, -1),
    (-1, 0, 1),
    (0, 1, 1),
    (0, -1, -1),
    (0, 1, -1),
    (0, -1, 1),
]
SIDE_SWAP = [1, 0, 3, 2, 5, 4]
WEIGHTS_HEAT = [0.25] + [0.125] * 6
TAU_FLOW, TAU_HEAT = 0.8, 0.9
BUOYANCY = 0.002
WALL_COEF = 0.1
BRICK_LOSS = 0.5
COND_BASE, COND_SLOPE = 0.04, 0.1
LATENT, MELT, MELT_WIDTH = 2.0, 4.0, 0.5

GX, GY = 16, 8
DEV = GX * GY
CAP = 16
ROWS, TILES, NZ = 32, 16, 32
PITCH = 48
TALL = (TILES + 2) * PITCH
SLOTS = CAP * DEV

ALL_VELOCITY = VELOCITY + VELOCITY[:7]
SIDES = [([9, 1, 11, 13, 7], 20), ([10, 2, 12, 14, 8], 21)]
SIDES += [([7, 3, 15, 17, 10], 22), ([8, 4, 16, 18, 9], 23)]
CORNERS = [(7, 1, 1), (8, -1, -1), (9, 1, -1), (10, -1, 1)]


def iota(shape, dim):
    return lax.broadcasted_iota(I32, shape, dim)


def lane_pick(rows, index):
    return jnp.take_along_axis(rows, index, axis=1, mode="promise_in_bounds")


def compact(get, key, val, packed):
    square = (128, 128)
    wide_row, wide_lane = iota((128, 256), 0), iota((128, 256), 1)
    prefix = jnp.where(wide_row <= wide_lane, 1.0, 0.0).astype(BF16)
    before = jnp.zeros(square, F32)
    for b in range(8):
        mask, value = get(b)
        counts = jnp.dot(
            jnp.where(mask, 1.0, 0.0).astype(BF16), prefix, preferred_element_type=F32
        )
        key[b] = jnp.where(mask, counts[:, :128] + before, 0.0)
        val[b] = value
        before = before + counts[:, 128:]

    @pl.loop(0, 4)
    def _(c):
        for u in range(4):
            rows = pl.ds(pl.multiple_of(c * 32 + u * 8, 8), 8)
            keys = [key[b, rows, :] for b in range(8)]
            vals = [val[b, rows, :] for b in range(8)]
            at = iota((8, 128), 1)
            out = jnp.zeros((8, 128), F32)
            for r in range(CAP):
                hit = jnp.zeros((8, 128), F32)
                for b in range(8):
                    hit = jnp.where(keys[b] == float(r + 1), vals[b], hit)
                out = jnp.where(at == r, jnp.sum(hit, axis=1, keepdims=True), out)
            packed[rows, :] = out

    return packed[...]


def split_cell(c):
    c = c.astype(I32) - 1
    live = c >= 0
    a = ((c >> 7) & 15) * ROWS + (c >> 11)
    return jnp.where(live, a, -1), c & 127, live


def split_spot(c):
    c = c.astype(I32) - 1
    live = c >= 0
    return jnp.where(live, c >> 6, -1), c & 63, live


def fill_onehots(row, onehot):
    count = onehot.shape[0]
    for r in range(CAP):
        for q in range(0, count, 128):
            size = min(128, count)
            part = iota((size, 128), 0) + q == row[r : r + 1, :]
            onehot[q : q + size, r * 128 : (r + 1) * 128] = jnp.where(part, 1.0, 0.0).astype(BF16)


def ranked(device):
    return (((device >> 2) & 1) << 6) | ((device >> 4) << 3) | (((device >> 3) & 1) << 2) | (device & 3)


def fill_pick(spot, ids, links, wide, by_slot, pick):
    core, xc, ylo, q, inner, outer = spot
    order = jnp.concatenate([ids[0:1, :], ids[1:2, :]], axis=1)
    chosen = jnp.where(iota((256, 256), 0) == order, 1.0, 0.0).astype(BF16)
    wide[...] = jnp.zeros((128, 256), F32)
    wide[0:6, :] = jnp.dot(
        links.astype(F32).astype(BF16), chosen, preferred_element_type=F32
    )
    by_slot[0:128, :] = jnp.transpose(wide[:, 0:128])
    by_slot[128:256, :] = jnp.transpose(wide[:, 128:256])
    at, to = iota((16, 128), 1), iota((16, 128), 0)
    half = jnp.where(q >= 4, ids[1:2, :], ids[0:1, :])
    from_b, from_inner, side = at >> 6, (at >> 3) & 7, at & 7
    column = lax.rem(q, 4) * 32 + (from_inner >> 2) * 16 + ylo * 8 + (from_inner & 3) * 2 + from_b
    here = lane_pick(jnp.broadcast_to(half.astype(F32), (16, 128)), column)
    for b in range(2):
        named = jnp.concatenate(
            [
                by_slot[pl.ds((core * 8 + low * 4 + xc) * 2 + b, 8, stride=32), :]
                for low in range(2)
            ],
            axis=0,
        )
        for s in range(6):
            j = s * 2 + b
            n = named[:, s : s + 1]
            remote = (n == here) & (side == SIDE_SWAP[s])
            own = (n < 0.0) & (to == outer) & (at == b * 64 + inner * 8 + s)
            pick[j * 16 : (j + 1) * 16, :] = jnp.where(remote | own, 1.0, 0.0).astype(BF16)


def to_rows(brick):
    at = iota((1, 128), 1)
    rows = []
    for b in range(2):
        for x in range(8):
            part = brick[b : b + 1, (x // 2) * 128 : (x // 2 + 1) * 128]
            part = pltpu.roll(part, 64, 1) if x % 2 else part
            rows.append(jnp.where(at < 64, part, 0.0))
    return jnp.concatenate(rows, axis=0)


def from_rows(rows, out):
    turned = pltpu.roll(rows, 64, 1)
    at = iota((1, 128), 1)
    for b in range(2):
        for q in range(4):
            r = b * 8 + q * 2
            out[b : b + 1, q * 128 : (q + 1) * 128] = jnp.where(
                at < 64, rows[r : r + 1, :], turned[r + 1 : r + 2, :]
            )


def collide(f, g, solid):
    pairs = [(1, 2), (3, 4), (5, 6), (7, 8), (9, 10), (11, 12), (13, 14), (15, 16), (17, 18)]
    total = {a: f[a] + f[b] for a, b in pairs}
    diff = {a: f[a] - f[b] for a, b in pairs}
    density = f[0] + (
        (total[1] + total[3])
        + (total[5] + total[7])
        + (total[9] + total[11])
        + (total[13] + total[15])
        + total[17]
    )
    inverse = 1.0 / density
    ux = (diff[1] + diff[7] + diff[9] + diff[11] + diff[13]) * inverse
    uy = (diff[3] + diff[7] - diff[9] + diff[15] + diff[17]) * inverse
    uz = (diff[5] + diff[11] - diff[13] + diff[15] - diff[17]) * inverse
    temp = g[0] + ((g[1] + g[2]) + (g[3] + g[4]) + (g[5] + g[6]))
    sz = uz + (TAU_FLOW * BUOYANCY) * (temp - 1.0) * inverse
    base = 1.0 - 1.5 * (ux * ux + uy * uy + sz * sz)
    keep = 1.0 - 1.0 / TAU_FLOW
    along_of = {1: ux, 3: uy, 5: sz, 7: ux + uy, 9: ux - uy}
    along_of.update({11: ux + sz, 13: ux - sz, 15: uy + sz, 17: uy - sz})
    out_f = [None] * 19
    k0 = density * (1.0 / 3.0 / TAU_FLOW)
    out_f[0] = jnp.where(solid, f[0], keep * f[0] + k0 * base)
    scale = {1: density * (1.0 / 18.0 / TAU_FLOW), 7: density * (1.0 / 36.0 / TAU_FLOW)}
    for a, b in pairs:
        k = scale[1 if a < 7 else 7]
        along = along_of[a]
        even = k * (base + 4.5 * (along * along))
        odd = (3.0 * k) * along
        out_f[a] = jnp.where(solid, f[b], (even + odd) + keep * f[a])
        out_f[b] = jnp.where(solid, f[a], (even - odd) + keep * f[b])
    keep = 1.0 - 1.0 / TAU_HEAT
    out_g = [None] * 7
    out_g[0] = jnp.where(solid, g[0], keep * g[0] + (0.25 / TAU_HEAT) * temp)
    k = (0.125 / TAU_HEAT) * temp
    for a, u in ((1, ux), (3, uy), (5, uz)):
        odd = (4.0 * k) * u
        out_g[a] = jnp.where(solid, g[a + 1], (k + odd) + keep * g[a])
        out_g[a + 1] = jnp.where(solid, g[a], (k - odd) + keep * g[a + 1])
    return out_f, out_g


class Lattice:
    def __init__(self, flow, heat):
        self.flow, self.heat = flow, heat

    def at(self, key):
        pop = key[0]
        if pop < 19:
            return self.flow, key
        return self.heat, (pop - 19,) + tuple(key[1:])

    def __getitem__(self, key):
        ref, key = self.at(key)
        return ref[key]

    def __setitem__(self, key, value):
        ref, key = self.at(key)
        ref[key] = value


def pull(store, pop, t, xb, lane):
    cx, cy, cz = ALL_VELOCITY[pop]
    at = pop

    def tile(step):
        return store[at, pl.ds((t + 1 + step) * PITCH + 8 + xb * 8 - cx, 8), :]

    here = tile(0)
    if cy == 1:
        here = jnp.where(lane >= 128 - NZ, tile(-1), here)
    if cy == -1:
        here = jnp.where(lane < NZ, tile(1), here)
    shift = (cy * NZ + cz) % 128
    if shift:
        here = pltpu.roll(here, shift, 1)
    if cz == 1:
        here = jnp.where(lane & (NZ - 1) == 0, 0.0, here)
    if cz == -1:
        here = jnp.where(lane & (NZ - 1) == NZ - 1, 0.0, here)
    return here


def own_rows(t, xb):
    return pl.ds((t + 1) * PITCH + 8 + xb * 8, 8)


def natural(t, xb):
    return pl.ds(xb * 8, 8), pl.ds(pl.multiple_of(t * 128, 128), 128)


def temp_rows(t, xb):
    return pl.ds(pl.multiple_of(t * ROWS + xb * 8, 8), 8)


def halves(value):
    high = value.astype(BF16)
    return high, (value - high.astype(F32)).astype(BF16)


def scatter(onehot, columns, flux, spread):
    high, low = halves(flux)
    high, low = high.astype(F32), low.astype(F32)
    at = iota((128, 128), 1)
    for r in range(CAP):
        hit = at == columns[:, r : r + 1]
        rows = slice(r * 128, (r + 1) * 128)
        spread[rows, 0:128] = jnp.where(hit, high[:, r : r + 1], 0.0).astype(BF16)
        spread[rows, 128:256] = jnp.where(hit, low[:, r : r + 1], 0.0).astype(BF16)
    both = jnp.dot(onehot[...], spread[...], preferred_element_type=F32)
    return both[:, :128] + both[:, 128:]


def brick_lookup(brick, brow, blrow):
    out = jnp.zeros((CAP, 128), F32)
    for a in range(16):
        row = jnp.broadcast_to(brick[a : a + 1, :], (CAP, 128))
        out = jnp.where(brow == a, lane_pick(row, blrow), out)
    return out


def store_faces(brick, faces):
    at, row = iota((16, 128), 1), iota((16, 128), 0)
    line = iota((1, 128), 1)
    mine = ((at >> 3) & 7) == (row & 7)
    wanted = {
        2: at & 7,
        3: 56 + (at & 7),
        4: (at & 7) * 8,
        5: (at & 7) * 8 + 7,
    }
    faces[6:8, :] = jnp.zeros((2, 128), F32)
    for s in range(6):
        if s < 2:
            low, high = brick[7 * s : 7 * s + 1, :], brick[8 + 7 * s : 9 + 7 * s, :]
        else:
            got = jnp.where(mine, lane_pick(brick, wanted[s]), 0.0)
            low = jnp.sum(got[0:8], axis=0, keepdims=True)
            high = jnp.sum(got[8:16], axis=0, keepdims=True)
        faces[s : s + 1, :] = jnp.where(line < 64, low, pltpu.roll(high, 64, 1))


def conduct(brick, ghost, loss):
    at, row = iota((16, 128), 1), iota((16, 128), 0)
    x = row & 7

    other_brick = pltpu.roll(ghost, 64, 1)

    def ghost_rows(s):
        return jnp.where(row < 8, ghost[s : s + 1, :], other_brick[s : s + 1, :])

    over_z = x * 8 + (at & 7)
    over_y = x * 8 + ((at >> 3) & 7)
    beside = [
        jnp.where(x == 0, ghost_rows(0), pltpu.roll(brick, 1, 0)),
        jnp.where(x == 7, ghost_rows(1), pltpu.roll(brick, 15, 0)),
        jnp.where(at < 8, lane_pick(ghost_rows(2), over_z), pltpu.roll(brick, 8, 1)),
        jnp.where(at >= 56, lane_pick(ghost_rows(3), over_z), pltpu.roll(brick, 120, 1)),
        jnp.where((at & 7) == 0, lane_pick(ghost_rows(4), over_y), pltpu.roll(brick, 1, 1)),
        jnp.where((at & 7) == 7, lane_pick(ghost_rows(5), over_y), pltpu.roll(brick, 127, 1)),
    ]
    here = COND_BASE * (1.0 + COND_SLOPE * brick)
    spread = jnp.zeros((16, 128), F32)
    for other in beside:
        spread += 0.5 * (here + COND_BASE * (1.0 + COND_SLOPE * other)) * (other - brick)
    phase = 1.0 / (1.0 + jnp.exp(-(brick - MELT) / MELT_WIDTH))
    capacity = 1.0 + LATENT * phase * (1.0 - phase) / MELT_WIDTH
    return jnp.where(at < 64, brick + (spread - BRICK_LOSS * loss) / capacity, 0.0)


def steps_kernel(
    flow_in,
    heat_in,
    solid_in,
    owners_in,
    spots_in,
    cells_in,
    brick_in,
    ids_in,
    links_in,
    flow_out,
    second_heat,
    brick_out,
    first,
    second_flow,
    flow,
    heat,
    solid,
    owners,
    spots,
    cells,
    brick_flat,
    ids,
    links,
    key,
    val,
    packed,
    reordered,
    wide,
    by_slot,
    pick,
    oh_cell,
    oh_brick,
    arow,
    lrow,
    lcol,
    brow,
    blrow,
    blcol,
    temps,
    gain,
    spread,
    found,
    asked,
    msg,
    faces,
    brick,
    s1,
    r1,
    s2,
    r2,
    xf,
    xfr,
    yf,
    yfr,
    cf,
    cfr,
    xh,
    xhr,
    yh,
    yhr,
    load_sem,
    s1_send,
    s1_recv,
    s2_send,
    s2_recv,
    flow_send,
    flow_recv,
    heat_send,
    heat_recv,
):
    x, y = lax.axis_index("gx"), lax.axis_index("gy")
    me = x * GY + y
    core, q = lax.rem(x, 2), x // 2
    xc, ylo = lax.rem(y, 4), y // 4
    inner, outer = core * 4 + xc, ylo * 8 + q

    def inner_peer(i):
        return (q * 2 + i // 4, ylo * 4 + lax.rem(i, 4))

    def outer_peer(h):
        return (lax.rem(h, 8) * 2 + core, (h // 8) * 4 + xc)

    def inner_next(k):
        return lax.rem(inner + k, 8)

    def outer_next(k):
        return lax.rem(outer + k, 16)

    def xn(k):
        return lax.rem(x + (k + GX), GX)

    def yn(k):
        return lax.rem(y + (k + GY), GY)

    second = Lattice(second_flow, second_heat)
    own_faces = pl.ds(pl.multiple_of(me * 8, 8), 8)
    loads = {}
    for n, (name, source, target) in enumerate(
        (
            ("owners", owners_in, owners),
            ("cells", cells_in.at[own_faces, :], cells),
            ("spots", spots_in, spots),
            ("heat", heat_in, heat),
            ("brick", brick_in, brick_flat),
            ("ids", ids_in, ids),
            ("links", links_in, links),
            ("solid", solid_in, solid),
            ("flow", flow_in, flow),
        )
    ):
        loads[name] = pltpu.make_async_copy(source, target, load_sem.at[n])
        loads[name].start()

    barrier = pltpu.get_barrier_semaphore()
    peers = [inner_peer(inner_next(k)) for k in range(1, 8)]
    peers += [outer_peer(outer_next(k)) for k in range(1, 16)]
    peers += [(xn(a), yn(b)) for a in (-1, 0, 1) for b in (-1, 0, 1) if a or b]
    for peer in peers:
        pl.semaphore_signal(barrier, inc=1, device_id=peer, device_id_type=MESH)

    lane = iota((8, 128), 1)


    def look_up_row(row, outs, u, a, low):
        line = jnp.broadcast_to(temps[pl.ds(row, 1), :], (CAP, 128))
        outs[u % 4] = jnp.where(a == row, lane_pick(line, low), outs[u % 4])

    def look_up(inner_only):
        parts = []
        for n in range(4):
            part = temps[n * 128 : (n + 1) * 128, :]
            if inner_only:
                row = iota((128, 128), 0)
                away = (row & 31 != 0) & (row & 31 != 31)
                if n == 0:
                    away = away & (row >= 32)
                if n == 3:
                    away = away & (row < 96)
                part = jnp.where(away, part, 0.0)
            parts.append(jnp.transpose(part))
        high, low = halves(jnp.concatenate(parts, axis=1))
        both = jnp.concatenate([high, low], axis=0)
        lanes = lrow[...]
        at = iota((128, 128), 0)
        for r in range(0, CAP, 2):
            got = jnp.dot(
                both, oh_cell[:, r * 128 : (r + 2) * 128], preferred_element_type=F32
            )
            got = got[:128] + got[128:]
            for u in range(2):
                hit = jnp.where(
                    at == lanes[r + u : r + u + 1, :], got[:, u * 128 : (u + 1) * 128], 0.0
                )
                found[r + u : r + u + 1, :] = jnp.sum(hit, axis=0, keepdims=True)

    def look_up_edges():
        a, low = arow[...], lrow[...]
        outs = [jnp.zeros((CAP, 128), F32)] * 4
        rows = [t * ROWS + row for t in range(1, TILES - 1) for row in (0, ROWS - 1)]
        rows += [t * ROWS + row for t in (0, TILES - 1) for row in range(ROWS)]
        for u, row in enumerate(rows):
            look_up_row(row, outs, u, a, low)
        return (outs[0] + outs[1]) + (outs[2] + outs[3])

    def ask():
        now = brick[...]
        asked[...] = brick_lookup(now, brow[...], blrow[...])
        store_faces(now, faces)

    def fill_message(n, temperatures, bricks):
        none = jnp.zeros((CAP, 128), F32)
        parts = [found[...] if temperatures else none, asked[...] if bricks else none]
        rest = jnp.zeros((128 - 2 * CAP, 128), F32)
        msg[n] = jnp.transpose(jnp.concatenate(parts + [rest], axis=0))


    def one(n, k, to, slot):
        count = 16 if n == 2 else 24
        return pltpu.make_async_remote_copy(
            src_ref=s1.at[n, pl.ds(pl.multiple_of(to * 24, 8), count), :],
            dst_ref=r1.at[n, pl.ds(pl.multiple_of(slot * 24, 8), count), :],
            send_sem=s1_send.at[n, k],
            recv_sem=s1_recv.at[n, slot],
            device_id=inner_peer(to),
            device_id_type=MESH,
        )

    def two(n, k, to, slot):
        count = 8 if n == 2 else 16
        return pltpu.make_async_remote_copy(
            src_ref=s2.at[n, pl.ds(pl.multiple_of(to * 16, 8), count), :],
            dst_ref=r2.at[n, pl.ds(pl.multiple_of(slot * 16, 8), count), :],
            send_sem=s2_send.at[n, k],
            recv_sem=s2_recv.at[n, slot],
            device_id=outer_peer(to),
            device_id_type=MESH,
        )

    def start_one(n):
        for k in range(8):
            s1[n, k * 24 : k * 24 + 16, :] = msg[n, pl.ds(k, 16, stride=8), :]
            if n < 2:
                s1[n, k * 24 + 16 : k * 24 + 24, :] = faces[...]
        for k in range(1, 8):
            one(n, k, inner_next(k), inner).start()
        own = pl.ds(pl.multiple_of(inner * 24, 8), 24)
        r1[n, own, :] = s1[n, own, :]

    def end_one(n):
        for k in range(1, 8):
            one(n, k, inner_next(k), inner_next(k)).wait_recv()

    def start_two(n):
        if n < 2:
            every = jnp.concatenate(
                [r1[n, k * 24 + 16 : k * 24 + 24, :] for k in range(8)], axis=0
            )
            every = jnp.concatenate([every, pltpu.roll(every, 64, 1)], axis=0)
            high = every.astype(BF16)
            low = every - high.astype(F32)
            at = iota((128, 128), 1)
            both = jnp.where(at < 64, high.astype(F32), pltpu.roll(low, 64, 1)).astype(BF16)
            picked = jnp.dot(pick[...], both, preferred_element_type=F32)
            picked = picked + pltpu.roll(picked, 64, 1)
            at = iota((16, 128), 1)
            for s in range(8):
                pair = jnp.zeros((16, 128), F32)
                if s < 6:
                    top = s * 32
                    pair = jnp.where(at < 64, picked[top : top + 16], picked[top + 16 : top + 32])
                s2[n, pl.ds(8 + s, 16, stride=16), :] = pair
        for h in range(16):
            s2[n, h * 16 : h * 16 + 8, :] = r1[n, pl.ds(h, 8, stride=24), :]
        for k in range(1, 16):
            two(n, k, outer_next(k), outer).start()
        own = pl.ds(pl.multiple_of(outer * 16, 8), 16)
        r2[n, own, :] = s2[n, own, :]

    def end_two(n):
        for k in range(1, 16):
            two(n, k, outer_next(k), outer_next(k)).wait_recv()

    def end_sends(n):
        for k in range(1, 8):
            one(n, k, inner_next(k), inner).wait_send()
        for k in range(1, 16):
            two(n, k, outer_next(k), outer).wait_send()

    def arrived(n):
        return jnp.concatenate([r2[n, h * 16 : h * 16 + 8, :] for h in range(16)], axis=0)

    def heat_faces(store, came, mine):
        flux = WALL_COEF * (pltpu.roll(arrived(came), 128 - CAP, 1) - msg[mine])
        gain[...] = scatter(oh_cell, lcol[...], flux, spread)

        @pl.loop(0, TILES)
        def _(t):
            for xb in range(4):
                more = gain[temp_rows(t, xb), :]
                rows = own_rows(t, xb)
                for j in range(7):
                    store[19 + j, rows, :] = store[19 + j, rows, :] + WEIGHTS_HEAT[j] * more

    def cool_bricks(came, mine, layers):
        flux = WALL_COEF * (pltpu.roll(msg[mine], 128 - CAP, 1) - arrived(came))
        loss = scatter(oh_brick, blcol[...], flux, spread)
        ghost = r2[layers, 8:16, :]
        for h in range(1, 16):
            ghost = ghost + r2[layers, h * 16 + 8 : h * 16 + 16, :]
        brick[...] = conduct(brick[...], ghost, loss)


    ways = [(1, 0), (-1, 0), (0, 1), (0, -1)]
    inside = {(1, 0): x > 0, (-1, 0): x < GX - 1, (0, 1): y > 0, (0, -1): y < GY - 1}
    leave_row, leave_tile = (39, 8), (TILES, 1)
    enter_row, enter_tile = (7, 40), (0, TILES + 1)
    edge_lane = (128 - NZ, 0)

    def plan_copies(step, plan, send, recv):
        return [
            pltpu.make_async_remote_copy(
                src_ref=source,
                dst_ref=target,
                send_sem=send.at[step, n],
                recv_sem=recv.at[step, n],
                device_id=peer,
                device_id_type=MESH,
            )
            for n, (source, target, peer) in enumerate(plan)
        ]

    def flow_copies(step):
        plan = []
        for n, (dx, dy) in enumerate(ways):
            source, target = (xf, xfr) if n < 2 else (yf, yfr)
            plan.append((source.at[step, n % 2], target.at[step, n % 2], (xn(dx), yn(dy))))
        for c, (_, dx, dy) in enumerate(CORNERS):
            plan.append((cf.at[step, c], cfr.at[step, c], (xn(dx), yn(dy))))
        return plan_copies(step, plan, flow_send, flow_recv)

    def heat_copies(step):
        plan = []
        for n, (dx, dy) in enumerate(ways):
            source, target = (xh, xhr) if n < 2 else (yh, yhr)
            plan.append((source.at[step, n % 2], target.at[step, n % 2], (xn(dx), yn(dy))))
        return plan_copies(step, plan, heat_send, heat_recv)

    def send_flow_halo(step, store):
        for n in range(2):
            for k, pop in enumerate(SIDES[n][0]):
                rows = pl.ds(PITCH + leave_row[n], 16, stride=PITCH)
                xf[step, n, k * 16 : (k + 1) * 16, :] = store[pop, rows, :]
        at = iota((32, 128), 1)
        for n in range(2):
            top = leave_tile[n] * PITCH + 8
            parts = []
            for k, pop in enumerate(SIDES[2 + n][0]):
                turn = ((k % 4) * NZ - edge_lane[n]) % 128
                part = store[pop, top : top + 32, :]
                parts.append(pltpu.roll(part, turn, 1) if turn else part)
            for k in range(1, 4):
                parts[0] = jnp.where(at >= k * NZ, parts[k], parts[0])
            yf[step, n, 0:32, :] = parts[0]
            yf[step, n, 32:64, :] = parts[4]
        for c, (pop, dx, dy) in enumerate(CORNERS):
            row = leave_tile[dy < 0] * PITCH + leave_row[dx < 0]
            cf[step, c] = jnp.broadcast_to(store[pop, row : row + 1, :], (8, 128))
        for copy in flow_copies(step):
            copy.start()

    def end_flow_halo(step, store):
        for copy in flow_copies(step):
            copy.wait()
        for n in range(2):
            for k, pop in enumerate(SIDES[n][0]):
                rows = pl.ds(PITCH + enter_row[n], 16, stride=PITCH)
                store[pop, rows, :] = jnp.where(
                    inside[ways[n]], xfr[step, n, k * 16 : (k + 1) * 16, :], 0.0
                )
        for n in range(2):
            top = enter_tile[n] * PITCH + 8
            for k, pop in enumerate(SIDES[2 + n][0]):
                part = yfr[step, n, (k // 4) * 32 : (k // 4 + 1) * 32, :]
                turn = (edge_lane[n] - (k % 4) * NZ) % 128
                part = pltpu.roll(part, turn, 1) if turn else part
                store[pop, top : top + 32, :] = jnp.where(inside[ways[2 + n]], part, 0.0)
        for c, (pop, dx, dy) in enumerate(CORNERS):
            row = enter_tile[dy < 0] * PITCH + enter_row[dx < 0]
            known = inside[(dx, 0)] & inside[(0, dy)]
            store[pop, row : row + 1, :] = jnp.where(known, cfr[step, c, 0:1, :], 0.0)

    def send_heat_halo(step, store):
        for n in range(2):
            rows = pl.ds(PITCH + leave_row[n], 16, stride=PITCH)
            xh[step, n] = store[SIDES[n][1], rows, :]
            top = leave_tile[n] * PITCH + 8
            yh[step, n] = store[SIDES[2 + n][1], top : top + 32, :]
        for copy in heat_copies(step):
            copy.start()

    def end_heat_halo(step, store):
        for copy in heat_copies(step):
            copy.wait()
        for n in range(2):
            rows = pl.ds(PITCH + enter_row[n], 16, stride=PITCH)
            store[SIDES[n][1], rows, :] = jnp.where(inside[ways[n]], xhr[step, n], 0.0)
            top = enter_tile[n] * PITCH + 8
            store[SIDES[2 + n][1], top : top + 32, :] = jnp.where(
                inside[ways[2 + n]], yhr[step, n], 0.0
            )


    def store_relaxed(store, t, xb, f, g):
        out_f, out_g = collide(f, g, solid[natural(t, xb)] == 1)
        rows = own_rows(t, xb)
        for i, value in enumerate(out_f + out_g):
            store[i, rows, :] = value

    def relax_first(low, high):
        @pl.loop(low, high)
        def _(t):
            for xb in range(4):
                rows, lanes = natural(t, xb)
                f = [flow[i, rows, lanes] for i in range(19)]
                g = [heat[j, rows, lanes] for j in range(7)]
                store_relaxed(first, t, xb, f, g)

    def relax_second(low, high):
        @pl.loop(low, high)
        def _(t):
            for xb in range(4):
                f = [pull(first, i, t, xb, lane) for i in range(19)]
                g = [pull(first, 19 + j, t, xb, lane) for j in range(7)]
                store_relaxed(second, t, xb, f, g)

    def sum_heat(g):
        return g[0] + ((g[1] + g[2]) + (g[3] + g[4]) + (g[5] + g[6]))

    def pulled_temp(t, xb):
        temps[temp_rows(t, xb), :] = sum_heat([pull(first, 19 + j, t, xb, lane) for j in range(7)])


    square = (128, 128)
    loads["owners"].wait()
    loads["cells"].wait()
    row_index = iota(square, 0)
    own_place = ranked(owners[own_faces, :])
    own_cell = cells[...].astype(F32) + 1.0
    table = compact(
        lambda b: (
            row_index == own_place[b : b + 1, :],
            jnp.broadcast_to(own_cell[b : b + 1, :], square),
        ),
        key,
        val,
        packed,
    )
    _, low, live = split_cell(table)
    lcol[...] = jnp.where(live, low, -1)
    a, low, live = split_cell(jnp.transpose(table)[:CAP, :])
    arow[...] = a
    lrow[...] = jnp.where(live, low, 0)

    loads["spots"].wait()

    def from_device(b):
        rows = pl.ds(b, 128, stride=8)
        return owners[rows, :] == me, spots[rows, :].astype(F32) + 1.0

    table = compact(from_device, key, val, packed)
    for n in range(32):
        source = ((n >> 1) & 7) * 16 + (n & 1) * 8 + (n >> 4) * 4
        reordered[n * 4 : n * 4 + 4, :] = packed[source : source + 4, :]
    table = reordered[...]
    _, low, live = split_spot(table)
    blcol[...] = jnp.where(live, low, -1)
    a, low, live = split_spot(jnp.transpose(table)[:CAP, :])
    brow[...] = a
    blrow[...] = jnp.where(live, low, 0)


    loads["heat"].wait()

    @pl.loop(0, TILES)
    def _(t):
        for xb in range(4):
            rows, lanes = natural(t, xb)
            temps[temp_rows(t, xb), :] = sum_heat([heat[j, rows, lanes] for j in range(7)])

    fill_onehots(arow[...], oh_cell)
    look_up(False)
    loads["brick"].wait()
    brick[...] = to_rows(brick_flat[...])
    ask()
    fill_message(0, True, True)
    pl.semaphore_wait(barrier, len(peers))
    start_one(0)
    loads["ids"].wait()
    loads["links"].wait()
    place = (core, xc, ylo, q, inner, outer)
    fill_pick(place, ids[...], links[...], wide, by_slot, pick)
    fill_onehots(brow[...], oh_brick)
    loads["solid"].wait()
    loads["flow"].wait()
    relax_first(0, TILES // 4)
    end_one(0)
    start_two(0)
    relax_first(TILES // 4, TILES)
    send_flow_halo(0, first)
    end_two(0)
    heat_faces(first, 0, 0)
    send_heat_halo(0, first)
    cool_bricks(0, 0, 0)
    ask()
    fill_message(1, False, True)
    start_one(1)


    @pl.loop(0, (TILES - 2) // 2)
    def _(n):
        for u in range(2):
            for xb in range(4):
                pulled_temp(1 + 2 * n + u, xb)

    look_up(True)
    end_one(1)
    start_two(1)
    end_heat_halo(0, first)
    for t in range(TILES):
        for xb in range(4):
            if t in (0, TILES - 1) or xb in (0, 3):
                pulled_temp(t, xb)
    found[...] = found[...] + look_up_edges()
    fill_message(2, True, False)
    start_one(2)
    end_flow_halo(0, first)
    relax_second(0, 8)
    end_one(2)
    start_two(2)
    relax_second(8, TILES)
    send_flow_halo(1, second)
    end_two(1)
    heat_faces(second, 1, 2)
    send_heat_halo(1, second)
    end_flow_halo(1, second)

    @pl.loop(0, TILES)
    def _(t):
        for xb in range(4):
            for i in range(19):
                rows, lanes = natural(t, xb)
                flow_out[i, rows, lanes] = pull(second, i, t, xb, lane)

    end_sends(0)
    end_sends(1)
    end_two(2)
    cool_bricks(2, 1, 1)
    from_rows(brick[...], brick_out)
    end_sends(2)
    end_heat_halo(1, second)


def hand_out_kernel(flow, second_heat, brick, flow_out, heat_out, brick_out, heat, sems):
    lane = iota((8, 128), 1)
    copies = [
        pltpu.make_async_copy(flow, flow_out, sems.at[0]),
        pltpu.make_async_copy(brick, brick_out, sems.at[1]),
    ]
    for copy in copies:
        copy.start()
    store = Lattice(None, second_heat)

    @pl.loop(0, TILES // 4)
    def _(n):
        for u in range(4):
            t = n * 4 + u
            for xb in range(4):
                for j in range(7):
                    rows, lanes = natural(t, xb)
                    heat[j, rows, lanes] = pull(store, 19 + j, t, xb, lane)

    copies.append(pltpu.make_async_copy(heat, heat_out, sems.at[2]))
    copies[-1].start()
    for copy in copies:
        copy.wait()


def body(
    flow_pops,
    heat_pops,
    solid_flag,
    brick_temp,
    brick_ids,
    brick_links,
    face_cell,
    face_owner,
    face_spot,
):
    shape = jax.ShapeDtypeStruct
    dma = pltpu.SemaphoreType.DMA
    near = pl.BlockSpec(memory_space=pltpu.VMEM)
    far = pl.BlockSpec(memory_space=pltpu.HBM)
    grid = (TILES * ROWS, 128)
    inputs = (
        flow_pops,
        heat_pops,
        solid_flag,
        face_owner.reshape(1024, 128),
        face_spot.reshape(1024, 128),
        face_cell.reshape(1024, 128),
        brick_temp,
        brick_ids.reshape(2, 128),
        brick_links.T,
    )
    results = pl.pallas_call(
        steps_kernel,
        out_shape=[
            pltpu.VMEM(flow_pops.shape, F32),
            pltpu.VMEM((7, TALL, 128), F32),
            pltpu.VMEM(brick_temp.shape, F32),
        ],
        in_specs=[far] * 9,
        out_specs=[near] * 3,
        scratch_shapes=[
            pltpu.VMEM((26, TALL, 128), F32),
            pltpu.VMEM((19, TALL, 128), F32),
            pltpu.VMEM(flow_pops.shape, F32),
            pltpu.VMEM(heat_pops.shape, F32),
            pltpu.VMEM(solid_flag.shape, I32),
            pltpu.VMEM((1024, 128), I32),
            pltpu.VMEM((1024, 128), I32),
            pltpu.VMEM((8, 128), I32),
            pltpu.VMEM((2, 512), F32),
            pltpu.VMEM((2, 128), I32),
            pltpu.VMEM((6, 256), I32),
            pltpu.VMEM((8, 128, 128), F32),
            pltpu.VMEM((8, 128, 128), F32),
            pltpu.VMEM((128, 128), F32),
            pltpu.VMEM((128, 128), F32),
            pltpu.VMEM((128, 256), F32),
            pltpu.VMEM((256, 128), F32),
            pltpu.VMEM((192, 128), BF16),
            pltpu.VMEM((TILES * ROWS, SLOTS), BF16),
            pltpu.VMEM((16, SLOTS), BF16),
            pltpu.VMEM((CAP, 128), I32),
            pltpu.VMEM((CAP, 128), I32),
            pltpu.VMEM((128, 128), I32),
            pltpu.VMEM((CAP, 128), I32),
            pltpu.VMEM((CAP, 128), I32),
            pltpu.VMEM((128, 128), I32),
            pltpu.VMEM(grid, F32),
            pltpu.VMEM(grid, F32),
            pltpu.VMEM((SLOTS, 256), BF16),
            pltpu.VMEM((CAP, 128), F32),
            pltpu.VMEM((CAP, 128), F32),
            pltpu.VMEM((3, 128, 128), F32),
            pltpu.VMEM((8, 128), F32),
            pltpu.VMEM((16, 128), F32),
            pltpu.VMEM((3, 8 * 24, 128), F32),
            pltpu.VMEM((3, 8 * 24, 128), F32),
            pltpu.VMEM((3, 16 * 16, 128), F32),
            pltpu.VMEM((3, 16 * 16, 128), F32),
            pltpu.VMEM((2, 2, 80, 128), F32),
            pltpu.VMEM((2, 2, 80, 128), F32),
            pltpu.VMEM((2, 2, 64, 128), F32),
            pltpu.VMEM((2, 2, 64, 128), F32),
            pltpu.VMEM((2, 4, 8, 128), F32),
            pltpu.VMEM((2, 4, 8, 128), F32),
            pltpu.VMEM((2, 2, 16, 128), F32),
            pltpu.VMEM((2, 2, 16, 128), F32),
            pltpu.VMEM((2, 2, 32, 128), F32),
            pltpu.VMEM((2, 2, 32, 128), F32),
            dma((9,)),
            dma((3, 8)),
            dma((3, 8)),
            dma((3, 16)),
            dma((3, 16)),
            dma((2, 8)),
            dma((2, 8)),
            dma((2, 4)),
            dma((2, 4)),
        ],
        compiler_params=pltpu.CompilerParams(
            collective_id=0, has_side_effects=True, vmem_limit_bytes=46 << 20
        ),
    )(*(pltpu.with_memory_space_constraint(value, pltpu.HBM) for value in inputs))
    flow, heat, brick = pl.pallas_call(
        hand_out_kernel,
        out_shape=[
            shape(flow_pops.shape, F32),
            shape(heat_pops.shape, F32),
            shape(brick_temp.shape, F32),
        ],
        in_specs=[near] * 3,
        out_specs=[far] * 3,
        scratch_shapes=[pltpu.VMEM(heat_pops.shape, F32), dma((3,))],
        compiler_params=pltpu.CompilerParams(vmem_limit_bytes=8 << 20),
    )(*results)
    return flow, heat, brick


def solution(mesh):
    return jax.shard_map(
        body,
        mesh=mesh,
        in_specs=(
            P(None, "gx", "gy"),
            P(None, "gx", "gy"),
            P("gx", "gy"),
            P(("gx", "gy"), None),
            P(),
            P(),
            P(),
            P(),
            P(),
        ),
        out_specs=(P(None, "gx", "gy"), P(None, "gx", "gy"), P(("gx", "gy"), None)),
        check_vma=False,
    )
```

```python
import functools

import jax
import jax.numpy as jnp
from jax import lax
from jax.experimental import pallas as pl
from jax.experimental.pallas import tpu as pltpu
from jax.sharding import PartitionSpec as P

MESH = pl.DeviceIdType.MESH
F32, BF16, I32 = jnp.float32, jnp.bfloat16, jnp.int32

VELOCITY = [
    (0, 0, 0),
    (1, 0, 0),
    (-1, 0, 0),
    (0, 1, 0),
    (0, -1, 0),
    (0, 0, 1),
    (0, 0, -1),
    (1, 1, 0),
    (-1, -1, 0),
    (1, -1, 0),
    (-1, 1, 0),
    (1, 0, 1),
    (-1, 0, -1),
    (1, 0, -1),
    (-1, 0, 1),
    (0, 1, 1),
    (0, -1, -1),
    (0, 1, -1),
    (0, -1, 1),
]
SIDE_SWAP = [1, 0, 3, 2, 5, 4]
WEIGHTS_HEAT = [0.25] + [0.125] * 6
TAU_FLOW, TAU_HEAT = 0.8, 0.9
BUOYANCY = 0.002
WALL_COEF = 0.1
BRICK_LOSS = 0.5
COND_BASE, COND_SLOPE = 0.04, 0.1
LATENT, MELT, MELT_WIDTH = 2.0, 4.0, 0.5

GX, GY = 16, 8
DEV = GX * GY
CAP = 16
ROWS, TILES, NZ = 32, 16, 32
PITCH = 48
TALL = (TILES + 2) * PITCH
SLOTS = CAP * DEV

ALL_VELOCITY = VELOCITY + VELOCITY[:7]
SIDES = [([9, 1, 11, 13, 7], 20), ([10, 2, 12, 14, 8], 21)]
SIDES += [([7, 3, 15, 17, 10], 22), ([8, 4, 16, 18, 9], 23)]
CORNERS = [(7, 1, 1), (8, -1, -1), (9, 1, -1), (10, -1, 1)]


def iota(shape, dim):
    return lax.broadcasted_iota(I32, shape, dim)


def lane_pick(rows, index):
    return jnp.take_along_axis(rows, index, axis=1, mode="promise_in_bounds")


def compact(get, key, val, packed):
    square = (128, 128)
    wide_row, wide_lane = iota((128, 256), 0), iota((128, 256), 1)
    prefix = jnp.where(wide_row <= wide_lane, 1.0, 0.0).astype(BF16)
    before = jnp.zeros(square, F32)
    for b in range(8):
        mask, value = get(b)
        counts = jnp.dot(
            jnp.where(mask, 1.0, 0.0).astype(BF16), prefix, preferred_element_type=F32
        )
        key[b] = jnp.where(mask, counts[:, :128] + before, 0.0)
        val[b] = value
        before = before + counts[:, 128:]

    @pl.loop(0, 4)
    def _(c):
        for u in range(4):
            rows = pl.ds(pl.multiple_of(c * 32 + u * 8, 8), 8)
            keys = [key[b, rows, :] for b in range(8)]
            vals = [val[b, rows, :] for b in range(8)]
            at = iota((8, 128), 1)
            out = jnp.zeros((8, 128), F32)
            for r in range(CAP):
                hit = jnp.zeros((8, 128), F32)
                for b in range(8):
                    hit = jnp.where(keys[b] == float(r + 1), vals[b], hit)
                out = jnp.where(at == r, jnp.sum(hit, axis=1, keepdims=True), out)
            packed[rows, :] = out

    return packed[...]


def split_cell(c):
    c = c.astype(I32) - 1
    live = c >= 0
    a = ((c >> 7) & 15) * ROWS + (c >> 11)
    return jnp.where(live, a, -1), c & 127, live


def split_spot(c):
    c = c.astype(I32) - 1
    live = c >= 0
    return jnp.where(live, c >> 6, -1), c & 63, live


def fill_onehots(row, onehot):
    count = onehot.shape[0]
    for r in range(CAP):
        for q in range(0, count, 128):
            size = min(128, count)
            part = iota((size, 128), 0) + q == row[r : r + 1, :]
            onehot[q : q + size, r * 128 : (r + 1) * 128] = jnp.where(part, 1.0, 0.0).astype(BF16)


def fill_edges(row, onehot):
    n = iota((96, 128), 0)
    last = n - 32 + (TILES - 1) * ROWS
    sides = jnp.where(n < 80, (n - 64) * ROWS, (n - 80) * ROWS + ROWS - 1)
    wanted = jnp.where(n < 32, n, jnp.where(n < 64, last, sides))
    for r in range(CAP):
        part = wanted == row[r : r + 1, :]
        onehot[:, r * 128 : (r + 1) * 128] = jnp.where(part, 1.0, 0.0).astype(BF16)


def ranked(device):
    return (((device >> 2) & 1) << 6) | ((device >> 4) << 3) | (((device >> 3) & 1) << 2) | (device & 3)


def fill_pick(spot, ids, links, wide, by_slot, pick):
    core, xc, ylo, q, inner, outer = spot
    order = jnp.concatenate([ids[0:1, :], ids[1:2, :]], axis=1)
    chosen = jnp.where(iota((256, 256), 0) == order, 1.0, 0.0).astype(BF16)
    wide[...] = jnp.zeros((128, 256), F32)
    wide[0:6, :] = jnp.dot(
        links.astype(F32).astype(BF16), chosen, preferred_element_type=F32
    )
    by_slot[0:128, :] = jnp.transpose(wide[:, 0:128])
    by_slot[128:256, :] = jnp.transpose(wide[:, 128:256])
    at, to = iota((16, 128), 1), iota((16, 128), 0)
    half = jnp.where(q >= 4, ids[1:2, :], ids[0:1, :])
    from_b, from_inner, side = at >> 6, (at >> 3) & 7, at & 7
    column = lax.rem(q, 4) * 32 + (from_inner >> 2) * 16 + ylo * 8 + (from_inner & 3) * 2 + from_b
    here = lane_pick(jnp.broadcast_to(half.astype(F32), (16, 128)), column)
    for b in range(2):
        named = jnp.concatenate(
            [
                by_slot[pl.ds((core * 8 + low * 4 + xc) * 2 + b, 8, stride=32), :]
                for low in range(2)
            ],
            axis=0,
        )
        for s in range(6):
            j = s * 2 + b
            n = named[:, s : s + 1]
            remote = (n == here) & (side == SIDE_SWAP[s])
            own = (n < 0.0) & (to == outer) & (at == b * 64 + inner * 8 + s)
            pick[j * 16 : (j + 1) * 16, :] = jnp.where(remote | own, 1.0, 0.0).astype(BF16)


def to_rows(brick):
    at = iota((1, 128), 1)
    rows = []
    for b in range(2):
        for x in range(8):
            part = brick[b : b + 1, (x // 2) * 128 : (x // 2 + 1) * 128]
            part = pltpu.roll(part, 64, 1) if x % 2 else part
            rows.append(jnp.where(at < 64, part, 0.0))
    return jnp.concatenate(rows, axis=0)


def from_rows(rows, out):
    turned = pltpu.roll(rows, 64, 1)
    at = iota((1, 128), 1)
    for b in range(2):
        for q in range(4):
            r = b * 8 + q * 2
            out[b : b + 1, q * 128 : (q + 1) * 128] = jnp.where(
                at < 64, rows[r : r + 1, :], turned[r + 1 : r + 2, :]
            )


def collide(f, g, solid):
    pairs = [(1, 2), (3, 4), (5, 6), (7, 8), (9, 10), (11, 12), (13, 14), (15, 16), (17, 18)]
    total = {a: f[a] + f[b] for a, b in pairs}
    diff = {a: f[a] - f[b] for a, b in pairs}
    density = f[0] + (
        (total[1] + total[3])
        + (total[5] + total[7])
        + (total[9] + total[11])
        + (total[13] + total[15])
        + total[17]
    )
    inverse = 1.0 / density
    ux = (diff[1] + diff[7] + diff[9] + diff[11] + diff[13]) * inverse
    uy = (diff[3] + diff[7] - diff[9] + diff[15] + diff[17]) * inverse
    uz = (diff[5] + diff[11] - diff[13] + diff[15] - diff[17]) * inverse
    temp = g[0] + ((g[1] + g[2]) + (g[3] + g[4]) + (g[5] + g[6]))
    sz = uz + (TAU_FLOW * BUOYANCY) * (temp - 1.0) * inverse
    base = 1.0 - 1.5 * (ux * ux + uy * uy + sz * sz)
    keep = 1.0 - 1.0 / TAU_FLOW
    along_of = {1: ux, 3: uy, 5: sz, 7: ux + uy, 9: ux - uy}
    along_of.update({11: ux + sz, 13: ux - sz, 15: uy + sz, 17: uy - sz})
    out_f = [None] * 19
    k0 = density * (1.0 / 3.0 / TAU_FLOW)
    out_f[0] = jnp.where(solid, f[0], keep * f[0] + k0 * base)
    scale = {1: density * (1.0 / 18.0 / TAU_FLOW), 7: density * (1.0 / 36.0 / TAU_FLOW)}
    for a, b in pairs:
        k = scale[1 if a < 7 else 7]
        along = along_of[a]
        even = k * (base + 4.5 * (along * along))
        odd = (3.0 * k) * along
        out_f[a] = jnp.where(solid, f[b], (even + odd) + keep * f[a])
        out_f[b] = jnp.where(solid, f[a], (even - odd) + keep * f[b])
    keep = 1.0 - 1.0 / TAU_HEAT
    out_g = [None] * 7
    out_g[0] = jnp.where(solid, g[0], keep * g[0] + (0.25 / TAU_HEAT) * temp)
    k = (0.125 / TAU_HEAT) * temp
    for a, u in ((1, ux), (3, uy), (5, uz)):
        odd = (4.0 * k) * u
        out_g[a] = jnp.where(solid, g[a + 1], (k + odd) + keep * g[a])
        out_g[a + 1] = jnp.where(solid, g[a], (k - odd) + keep * g[a + 1])
    return out_f, out_g


class Lattice:
    def __init__(self, flow, heat):
        self.flow, self.heat = flow, heat

    def at(self, key):
        pop = key[0]
        if pop < 19:
            return self.flow, key
        return self.heat, (pop - 19,) + tuple(key[1:])

    def __getitem__(self, key):
        ref, key = self.at(key)
        return ref[key]

    def __setitem__(self, key, value):
        ref, key = self.at(key)
        ref[key] = value


def pull(store, pop, t, xb, lane):
    cx, cy, cz = ALL_VELOCITY[pop]
    at = pop

    def tile(step):
        return store[at, pl.ds((t + 1 + step) * PITCH + 8 + xb * 8 - cx, 8), :]

    here = tile(0)
    if cy == 1:
        here = jnp.where(lane >= 128 - NZ, tile(-1), here)
    if cy == -1:
        here = jnp.where(lane < NZ, tile(1), here)
    shift = (cy * NZ + cz) % 128
    if shift:
        here = pltpu.roll(here, shift, 1)
    if cz == 1:
        here = jnp.where(lane & (NZ - 1) == 0, 0.0, here)
    if cz == -1:
        here = jnp.where(lane & (NZ - 1) == NZ - 1, 0.0, here)
    return here


def own_rows(t, xb):
    return pl.ds((t + 1) * PITCH + 8 + xb * 8, 8)


def natural(t, xb):
    return pl.ds(xb * 8, 8), pl.ds(pl.multiple_of(t * 128, 128), 128)


def temp_rows(t, xb):
    return pl.ds(pl.multiple_of(t * ROWS + xb * 8, 8), 8)


def halves(value):
    high = value.astype(BF16)
    return high, (value - high.astype(F32)).astype(BF16)


def fill_spread(columns, flux, spread):
    high, low = halves(flux)
    high, low = high.astype(F32), low.astype(F32)
    at = iota((128, 128), 1)
    for r in range(CAP):
        hit = at == columns[:, r : r + 1]
        rows = slice(r * 128, (r + 1) * 128)
        spread[rows, 0:128] = jnp.where(hit, high[:, r : r + 1], 0.0).astype(BF16)
        spread[rows, 128:256] = jnp.where(hit, low[:, r : r + 1], 0.0).astype(BF16)


def gather_spread(onehot, spread):
    both = jnp.dot(onehot[...], spread[...], preferred_element_type=F32)
    return both[:, :128] + both[:, 128:]


def brick_lookup(brick, brow, blrow):
    out = jnp.zeros((CAP, 128), F32)
    for a in range(16):
        row = jnp.broadcast_to(brick[a : a + 1, :], (CAP, 128))
        out = jnp.where(brow == a, lane_pick(row, blrow), out)
    return out


def store_faces(brick, faces):
    at, row = iota((16, 128), 1), iota((16, 128), 0)
    line = iota((1, 128), 1)
    mine = ((at >> 3) & 7) == (row & 7)
    wanted = {
        2: at & 7,
        3: 56 + (at & 7),
        4: (at & 7) * 8,
        5: (at & 7) * 8 + 7,
    }
    faces[6:8, :] = jnp.zeros((2, 128), F32)
    for s in range(6):
        if s < 2:
            low, high = brick[7 * s : 7 * s + 1, :], brick[8 + 7 * s : 9 + 7 * s, :]
        else:
            got = jnp.where(mine, lane_pick(brick, wanted[s]), 0.0)
            low = jnp.sum(got[0:8], axis=0, keepdims=True)
            high = jnp.sum(got[8:16], axis=0, keepdims=True)
        faces[s : s + 1, :] = jnp.where(line < 64, low, pltpu.roll(high, 64, 1))


def conduct(brick, ghost, loss):
    at, row = iota((16, 128), 1), iota((16, 128), 0)
    x = row & 7

    other_brick = pltpu.roll(ghost, 64, 1)

    def ghost_rows(s):
        return jnp.where(row < 8, ghost[s : s + 1, :], other_brick[s : s + 1, :])

    over_z = x * 8 + (at & 7)
    over_y = x * 8 + ((at >> 3) & 7)
    beside = [
        jnp.where(x == 0, ghost_rows(0), pltpu.roll(brick, 1, 0)),
        jnp.where(x == 7, ghost_rows(1), pltpu.roll(brick, 15, 0)),
        jnp.where(at < 8, lane_pick(ghost_rows(2), over_z), pltpu.roll(brick, 8, 1)),
        jnp.where(at >= 56, lane_pick(ghost_rows(3), over_z), pltpu.roll(brick, 120, 1)),
        jnp.where((at & 7) == 0, lane_pick(ghost_rows(4), over_y), pltpu.roll(brick, 1, 1)),
        jnp.where((at & 7) == 7, lane_pick(ghost_rows(5), over_y), pltpu.roll(brick, 127, 1)),
    ]
    here = COND_BASE * (1.0 + COND_SLOPE * brick)
    spread = jnp.zeros((16, 128), F32)
    for other in beside:
        spread += 0.5 * (here + COND_BASE * (1.0 + COND_SLOPE * other)) * (other - brick)
    phase = 1.0 / (1.0 + jnp.exp(-(brick - MELT) / MELT_WIDTH))
    capacity = 1.0 + LATENT * phase * (1.0 - phase) / MELT_WIDTH
    return jnp.where(at < 64, brick + (spread - BRICK_LOSS * loss) / capacity, 0.0)


def steps_kernel(
    flow_in,
    heat_in,
    solid_in,
    owners_in,
    spots_in,
    cells_in,
    brick_in,
    ids_in,
    links_in,
    flow_out,
    second_heat,
    brick,
    lost,
    layers,
    blcol,
    oh_brick,
    first,
    second_flow,
    flow,
    heat,
    solid,
    owners,
    spots,
    cells,
    brick_flat,
    ids,
    links,
    key,
    val,
    packed,
    reordered,
    wide,
    by_slot,
    pick,
    oh_cell,
    oh_edge,
    arow,
    lrow,
    lcol,
    brow,
    blrow,
    temps,
    gain,
    edge,
    spread,
    found,
    msg,
    faces,
    s1,
    r1,
    s2,
    r2,
    xf,
    xfr,
    yf,
    yfr,
    cf,
    cfr,
    xh,
    xhr,
    yh,
    yhr,
    load_sem,
    s1_send,
    s1_recv,
    s2_send,
    s2_recv,
    flow_send,
    flow_recv,
    heat_send,
    heat_recv,
):
    x, y = lax.axis_index("gx"), lax.axis_index("gy")
    me = x * GY + y
    core, q = lax.rem(x, 2), x // 2
    xc, ylo = lax.rem(y, 4), y // 4
    inner, outer = core * 4 + xc, ylo * 8 + q

    def inner_peer(i):
        return (q * 2 + i // 4, ylo * 4 + lax.rem(i, 4))

    def outer_peer(h):
        return (lax.rem(h, 8) * 2 + core, (h // 8) * 4 + xc)

    def inner_next(k):
        return lax.rem(inner + k, 8)

    def outer_next(k):
        return lax.rem(outer + k, 16)

    def xn(k):
        return lax.rem(x + (k + GX), GX)

    def yn(k):
        return lax.rem(y + (k + GY), GY)

    barrier = pltpu.get_barrier_semaphore()
    peers = [(xn(a), yn(b)) for a in (-1, 1) for b in (-1, 1)]
    peers += [outer_peer(outer_next(k)) for k in (10, 6, 2, 14, 9, 11, 5, 7, 1, 3, 13, 15, 8, 4, 12)]
    peers += [(xn(a), yn(b)) for a, b in ((-1, 0), (1, 0), (0, -1), (0, 1))]
    peers += [inner_peer(inner_next(k)) for k in range(1, 8)]
    for peer in peers:
        pl.semaphore_signal(barrier, inc=1, device_id=peer, device_id_type=MESH)

    second = Lattice(second_flow, second_heat)
    own_faces = pl.ds(pl.multiple_of(me * 8, 8), 8)
    loads = {}
    for n, (name, source, target) in enumerate(
        (
            ("owners", owners_in, owners),
            ("cells", cells_in.at[own_faces, :], cells),
            ("heat", heat_in, heat),
            ("spots", spots_in, spots),
            ("brick", brick_in, brick_flat),
            ("ids", ids_in, ids),
            ("links", links_in, links),
            ("solid", solid_in, solid),
            ("flow", flow_in, flow),
        )
    ):
        loads[name] = pltpu.make_async_copy(source, target, load_sem.at[n])
        if name not in ("solid", "flow"):
            loads[name].start()

    lane = iota((8, 128), 1)


    def look_up_row(row, outs, u, a, low):
        line = jnp.broadcast_to(temps[pl.ds(row, 1), :], (CAP, 128))
        outs[u % 4] = jnp.where(a == row, lane_pick(line, low), outs[u % 4])

    def look_up(inner_only):
        parts = []
        for n in range(4):
            part = temps[n * 128 : (n + 1) * 128, :]
            if inner_only:
                row = iota((128, 128), 0)
                away = (row & 31 != 0) & (row & 31 != 31)
                if n == 0:
                    away = away & (row >= 32)
                if n == 3:
                    away = away & (row < 96)
                part = jnp.where(away, part, 0.0)
            parts.append(jnp.transpose(part))
        high, low = halves(jnp.concatenate(parts, axis=1))
        both = jnp.concatenate([high, low], axis=0)
        lanes = lrow[...]
        at = iota((128, 128), 0)
        for r in range(0, CAP, 2):
            got = jnp.dot(
                both, oh_cell[:, r * 128 : (r + 2) * 128], preferred_element_type=F32
            )
            got = got[:128] + got[128:]
            for u in range(2):
                hit = jnp.where(
                    at == lanes[r + u : r + u + 1, :], got[:, u * 128 : (u + 1) * 128], 0.0
                )
                found[r + u : r + u + 1, :] = jnp.sum(hit, axis=0, keepdims=True)

    def look_up_edges():
        a, low = arow[...], lrow[...]
        outs = [jnp.zeros((CAP, 128), F32)] * 4
        rows = [t * ROWS + row for t in range(1, TILES - 1) for row in (0, ROWS - 1)]
        rows += [t * ROWS + row for t in (0, TILES - 1) for row in range(ROWS)]
        for u, row in enumerate(rows):
            look_up_row(row, outs, u, a, low)
        return (outs[0] + outs[1]) + (outs[2] + outs[3])

    def fill_message(n, value):
        rest = jnp.zeros((128 - CAP, 128), F32)
        msg[n] = jnp.transpose(jnp.concatenate([value, rest], axis=0))

    def ask_bricks(n):
        fill_message(n, brick_lookup(brick[...], brow[...], blrow[...]))


    def one(n, k, to, slot):
        count = 16 if n % 2 else 24
        return pltpu.make_async_remote_copy(
            src_ref=s1.at[n, pl.ds(pl.multiple_of(to * 24, 8), count), :],
            dst_ref=r1.at[n, pl.ds(pl.multiple_of(slot * 24, 8), count), :],
            send_sem=s1_send.at[n, k],
            recv_sem=s1_recv.at[n, slot],
            device_id=inner_peer(to),
            device_id_type=MESH,
        )

    def two(n, k, to, slot):
        count = 8 if n % 2 else 16
        return pltpu.make_async_remote_copy(
            src_ref=s2.at[n, pl.ds(pl.multiple_of(to * 16, 8), count), :],
            dst_ref=r2.at[n, pl.ds(pl.multiple_of(slot * 16, 8), count), :],
            send_sem=s2_send.at[n, k],
            recv_sem=s2_recv.at[n, slot],
            device_id=outer_peer(to),
            device_id_type=MESH,
        )

    def start_one(n):
        for k in range(8):
            s1[n, k * 24 : k * 24 + 16, :] = msg[n, pl.ds(k, 16, stride=8), :]
            if n % 2 == 0:
                s1[n, k * 24 + 16 : k * 24 + 24, :] = faces[...]
        for k in range(1, 8):
            one(n, k, inner_next(k), inner).start()
        own = pl.ds(pl.multiple_of(inner * 24, 8), 24)
        r1[n, own, :] = s1[n, own, :]

    def end_one(n):
        for k in range(1, 8):
            one(n, k, inner_next(k), inner_next(k)).wait_recv()

    def start_two(n):
        if n % 2 == 0:
            every = jnp.concatenate(
                [r1[n, k * 24 + 16 : k * 24 + 24, :] for k in range(8)], axis=0
            )
            every = jnp.concatenate([every, pltpu.roll(every, 64, 1)], axis=0)
            high = every.astype(BF16)
            low = every - high.astype(F32)
            at = iota((128, 128), 1)
            both = jnp.where(at < 64, high.astype(F32), pltpu.roll(low, 64, 1)).astype(BF16)
            picked = jnp.dot(pick[...], both, preferred_element_type=F32)
            picked = picked + pltpu.roll(picked, 64, 1)
            at = iota((16, 128), 1)
            for s in range(8):
                pair = jnp.zeros((16, 128), F32)
                if s < 6:
                    top = s * 32
                    pair = jnp.where(at < 64, picked[top : top + 16], picked[top + 16 : top + 32])
                s2[n, pl.ds(8 + s, 16, stride=16), :] = pair
        for h in range(16):
            s2[n, h * 16 : h * 16 + 8, :] = r1[n, pl.ds(h, 8, stride=24), :]
        for k in range(1, 16):
            two(n, k, outer_next(k), outer).start()
        own = pl.ds(pl.multiple_of(outer * 16, 8), 16)
        r2[n, own, :] = s2[n, own, :]

    def end_two(n):
        for k in range(1, 16):
            two(n, k, outer_next(k), outer_next(k)).wait_recv()

    def end_sends(n):
        for k in range(1, 8):
            one(n, k, inner_next(k), inner).wait_send()
        for k in range(1, 16):
            two(n, k, outer_next(k), outer).wait_send()

    def arrived(n):
        return jnp.concatenate([r2[n, h * 16 : h * 16 + 8, :] for h in range(16)], axis=0)

    def heat_sides(bricks, fluid):
        fill_spread(lcol[...], WALL_COEF * (arrived(bricks) - msg[fluid]), spread)
        edge[...] = gather_spread(oh_edge, spread)

    def heat_faces(store):
        gain[...] = gather_spread(oh_cell, spread)

        @pl.loop(0, TILES)
        def _(t):
            for xb in range(4):
                more = gain[temp_rows(t, xb), :]
                rows = own_rows(t, xb)
                for j in range(7):
                    store[19 + j, rows, :] = store[19 + j, rows, :] + WEIGHTS_HEAT[j] * more

    def ghosts(n):
        ghost = r2[n, 8:16, :]
        for h in range(1, 16):
            ghost = ghost + r2[n, h * 16 + 8 : h * 16 + 16, :]
        return ghost

    def cool_bricks(bricks, fluid, layers):
        fill_spread(blcol[...], WALL_COEF * (msg[bricks] - arrived(fluid)), spread)
        loss = gather_spread(oh_brick, spread)
        brick[...] = conduct(brick[...], ghosts(layers), loss)


    ways = [(1, 0), (-1, 0), (0, 1), (0, -1)]
    inside = {(1, 0): x > 0, (-1, 0): x < GX - 1, (0, 1): y > 0, (0, -1): y < GY - 1}
    leave_row, leave_tile = (39, 8), (TILES, 1)
    enter_row, enter_tile = (7, 40), (0, TILES + 1)
    edge_lane = (128 - NZ, 0)

    def plan_copies(step, plan, send, recv):
        return [
            pltpu.make_async_remote_copy(
                src_ref=source,
                dst_ref=target,
                send_sem=send.at[step, n],
                recv_sem=recv.at[step, n],
                device_id=peer,
                device_id_type=MESH,
            )
            for n, (source, target, peer) in enumerate(plan)
        ]

    def flow_copies(step):
        plan = []
        for n, (dx, dy) in enumerate(ways):
            source, target = (xf, xfr) if n < 2 else (yf, yfr)
            plan.append((source.at[step, n % 2], target.at[step, n % 2], (xn(dx), yn(dy))))
        for c, (_, dx, dy) in enumerate(CORNERS):
            plan.append((cf.at[step, c], cfr.at[step, c], (xn(dx), yn(dy))))
        return plan_copies(step, plan, flow_send, flow_recv)

    def heat_copies(step):
        plan = []
        for n, (dx, dy) in enumerate(ways):
            source, target = (xh, xhr) if n < 2 else (yh, yhr)
            plan.append((source.at[step, n % 2], target.at[step, n % 2], (xn(dx), yn(dy))))
        return plan_copies(step, plan, heat_send, heat_recv)

    def send_flow_halo(step, store):
        for n in range(2):
            for k, pop in enumerate(SIDES[n][0]):
                rows = pl.ds(PITCH + leave_row[n], 16, stride=PITCH)
                xf[step, n, k * 16 : (k + 1) * 16, :] = store[pop, rows, :]
        at = iota((32, 128), 1)
        for n in range(2):
            top = leave_tile[n] * PITCH + 8
            parts = []
            for k, pop in enumerate(SIDES[2 + n][0]):
                turn = ((k % 4) * NZ - edge_lane[n]) % 128
                part = store[pop, top : top + 32, :]
                parts.append(pltpu.roll(part, turn, 1) if turn else part)
            for k in range(1, 4):
                parts[0] = jnp.where(at >= k * NZ, parts[k], parts[0])
            yf[step, n, 0:32, :] = parts[0]
            yf[step, n, 32:64, :] = parts[4]
        for c, (pop, dx, dy) in enumerate(CORNERS):
            row = leave_tile[dy < 0] * PITCH + leave_row[dx < 0]
            cf[step, c] = jnp.broadcast_to(store[pop, row : row + 1, :], (8, 128))
        for copy in flow_copies(step):
            copy.start()

    def end_flow_halo(step, store):
        for copy in flow_copies(step):
            copy.wait()
        for n in range(2):
            for k, pop in enumerate(SIDES[n][0]):
                rows = pl.ds(PITCH + enter_row[n], 16, stride=PITCH)
                store[pop, rows, :] = jnp.where(
                    inside[ways[n]], xfr[step, n, k * 16 : (k + 1) * 16, :], 0.0
                )
        for n in range(2):
            top = enter_tile[n] * PITCH + 8
            for k, pop in enumerate(SIDES[2 + n][0]):
                part = yfr[step, n, (k // 4) * 32 : (k // 4 + 1) * 32, :]
                turn = (edge_lane[n] - (k % 4) * NZ) % 128
                part = pltpu.roll(part, turn, 1) if turn else part
                store[pop, top : top + 32, :] = jnp.where(inside[ways[2 + n]], part, 0.0)
        for c, (pop, dx, dy) in enumerate(CORNERS):
            row = enter_tile[dy < 0] * PITCH + enter_row[dx < 0]
            known = inside[(dx, 0)] & inside[(0, dy)]
            store[pop, row : row + 1, :] = jnp.where(known, cfr[step, c, 0:1, :], 0.0)

    def send_heat_halo(step, store):
        for n in range(2):
            rows = pl.ds(PITCH + leave_row[n], 16, stride=PITCH)
            more = WEIGHTS_HEAT[1] * edge[80 - 16 * n : 96 - 16 * n, :]
            xh[step, n] = store[SIDES[n][1], rows, :] + more
            top = leave_tile[n] * PITCH + 8
            more = WEIGHTS_HEAT[1] * edge[32 - 32 * n : 64 - 32 * n, :]
            yh[step, n] = store[SIDES[2 + n][1], top : top + 32, :] + more
        for copy in heat_copies(step):
            copy.start()

    def end_heat_halo(step, store):
        for copy in heat_copies(step):
            copy.wait()
        for n in range(2):
            rows = pl.ds(PITCH + enter_row[n], 16, stride=PITCH)
            store[SIDES[n][1], rows, :] = jnp.where(inside[ways[n]], xhr[step, n], 0.0)
            top = enter_tile[n] * PITCH + 8
            store[SIDES[2 + n][1], top : top + 32, :] = jnp.where(
                inside[ways[2 + n]], yhr[step, n], 0.0
            )


    def store_relaxed(store, t, xb, f, g):
        out_f, out_g = collide(f, g, solid[natural(t, xb)] == 1)
        rows = own_rows(t, xb)
        for i, value in enumerate(out_f + out_g):
            store[i, rows, :] = value

    def relax_first(low, high):
        @pl.loop(low, high)
        def _(t):
            for xb in range(4):
                rows, lanes = natural(t, xb)
                f = [flow[i, rows, lanes] for i in range(19)]
                g = [heat[j, rows, lanes] for j in range(7)]
                store_relaxed(first, t, xb, f, g)

    def relax_second(t, xb):
        f = [pull(first, i, t, xb, lane) for i in range(19)]
        g = [pull(first, 19 + j, t, xb, lane) for j in range(7)]
        store_relaxed(second, t, xb, f, g)

    def hand_flow(t, xb):
        rows, lanes = natural(t, xb)
        for i in range(19):
            flow_out[i, rows, lanes] = pull(second, i, t, xb, lane)

    def along_sides(act):
        @pl.loop(0, (TILES - 2) // 2)
        def _(n):
            for u in range(2):
                for xb in (0, 3):
                    act(1 + 2 * n + u, xb)

        @pl.loop(0, 2)
        def _(n):
            for xb in range(4):
                act(n * (TILES - 1), xb)

    def inside_sides(act):
        @pl.loop(0, (TILES - 2) // 2)
        def _(n):
            for u in range(2):
                for xb in (1, 2):
                    act(1 + 2 * n + u, xb)

    def sum_heat(g):
        return g[0] + ((g[1] + g[2]) + (g[3] + g[4]) + (g[5] + g[6]))

    def pulled_temp(t, xb):
        temps[temp_rows(t, xb), :] = sum_heat([pull(first, 19 + j, t, xb, lane) for j in range(7)])


    square = (128, 128)
    loads["owners"].wait()
    loads["cells"].wait()
    row_index = iota(square, 0)
    own_place = ranked(owners[own_faces, :])
    own_cell = cells[...].astype(F32) + 1.0
    table = compact(
        lambda b: (
            row_index == own_place[b : b + 1, :],
            jnp.broadcast_to(own_cell[b : b + 1, :], square),
        ),
        key,
        val,
        packed,
    )
    _, low, live = split_cell(table)
    lcol[...] = jnp.where(live, low, -1)
    a, low, live = split_cell(jnp.transpose(table)[:CAP, :])
    arow[...] = a
    lrow[...] = jnp.where(live, low, 0)


    loads["heat"].wait()
    loads["solid"].start()
    loads["flow"].start()

    @pl.loop(0, TILES // 2)
    def _(n):
        for u in range(2):
            for xb in range(4):
                rows, lanes = natural(n * 2 + u, xb)
                temps[temp_rows(n * 2 + u, xb), :] = sum_heat(
                    [heat[j, rows, lanes] for j in range(7)]
                )

    fill_onehots(arow[...], oh_cell)
    look_up(False)
    fill_message(0, found[...])
    loads["brick"].wait()
    brick[...] = to_rows(brick_flat[...])
    store_faces(brick[...], faces)
    pl.semaphore_wait(barrier, len(peers))
    start_one(0)

    loads["spots"].wait()

    def from_device(b):
        rows = pl.ds(b, 128, stride=8)
        return owners[rows, :] == me, spots[rows, :].astype(F32) + 1.0

    table = compact(from_device, key, val, packed)
    for n in range(32):
        source = ((n >> 1) & 7) * 16 + (n & 1) * 8 + (n >> 4) * 4
        reordered[n * 4 : n * 4 + 4, :] = packed[source : source + 4, :]
    table = reordered[...]
    _, low, live = split_spot(table)
    blcol[...] = jnp.where(live, low, -1)
    a, low, live = split_spot(jnp.transpose(table)[:CAP, :])
    brow[...] = a
    blrow[...] = jnp.where(live, low, 0)

    ask_bricks(1)
    start_one(1)
    loads["ids"].wait()
    loads["links"].wait()
    place = (core, xc, ylo, q, inner, outer)
    fill_pick(place, ids[...], links[...], wide, by_slot, pick)
    end_one(0)
    start_two(0)
    fill_onehots(brow[...], oh_brick)
    fill_edges(arow[...], oh_edge)
    loads["solid"].wait()
    loads["flow"].wait()
    relax_first(0, 2)
    end_one(1)
    start_two(1)
    relax_first(2, TILES)
    send_flow_halo(0, first)
    end_two(0)
    cool_bricks(1, 0, 0)
    store_faces(brick[...], faces)
    ask_bricks(2)
    start_one(2)
    end_two(1)
    heat_sides(1, 0)
    send_heat_halo(0, first)
    heat_faces(first)


    @pl.loop(0, (TILES - 2) // 2)
    def _(n):
        for u in range(2):
            for xb in range(4):
                pulled_temp(1 + 2 * n + u, xb)

    look_up(True)
    end_one(2)
    start_two(2)
    end_heat_halo(0, first)
    for t in range(TILES):
        for xb in range(4):
            if t in (0, TILES - 1) or xb in (0, 3):
                pulled_temp(t, xb)
    fill_message(3, found[...] + look_up_edges())
    start_one(3)
    end_flow_halo(0, first)
    along_sides(relax_second)
    send_flow_halo(1, second)
    end_one(3)
    start_two(3)
    inside_sides(relax_second)
    end_two(2)
    heat_sides(2, 3)
    send_heat_halo(1, second)
    heat_faces(second)
    inside_sides(hand_flow)
    for n in range(3):
        end_sends(n)
    end_flow_halo(1, second)
    along_sides(hand_flow)
    end_two(3)
    lost[...] = WALL_COEF * (msg[2] - arrived(3))
    layers[...] = ghosts(2)
    end_sends(3)
    end_heat_halo(1, second)


def hand_out_kernel(
    flow,
    second_heat,
    brick,
    lost,
    layers,
    blcol,
    oh_brick,
    flow_out,
    heat_out,
    brick_out,
    heat,
    flat,
    spread,
    sems,
):
    lane = iota((8, 128), 1)
    copies = [pltpu.make_async_copy(flow, flow_out, sems.at[0])]
    copies[-1].start()
    store = Lattice(None, second_heat)

    @pl.loop(0, TILES // 4)
    def _(n):
        for u in range(4):
            t = n * 4 + u
            for xb in range(4):
                for j in range(7):
                    rows, lanes = natural(t, xb)
                    heat[j, rows, lanes] = pull(store, 19 + j, t, xb, lane)

    copies.append(pltpu.make_async_copy(heat, heat_out, sems.at[1]))
    copies[-1].start()
    fill_spread(blcol[...], lost[...], spread)
    loss = gather_spread(oh_brick, spread)
    from_rows(conduct(brick[...], layers[...], loss), flat)
    copies.append(pltpu.make_async_copy(flat, brick_out, sems.at[2]))
    copies[-1].start()
    for copy in copies:
        copy.wait()


def body(
    flow_pops,
    heat_pops,
    solid_flag,
    brick_temp,
    brick_ids,
    brick_links,
    face_cell,
    face_owner,
    face_spot,
):
    shape = jax.ShapeDtypeStruct
    dma = pltpu.SemaphoreType.DMA
    near = pl.BlockSpec(memory_space=pltpu.VMEM)
    far = pl.BlockSpec(memory_space=pltpu.HBM)
    grid = (TILES * ROWS, 128)
    inputs = (
        flow_pops,
        heat_pops,
        solid_flag,
        face_owner.reshape(1024, 128),
        face_spot.reshape(1024, 128),
        face_cell.reshape(1024, 128),
        brick_temp,
        brick_ids.reshape(2, 128),
        brick_links.T,
    )
    results = pl.pallas_call(
        steps_kernel,
        out_shape=[
            pltpu.VMEM(flow_pops.shape, F32),
            pltpu.VMEM((7, TALL, 128), F32),
            pltpu.VMEM((16, 128), F32),
            pltpu.VMEM((128, 128), F32),
            pltpu.VMEM((8, 128), F32),
            pltpu.VMEM((128, 128), I32),
            pltpu.VMEM((16, SLOTS), BF16),
        ],
        in_specs=[far] * 9,
        out_specs=[near] * 7,
        scratch_shapes=[
            pltpu.VMEM((26, TALL, 128), F32),
            pltpu.VMEM((19, TALL, 128), F32),
            pltpu.VMEM(flow_pops.shape, F32),
            pltpu.VMEM(heat_pops.shape, F32),
            pltpu.VMEM(solid_flag.shape, I32),
            pltpu.VMEM((1024, 128), I32),
            pltpu.VMEM((1024, 128), I32),
            pltpu.VMEM((8, 128), I32),
            pltpu.VMEM((2, 512), F32),
            pltpu.VMEM((2, 128), I32),
            pltpu.VMEM((6, 256), I32),
            pltpu.VMEM((8, 128, 128), F32),
            pltpu.VMEM((8, 128, 128), F32),
            pltpu.VMEM((128, 128), F32),
            pltpu.VMEM((128, 128), F32),
            pltpu.VMEM((128, 256), F32),
            pltpu.VMEM((256, 128), F32),
            pltpu.VMEM((192, 128), BF16),
            pltpu.VMEM((TILES * ROWS, SLOTS), BF16),
            pltpu.VMEM((96, SLOTS), BF16),
            pltpu.VMEM((CAP, 128), I32),
            pltpu.VMEM((CAP, 128), I32),
            pltpu.VMEM((128, 128), I32),
            pltpu.VMEM((CAP, 128), I32),
            pltpu.VMEM((CAP, 128), I32),
            pltpu.VMEM(grid, F32),
            pltpu.VMEM(grid, F32),
            pltpu.VMEM((96, 128), F32),
            pltpu.VMEM((SLOTS, 256), BF16),
            pltpu.VMEM((CAP, 128), F32),
            pltpu.VMEM((4, 128, 128), F32),
            pltpu.VMEM((8, 128), F32),
            pltpu.VMEM((4, 8 * 24, 128), F32),
            pltpu.VMEM((4, 8 * 24, 128), F32),
            pltpu.VMEM((4, 16 * 16, 128), F32),
            pltpu.VMEM((4, 16 * 16, 128), F32),
            pltpu.VMEM((2, 2, 80, 128), F32),
            pltpu.VMEM((2, 2, 80, 128), F32),
            pltpu.VMEM((2, 2, 64, 128), F32),
            pltpu.VMEM((2, 2, 64, 128), F32),
            pltpu.VMEM((2, 4, 8, 128), F32),
            pltpu.VMEM((2, 4, 8, 128), F32),
            pltpu.VMEM((2, 2, 16, 128), F32),
            pltpu.VMEM((2, 2, 16, 128), F32),
            pltpu.VMEM((2, 2, 32, 128), F32),
            pltpu.VMEM((2, 2, 32, 128), F32),
            dma((9,)),
            dma((4, 8)),
            dma((4, 8)),
            dma((4, 16)),
            dma((4, 16)),
            dma((2, 8)),
            dma((2, 8)),
            dma((2, 4)),
            dma((2, 4)),
        ],
        compiler_params=pltpu.CompilerParams(
            collective_id=0, has_side_effects=True, vmem_limit_bytes=46 << 20
        ),
    )(*(pltpu.with_memory_space_constraint(value, pltpu.HBM) for value in inputs))
    flow, heat, brick = pl.pallas_call(
        hand_out_kernel,
        out_shape=[
            shape(flow_pops.shape, F32),
            shape(heat_pops.shape, F32),
            shape(brick_temp.shape, F32),
        ],
        in_specs=[near] * 7,
        out_specs=[far] * 3,
        scratch_shapes=[
            pltpu.VMEM(heat_pops.shape, F32),
            pltpu.VMEM(brick_temp.shape, F32),
            pltpu.VMEM((SLOTS, 256), BF16),
            dma((3,)),
        ],
        compiler_params=pltpu.CompilerParams(vmem_limit_bytes=8 << 20),
    )(*results)
    return flow, heat, brick


def solution(mesh):
    return jax.shard_map(
        body,
        mesh=mesh,
        in_specs=(
            P(None, "gx", "gy"),
            P(None, "gx", "gy"),
            P("gx", "gy"),
            P(("gx", "gy"), None),
            P(),
            P(),
            P(),
            P(),
            P(),
        ),
        out_specs=(P(None, "gx", "gy"), P(None, "gx", "gy"), P(("gx", "gy"), None)),
        check_vma=False,
    )
```

```python
import functools

import jax
import jax.numpy as jnp
from jax import lax
from jax.experimental import pallas as pl
from jax.experimental.pallas import tpu as pltpu
from jax.sharding import PartitionSpec as P

MESH = pl.DeviceIdType.MESH
F32, BF16, I32 = jnp.float32, jnp.bfloat16, jnp.int32

VELOCITY = [
    (0, 0, 0),
    (1, 0, 0),
    (-1, 0, 0),
    (0, 1, 0),
    (0, -1, 0),
    (0, 0, 1),
    (0, 0, -1),
    (1, 1, 0),
    (-1, -1, 0),
    (1, -1, 0),
    (-1, 1, 0),
    (1, 0, 1),
    (-1, 0, -1),
    (1, 0, -1),
    (-1, 0, 1),
    (0, 1, 1),
    (0, -1, -1),
    (0, 1, -1),
    (0, -1, 1),
]
SIDE_SWAP = [1, 0, 3, 2, 5, 4]
WEIGHTS_HEAT = [0.25] + [0.125] * 6
TAU_FLOW, TAU_HEAT = 0.8, 0.9
BUOYANCY = 0.002
WALL_COEF = 0.1
BRICK_LOSS = 0.5
COND_BASE, COND_SLOPE = 0.04, 0.1
LATENT, MELT, MELT_WIDTH = 2.0, 4.0, 0.5

GX, GY = 16, 8
DEV = GX * GY
CAP = 16
ROWS, TILES, NZ = 32, 16, 32
PITCH = 48
TALL = (TILES + 2) * PITCH
SLOTS = CAP * DEV

ALL_VELOCITY = VELOCITY + VELOCITY[:7]
SIDES = [([9, 1, 11, 13, 7], 20), ([10, 2, 12, 14, 8], 21)]
SIDES += [([7, 3, 15, 17, 10], 22), ([8, 4, 16, 18, 9], 23)]
CORNERS = [(7, 1, 1), (8, -1, -1), (9, 1, -1), (10, -1, 1)]


def iota(shape, dim):
    return lax.broadcasted_iota(I32, shape, dim)


def lane_pick(rows, index):
    return jnp.take_along_axis(rows, index, axis=1, mode="promise_in_bounds")


def compact(get, key, val, packed):
    square = (128, 128)
    wide_row, wide_lane = iota((128, 256), 0), iota((128, 256), 1)
    prefix = jnp.where(wide_row <= wide_lane, 1.0, 0.0).astype(BF16)
    before = jnp.zeros(square, F32)
    for b in range(8):
        mask, value = get(b)
        counts = jnp.dot(
            jnp.where(mask, 1.0, 0.0).astype(BF16), prefix, preferred_element_type=F32
        )
        key[b] = jnp.where(mask, counts[:, :128] + before, 0.0)
        val[b] = value
        before = before + counts[:, 128:]

    @pl.loop(0, 4)
    def _(c):
        for u in range(4):
            rows = pl.ds(pl.multiple_of(c * 32 + u * 8, 8), 8)
            keys = [key[b, rows, :] for b in range(8)]
            vals = [val[b, rows, :] for b in range(8)]
            at = iota((8, 128), 1)
            out = jnp.zeros((8, 128), F32)
            for r in range(CAP):
                hit = jnp.zeros((8, 128), F32)
                for b in range(8):
                    hit = jnp.where(keys[b] == float(r + 1), vals[b], hit)
                out = jnp.where(at == r, jnp.sum(hit, axis=1, keepdims=True), out)
            packed[rows, :] = out

    return packed[...]


def compact_own(place, cell):
    square = (128, 128)
    wide_row, wide_lane = iota((128, 256), 0), iota((128, 256), 1)
    prefix = jnp.where(wide_row <= wide_lane, 1.0, 0.0).astype(BF16)
    device, rank = iota(square, 0), iota((CAP, 128), 0).astype(F32) + 1.0
    before = jnp.zeros(square, F32)
    masks, values = [], []
    for b in range(8):
        mask = device == place[b : b + 1, :]
        masks.append(jnp.where(mask, 1.0, 0.0).astype(BF16))
        counts = jnp.dot(masks[-1], prefix, preferred_element_type=F32)
        own = jnp.where(mask, counts[:, :128] + before, 0.0)
        before = before + counts[:, 128:]
        match = rank == jnp.sum(own, axis=0, keepdims=True)
        high = (cell[b : b + 1, :] >> 8).astype(F32)
        low = (cell[b : b + 1, :] & 255).astype(F32)
        both = [jnp.where(match, high, 0.0), jnp.where(match, low, 0.0)]
        values.append(jnp.concatenate(both, axis=0).astype(BF16))
    out = lax.dot_general(
        jnp.concatenate(values, axis=1),
        jnp.concatenate(masks, axis=1),
        (((1,), (1,)), ((), ())),
        preferred_element_type=F32,
    )
    return out[:CAP] * 256.0 + out[CAP:]


def split_cell(c):
    c = c.astype(I32) - 1
    live = c >= 0
    a = ((c >> 7) & 15) * ROWS + (c >> 11)
    return jnp.where(live, a, -1), c & 127, live


def split_spot(c):
    c = c.astype(I32) - 1
    live = c >= 0
    return jnp.where(live, c >> 6, -1), c & 63, live


def fill_onehots(row, onehot):
    count = onehot.shape[0]
    for r in range(CAP):
        for q in range(0, count, 128):
            size = min(128, count)
            part = iota((size, 128), 0) + q == row[r : r + 1, :]
            onehot[q : q + size, r * 128 : (r + 1) * 128] = jnp.where(part, 1.0, 0.0).astype(BF16)


def fill_edges(row, onehot):
    n = iota((96, 128), 0)
    last = n - 32 + (TILES - 1) * ROWS
    sides = jnp.where(n < 80, (n - 64) * ROWS, (n - 80) * ROWS + ROWS - 1)
    wanted = jnp.where(n < 32, n, jnp.where(n < 64, last, sides))
    for r in range(CAP):
        part = wanted == row[r : r + 1, :]
        onehot[:, r * 128 : (r + 1) * 128] = jnp.where(part, 1.0, 0.0).astype(BF16)


def ranked(device):
    return (((device >> 2) & 1) << 6) | ((device >> 4) << 3) | (((device >> 3) & 1) << 2) | (device & 3)


def fill_pick(spot, ids, links, wide, by_slot, pick):
    core, xc, ylo, q, inner, outer = spot
    order = jnp.concatenate([ids[0:1, :], ids[1:2, :]], axis=1)
    chosen = jnp.where(iota((256, 256), 0) == order, 1.0, 0.0).astype(BF16)
    wide[...] = jnp.zeros((128, 256), F32)
    wide[0:6, :] = jnp.dot(
        links.astype(F32).astype(BF16), chosen, preferred_element_type=F32
    )
    by_slot[0:128, :] = jnp.transpose(wide[:, 0:128])
    by_slot[128:256, :] = jnp.transpose(wide[:, 128:256])
    at, to = iota((16, 128), 1), iota((16, 128), 0)
    half = jnp.where(q >= 4, ids[1:2, :], ids[0:1, :])
    from_b, from_inner, side = at >> 6, (at >> 3) & 7, at & 7
    column = lax.rem(q, 4) * 32 + (from_inner >> 2) * 16 + ylo * 8 + (from_inner & 3) * 2 + from_b
    here = lane_pick(jnp.broadcast_to(half.astype(F32), (16, 128)), column)
    for b in range(2):
        named = jnp.concatenate(
            [
                by_slot[pl.ds((core * 8 + low * 4 + xc) * 2 + b, 8, stride=32), :]
                for low in range(2)
            ],
            axis=0,
        )
        for s in range(6):
            j = s * 2 + b
            n = named[:, s : s + 1]
            remote = (n == here) & (side == SIDE_SWAP[s])
            own = (n < 0.0) & (to == outer) & (at == b * 64 + inner * 8 + s)
            pick[j * 16 : (j + 1) * 16, :] = jnp.where(remote | own, 1.0, 0.0).astype(BF16)


def to_rows(brick):
    at = iota((1, 128), 1)
    rows = []
    for b in range(2):
        for x in range(8):
            part = brick[b : b + 1, (x // 2) * 128 : (x // 2 + 1) * 128]
            part = pltpu.roll(part, 64, 1) if x % 2 else part
            rows.append(jnp.where(at < 64, part, 0.0))
    return jnp.concatenate(rows, axis=0)


def from_rows(rows, out):
    turned = pltpu.roll(rows, 64, 1)
    at = iota((1, 128), 1)
    for b in range(2):
        for q in range(4):
            r = b * 8 + q * 2
            out[b : b + 1, q * 128 : (q + 1) * 128] = jnp.where(
                at < 64, rows[r : r + 1, :], turned[r + 1 : r + 2, :]
            )


def collide(f, g, solid):
    pairs = [(1, 2), (3, 4), (5, 6), (7, 8), (9, 10), (11, 12), (13, 14), (15, 16), (17, 18)]
    total = {a: f[a] + f[b] for a, b in pairs}
    diff = {a: f[a] - f[b] for a, b in pairs}
    density = f[0] + (
        (total[1] + total[3])
        + (total[5] + total[7])
        + (total[9] + total[11])
        + (total[13] + total[15])
        + total[17]
    )
    inverse = 1.0 / density
    ux = (diff[1] + diff[7] + diff[9] + diff[11] + diff[13]) * inverse
    uy = (diff[3] + diff[7] - diff[9] + diff[15] + diff[17]) * inverse
    uz = (diff[5] + diff[11] - diff[13] + diff[15] - diff[17]) * inverse
    temp = g[0] + ((g[1] + g[2]) + (g[3] + g[4]) + (g[5] + g[6]))
    sz = uz + (TAU_FLOW * BUOYANCY) * (temp - 1.0) * inverse
    base = 1.0 - 1.5 * (ux * ux + uy * uy + sz * sz)
    keep = 1.0 - 1.0 / TAU_FLOW
    along_of = {1: ux, 3: uy, 5: sz, 7: ux + uy, 9: ux - uy}
    along_of.update({11: ux + sz, 13: ux - sz, 15: uy + sz, 17: uy - sz})
    out_f = [None] * 19
    k0 = density * (1.0 / 3.0 / TAU_FLOW)
    out_f[0] = jnp.where(solid, f[0], keep * f[0] + k0 * base)
    scale = {1: density * (1.0 / 18.0 / TAU_FLOW), 7: density * (1.0 / 36.0 / TAU_FLOW)}
    level = {a: k * base for a, k in scale.items()}
    bend = {a: 4.5 * k for a, k in scale.items()}
    lean = {a: 3.0 * k for a, k in scale.items()}
    for a, b in pairs:
        kind = 1 if a < 7 else 7
        along = along_of[a]
        even = level[kind] + bend[kind] * (along * along)
        odd = lean[kind] * along
        out_f[a] = jnp.where(solid, f[b], (even + odd) + keep * f[a])
        out_f[b] = jnp.where(solid, f[a], (even - odd) + keep * f[b])
    keep = 1.0 - 1.0 / TAU_HEAT
    out_g = [None] * 7
    out_g[0] = jnp.where(solid, g[0], keep * g[0] + (0.25 / TAU_HEAT) * temp)
    k = (0.125 / TAU_HEAT) * temp
    for a, u in ((1, ux), (3, uy), (5, uz)):
        odd = (4.0 * k) * u
        out_g[a] = jnp.where(solid, g[a + 1], (k + odd) + keep * g[a])
        out_g[a + 1] = jnp.where(solid, g[a], (k - odd) + keep * g[a + 1])
    return out_f, out_g


class Lattice:
    def __init__(self, flow, heat):
        self.flow, self.heat = flow, heat

    def at(self, key):
        pop = key[0]
        if pop < 19:
            return self.flow, key
        return self.heat, (pop - 19,) + tuple(key[1:])

    def __getitem__(self, key):
        ref, key = self.at(key)
        return ref[key]

    def __setitem__(self, key, value):
        ref, key = self.at(key)
        ref[key] = value


def pull(store, pop, t, xb, lane):
    cx, cy, cz = ALL_VELOCITY[pop]
    at = pop

    def tile(step):
        return store[at, pl.ds((t + 1 + step) * PITCH + 8 + xb * 8 - cx, 8), :]

    here = tile(0)
    if cy == 1:
        here = jnp.where(lane >= 128 - NZ, tile(-1), here)
    if cy == -1:
        here = jnp.where(lane < NZ, tile(1), here)
    shift = (cy * NZ + cz) % 128
    if shift:
        here = pltpu.roll(here, shift, 1)
    if cz == 1:
        here = jnp.where(lane & (NZ - 1) == 0, 0.0, here)
    if cz == -1:
        here = jnp.where(lane & (NZ - 1) == NZ - 1, 0.0, here)
    return here


def own_rows(t, xb):
    return pl.ds((t + 1) * PITCH + 8 + xb * 8, 8)


def natural(t, xb):
    return pl.ds(xb * 8, 8), pl.ds(pl.multiple_of(t * 128, 128), 128)


def temp_rows(t, xb):
    return pl.ds(pl.multiple_of(t * ROWS + xb * 8, 8), 8)


def halves(value):
    high = value.astype(BF16)
    return high, (value - high.astype(F32)).astype(BF16)


def fill_spread(columns, flux, spread):
    high, low = halves(flux)
    high, low = high.astype(F32), low.astype(F32)
    at = iota((128, 128), 1)
    for r in range(CAP):
        hit = at == columns[:, r : r + 1]
        rows = slice(r * 128, (r + 1) * 128)
        spread[rows, 0:128] = jnp.where(hit, high[:, r : r + 1], 0.0).astype(BF16)
        spread[rows, 128:256] = jnp.where(hit, low[:, r : r + 1], 0.0).astype(BF16)


def gather_spread(onehot, spread):
    both = jnp.dot(onehot[...], spread[...], preferred_element_type=F32)
    return both[:, :128] + both[:, 128:]


def brick_lookup(brick, brow, blrow):
    out = jnp.zeros((CAP, 128), F32)
    for a in range(16):
        row = jnp.broadcast_to(brick[a : a + 1, :], (CAP, 128))
        out = jnp.where(brow == a, lane_pick(row, blrow), out)
    return out


def store_faces(brick, faces):
    at, row = iota((16, 128), 1), iota((16, 128), 0)
    line = iota((1, 128), 1)
    mine = ((at >> 3) & 7) == (row & 7)
    wanted = {
        2: at & 7,
        3: 56 + (at & 7),
        4: (at & 7) * 8,
        5: (at & 7) * 8 + 7,
    }
    faces[6:8, :] = jnp.zeros((2, 128), F32)
    for s in range(6):
        if s < 2:
            low, high = brick[7 * s : 7 * s + 1, :], brick[8 + 7 * s : 9 + 7 * s, :]
        else:
            got = jnp.where(mine, lane_pick(brick, wanted[s]), 0.0)
            low = jnp.sum(got[0:8], axis=0, keepdims=True)
            high = jnp.sum(got[8:16], axis=0, keepdims=True)
        faces[s : s + 1, :] = jnp.where(line < 64, low, pltpu.roll(high, 64, 1))


def conduct(brick, ghost, loss):
    at, row = iota((16, 128), 1), iota((16, 128), 0)
    x = row & 7

    other_brick = pltpu.roll(ghost, 64, 1)

    def ghost_rows(s):
        return jnp.where(row < 8, ghost[s : s + 1, :], other_brick[s : s + 1, :])

    over_z = x * 8 + (at & 7)
    over_y = x * 8 + ((at >> 3) & 7)
    beside = [
        jnp.where(x == 0, ghost_rows(0), pltpu.roll(brick, 1, 0)),
        jnp.where(x == 7, ghost_rows(1), pltpu.roll(brick, 15, 0)),
        jnp.where(at < 8, lane_pick(ghost_rows(2), over_z), pltpu.roll(brick, 8, 1)),
        jnp.where(at >= 56, lane_pick(ghost_rows(3), over_z), pltpu.roll(brick, 120, 1)),
        jnp.where((at & 7) == 0, lane_pick(ghost_rows(4), over_y), pltpu.roll(brick, 1, 1)),
        jnp.where((at & 7) == 7, lane_pick(ghost_rows(5), over_y), pltpu.roll(brick, 127, 1)),
    ]
    here = COND_BASE * (1.0 + COND_SLOPE * brick)
    spread = jnp.zeros((16, 128), F32)
    for other in beside:
        spread += 0.5 * (here + COND_BASE * (1.0 + COND_SLOPE * other)) * (other - brick)
    phase = 1.0 / (1.0 + jnp.exp(-(brick - MELT) / MELT_WIDTH))
    capacity = 1.0 + LATENT * phase * (1.0 - phase) / MELT_WIDTH
    return jnp.where(at < 64, brick + (spread - BRICK_LOSS * loss) / capacity, 0.0)


def steps_kernel(
    flow_in,
    heat_in,
    solid_in,
    owners_in,
    spots_in,
    cells_in,
    brick_in,
    ids_in,
    links_in,
    flow_out,
    second_heat,
    brick,
    lost,
    layers,
    blcol,
    oh_brick,
    first,
    second_flow,
    flow,
    heat,
    solid,
    owners,
    spots,
    cells,
    brick_flat,
    ids,
    links,
    key,
    val,
    packed,
    reordered,
    wide,
    by_slot,
    pick,
    oh_cell,
    oh_edge,
    arow,
    lrow,
    lcol,
    brow,
    blrow,
    temps,
    gain,
    edge,
    spread,
    found,
    msg,
    faces,
    s1,
    r1,
    s2,
    r2,
    xf,
    xfr,
    yf,
    yfr,
    cf,
    cfr,
    xh,
    xhr,
    yh,
    yhr,
    load_sem,
    s1_send,
    s1_recv,
    s2_send,
    s2_recv,
    flow_send,
    flow_recv,
    heat_send,
    heat_recv,
):
    x, y = lax.axis_index("gx"), lax.axis_index("gy")
    me = x * GY + y
    core, q = lax.rem(x, 2), x // 2
    xc, ylo = lax.rem(y, 4), y // 4
    inner, outer = core * 4 + xc, ylo * 8 + q

    def inner_peer(i):
        return (q * 2 + i // 4, ylo * 4 + lax.rem(i, 4))

    def outer_peer(h):
        return (lax.rem(h, 8) * 2 + core, (h // 8) * 4 + xc)

    def inner_next(k):
        return lax.rem(inner + k, 8)

    def outer_next(k):
        return lax.rem(outer + k, 16)

    def xn(k):
        return lax.rem(x + (k + GX), GX)

    def yn(k):
        return lax.rem(y + (k + GY), GY)

    second = Lattice(second_flow, second_heat)
    own_faces = pl.ds(pl.multiple_of(me * 8, 8), 8)
    loads = {}
    for n, (name, source, target) in enumerate(
        (
            ("owners", owners_in, owners),
            ("cells", cells_in.at[own_faces, :], cells),
            ("heat", heat_in, heat),
            ("spots", spots_in, spots),
            ("brick", brick_in, brick_flat),
            ("ids", ids_in, ids),
            ("links", links_in, links),
            ("solid", solid_in, solid),
            ("flow", flow_in, flow),
        )
    ):
        loads[name] = pltpu.make_async_copy(source, target, load_sem.at[n])
        if name not in ("solid", "flow"):
            loads[name].start()

    barrier = pltpu.get_barrier_semaphore()
    peers = [(xn(a), yn(b)) for a in (-1, 1) for b in (-1, 1)]
    peers += [outer_peer(outer_next(k)) for k in (10, 6, 2, 14, 9, 11, 5, 7, 1, 3, 13, 15, 8, 4, 12)]
    peers += [(xn(a), yn(b)) for a, b in ((-1, 0), (1, 0), (0, -1), (0, 1))]
    peers += [inner_peer(inner_next(k)) for k in range(1, 8)]
    for peer in peers:
        pl.semaphore_signal(barrier, inc=1, device_id=peer, device_id_type=MESH)

    lane = iota((8, 128), 1)


    def look_up_row(row, outs, u, a, low):
        line = jnp.broadcast_to(temps[pl.ds(row, 1), :], (CAP, 128))
        outs[u % 4] = jnp.where(a == row, lane_pick(line, low), outs[u % 4])

    def look_up(inner_only):
        parts = []
        for n in range(4):
            part = temps[n * 128 : (n + 1) * 128, :]
            if inner_only:
                row = iota((128, 128), 0)
                away = (row & 31 != 0) & (row & 31 != 31)
                if n == 0:
                    away = away & (row >= 32)
                if n == 3:
                    away = away & (row < 96)
                part = jnp.where(away, part, 0.0)
            parts.append(jnp.transpose(part))
        high, low = halves(jnp.concatenate(parts, axis=1))
        both = jnp.concatenate([high, low], axis=0)
        lanes = lrow[...]
        at = iota((128, 128), 0)
        for r in range(0, CAP, 2):
            got = jnp.dot(
                both, oh_cell[:, r * 128 : (r + 2) * 128], preferred_element_type=F32
            )
            got = got[:128] + got[128:]
            for u in range(2):
                hit = jnp.where(
                    at == lanes[r + u : r + u + 1, :], got[:, u * 128 : (u + 1) * 128], 0.0
                )
                found[r + u : r + u + 1, :] = jnp.sum(hit, axis=0, keepdims=True)

    def look_up_edges():
        a, low = arow[...], lrow[...]
        outs = [jnp.zeros((CAP, 128), F32)] * 4
        rows = [t * ROWS + row for t in range(1, TILES - 1) for row in (0, ROWS - 1)]
        rows += [t * ROWS + row for t in (0, TILES - 1) for row in range(ROWS)]
        for u, row in enumerate(rows):
            look_up_row(row, outs, u, a, low)
        return (outs[0] + outs[1]) + (outs[2] + outs[3])

    def fill_message(n, value):
        rest = jnp.zeros((128 - CAP, 128), F32)
        msg[n] = jnp.transpose(jnp.concatenate([value, rest], axis=0))

    def ask_bricks(n):
        fill_message(n, brick_lookup(brick[...], brow[...], blrow[...]))


    def one(n, k, to, slot):
        count = 16 if n % 2 else 24
        return pltpu.make_async_remote_copy(
            src_ref=s1.at[n, pl.ds(pl.multiple_of(to * 24, 8), count), :],
            dst_ref=r1.at[n, pl.ds(pl.multiple_of(slot * 24, 8), count), :],
            send_sem=s1_send.at[n, k],
            recv_sem=s1_recv.at[n, slot],
            device_id=inner_peer(to),
            device_id_type=MESH,
        )

    def two(n, k, to, slot):
        count = 8 if n % 2 else 16
        return pltpu.make_async_remote_copy(
            src_ref=s2.at[n, pl.ds(pl.multiple_of(to * 16, 8), count), :],
            dst_ref=r2.at[n, pl.ds(pl.multiple_of(slot * 16, 8), count), :],
            send_sem=s2_send.at[n, k],
            recv_sem=s2_recv.at[n, slot],
            device_id=outer_peer(to),
            device_id_type=MESH,
        )

    def start_one(n):
        for k in range(8):
            s1[n, k * 24 : k * 24 + 16, :] = msg[n, pl.ds(k, 16, stride=8), :]
            if n % 2 == 0:
                s1[n, k * 24 + 16 : k * 24 + 24, :] = faces[...]
        for k in range(1, 8):
            one(n, k, inner_next(k), inner).start()
        own = pl.ds(pl.multiple_of(inner * 24, 8), 24)
        r1[n, own, :] = s1[n, own, :]

    def end_one(n):
        for k in range(1, 8):
            one(n, k, inner_next(k), inner_next(k)).wait_recv()

    def start_two(n):
        if n % 2 == 0:
            every = jnp.concatenate(
                [r1[n, k * 24 + 16 : k * 24 + 24, :] for k in range(8)], axis=0
            )
            every = jnp.concatenate([every, pltpu.roll(every, 64, 1)], axis=0)
            high = every.astype(BF16)
            low = every - high.astype(F32)
            at = iota((128, 128), 1)
            both = jnp.where(at < 64, high.astype(F32), pltpu.roll(low, 64, 1)).astype(BF16)
            picked = jnp.dot(pick[...], both, preferred_element_type=F32)
            picked = picked + pltpu.roll(picked, 64, 1)
            at = iota((16, 128), 1)
            for s in range(8):
                pair = jnp.zeros((16, 128), F32)
                if s < 6:
                    top = s * 32
                    pair = jnp.where(at < 64, picked[top : top + 16], picked[top + 16 : top + 32])
                s2[n, pl.ds(8 + s, 16, stride=16), :] = pair
        for h in range(16):
            s2[n, h * 16 : h * 16 + 8, :] = r1[n, pl.ds(h, 8, stride=24), :]
        for k in range(1, 16):
            two(n, k, outer_next(k), outer).start()
        own = pl.ds(pl.multiple_of(outer * 16, 8), 16)
        r2[n, own, :] = s2[n, own, :]

    def end_two(n):
        for k in range(1, 16):
            two(n, k, outer_next(k), outer_next(k)).wait_recv()

    def end_sends(n):
        for k in range(1, 8):
            one(n, k, inner_next(k), inner).wait_send()
        for k in range(1, 16):
            two(n, k, outer_next(k), outer).wait_send()

    def arrived(n):
        return jnp.concatenate([r2[n, h * 16 : h * 16 + 8, :] for h in range(16)], axis=0)

    def heat_sides(bricks, fluid):
        fill_spread(lcol[...], WALL_COEF * (arrived(bricks) - msg[fluid]), spread)
        edge[...] = gather_spread(oh_edge, spread)

    def heat_faces(store):
        gain[...] = gather_spread(oh_cell, spread)

        @pl.loop(0, TILES)
        def _(t):
            for xb in range(4):
                more = gain[temp_rows(t, xb), :]
                rows = own_rows(t, xb)
                for j in range(7):
                    store[19 + j, rows, :] = store[19 + j, rows, :] + WEIGHTS_HEAT[j] * more

    def ghosts(n):
        ghost = r2[n, 8:16, :]
        for h in range(1, 16):
            ghost = ghost + r2[n, h * 16 + 8 : h * 16 + 16, :]
        return ghost

    def cool_bricks(bricks, fluid, layers):
        fill_spread(blcol[...], WALL_COEF * (msg[bricks] - arrived(fluid)), spread)
        loss = gather_spread(oh_brick, spread)
        brick[...] = conduct(brick[...], ghosts(layers), loss)


    ways = [(1, 0), (-1, 0), (0, 1), (0, -1)]
    inside = {(1, 0): x > 0, (-1, 0): x < GX - 1, (0, 1): y > 0, (0, -1): y < GY - 1}
    leave_row, leave_tile = (39, 8), (TILES, 1)
    enter_row, enter_tile = (7, 40), (0, TILES + 1)
    edge_lane = (128 - NZ, 0)

    def plan_copies(step, plan, send, recv):
        return [
            pltpu.make_async_remote_copy(
                src_ref=source,
                dst_ref=target,
                send_sem=send.at[step, n],
                recv_sem=recv.at[step, n],
                device_id=peer,
                device_id_type=MESH,
            )
            for n, (source, target, peer) in enumerate(plan)
        ]

    def flow_copies(step):
        plan = []
        for n, (dx, dy) in enumerate(ways):
            source, target = (xf, xfr) if n < 2 else (yf, yfr)
            plan.append((source.at[step, n % 2], target.at[step, n % 2], (xn(dx), yn(dy))))
        for c, (_, dx, dy) in enumerate(CORNERS):
            plan.append((cf.at[step, c], cfr.at[step, c], (xn(dx), yn(dy))))
        return plan_copies(step, plan, flow_send, flow_recv)

    def heat_copies(step):
        plan = []
        for n, (dx, dy) in enumerate(ways):
            source, target = (xh, xhr) if n < 2 else (yh, yhr)
            plan.append((source.at[step, n % 2], target.at[step, n % 2], (xn(dx), yn(dy))))
        return plan_copies(step, plan, heat_send, heat_recv)

    def send_flow_halo(step, store):
        for n in range(2):
            for k, pop in enumerate(SIDES[n][0]):
                rows = pl.ds(PITCH + leave_row[n], 16, stride=PITCH)
                xf[step, n, k * 16 : (k + 1) * 16, :] = store[pop, rows, :]
        at = iota((32, 128), 1)
        for n in range(2):
            top = leave_tile[n] * PITCH + 8
            parts = []
            for k, pop in enumerate(SIDES[2 + n][0]):
                turn = ((k % 4) * NZ - edge_lane[n]) % 128
                part = store[pop, top : top + 32, :]
                parts.append(pltpu.roll(part, turn, 1) if turn else part)
            for k in range(1, 4):
                parts[0] = jnp.where(at >= k * NZ, parts[k], parts[0])
            yf[step, n, 0:32, :] = parts[0]
            yf[step, n, 32:64, :] = parts[4]
        for c, (pop, dx, dy) in enumerate(CORNERS):
            row = leave_tile[dy < 0] * PITCH + leave_row[dx < 0]
            cf[step, c] = jnp.broadcast_to(store[pop, row : row + 1, :], (8, 128))
        for copy in flow_copies(step):
            copy.start()

    def end_flow_halo(step, store):
        for copy in flow_copies(step):
            copy.wait()
        for n in range(2):
            for k, pop in enumerate(SIDES[n][0]):
                rows = pl.ds(PITCH + enter_row[n], 16, stride=PITCH)
                store[pop, rows, :] = jnp.where(
                    inside[ways[n]], xfr[step, n, k * 16 : (k + 1) * 16, :], 0.0
                )
        for n in range(2):
            top = enter_tile[n] * PITCH + 8
            for k, pop in enumerate(SIDES[2 + n][0]):
                part = yfr[step, n, (k // 4) * 32 : (k // 4 + 1) * 32, :]
                turn = (edge_lane[n] - (k % 4) * NZ) % 128
                part = pltpu.roll(part, turn, 1) if turn else part
                store[pop, top : top + 32, :] = jnp.where(inside[ways[2 + n]], part, 0.0)
        for c, (pop, dx, dy) in enumerate(CORNERS):
            row = enter_tile[dy < 0] * PITCH + enter_row[dx < 0]
            known = inside[(dx, 0)] & inside[(0, dy)]
            store[pop, row : row + 1, :] = jnp.where(known, cfr[step, c, 0:1, :], 0.0)

    def send_heat_halo(step, store):
        for n in range(2):
            rows = pl.ds(PITCH + leave_row[n], 16, stride=PITCH)
            more = WEIGHTS_HEAT[1] * edge[80 - 16 * n : 96 - 16 * n, :]
            xh[step, n] = store[SIDES[n][1], rows, :] + more
            top = leave_tile[n] * PITCH + 8
            more = WEIGHTS_HEAT[1] * edge[32 - 32 * n : 64 - 32 * n, :]
            yh[step, n] = store[SIDES[2 + n][1], top : top + 32, :] + more
        for copy in heat_copies(step):
            copy.start()

    def end_heat_halo(step, store):
        for copy in heat_copies(step):
            copy.wait()
        for n in range(2):
            rows = pl.ds(PITCH + enter_row[n], 16, stride=PITCH)
            store[SIDES[n][1], rows, :] = jnp.where(inside[ways[n]], xhr[step, n], 0.0)
            top = enter_tile[n] * PITCH + 8
            store[SIDES[2 + n][1], top : top + 32, :] = jnp.where(
                inside[ways[2 + n]], yhr[step, n], 0.0
            )


    def store_relaxed(store, t, xb, f, g):
        out_f, out_g = collide(f, g, solid[natural(t, xb)] == 1)
        rows = own_rows(t, xb)
        for i, value in enumerate(out_f + out_g):
            store[i, rows, :] = value

    def relax_first(low, high):
        @pl.loop(low, high)
        def _(t):
            for xb in range(4):
                rows, lanes = natural(t, xb)
                f = [flow[i, rows, lanes] for i in range(19)]
                g = [heat[j, rows, lanes] for j in range(7)]
                store_relaxed(first, t, xb, f, g)

    def relax_second(t, xb):
        f = [pull(first, i, t, xb, lane) for i in range(19)]
        g = [pull(first, 19 + j, t, xb, lane) for j in range(7)]
        store_relaxed(second, t, xb, f, g)

    def hand_flow(t, xb):
        rows, lanes = natural(t, xb)
        for i in range(19):
            flow_out[i, rows, lanes] = pull(second, i, t, xb, lane)

    def along_sides(act):
        @pl.loop(0, (TILES - 2) // 2)
        def _(n):
            for u in range(2):
                for xb in (0, 3):
                    act(1 + 2 * n + u, xb)

        @pl.loop(0, 2)
        def _(n):
            for xb in range(4):
                act(n * (TILES - 1), xb)

    def inside_sides(act):
        @pl.loop(0, (TILES - 2) // 2)
        def _(n):
            for u in range(2):
                for xb in (1, 2):
                    act(1 + 2 * n + u, xb)

    def sum_heat(g):
        return g[0] + ((g[1] + g[2]) + (g[3] + g[4]) + (g[5] + g[6]))

    def pulled_temp(t, xb):
        temps[temp_rows(t, xb), :] = sum_heat([pull(first, 19 + j, t, xb, lane) for j in range(7)])


    loads["owners"].wait()
    loads["cells"].wait()
    by_rank = compact_own(ranked(owners[own_faces, :]), cells[...] + 1)
    table = jnp.transpose(
        jnp.concatenate([by_rank, jnp.zeros((128 - CAP, 128), F32)], axis=0)
    )
    _, low, live = split_cell(table)
    lcol[...] = jnp.where(live, low, -1)
    a, low, live = split_cell(by_rank)
    arow[...] = a
    lrow[...] = jnp.where(live, low, 0)


    loads["heat"].wait()
    loads["solid"].start()
    loads["flow"].start()

    @pl.loop(0, TILES // 2)
    def _(n):
        for u in range(2):
            for xb in range(4):
                rows, lanes = natural(n * 2 + u, xb)
                temps[temp_rows(n * 2 + u, xb), :] = sum_heat(
                    [heat[j, rows, lanes] for j in range(7)]
                )

    fill_onehots(arow[...], oh_cell)
    look_up(False)
    fill_message(0, found[...])
    loads["brick"].wait()
    brick[...] = to_rows(brick_flat[...])
    store_faces(brick[...], faces)
    pl.semaphore_wait(barrier, len(peers))
    start_one(0)

    loads["spots"].wait()

    def from_device(b):
        rows = pl.ds(b, 128, stride=8)
        return owners[rows, :] == me, spots[rows, :].astype(F32) + 1.0

    table = compact(from_device, key, val, packed)
    for n in range(32):
        source = ((n >> 1) & 7) * 16 + (n & 1) * 8 + (n >> 4) * 4
        reordered[n * 4 : n * 4 + 4, :] = packed[source : source + 4, :]
    table = reordered[...]
    _, low, live = split_spot(table)
    blcol[...] = jnp.where(live, low, -1)
    a, low, live = split_spot(jnp.transpose(table)[:CAP, :])
    brow[...] = a
    blrow[...] = jnp.where(live, low, 0)

    ask_bricks(1)
    start_one(1)
    loads["ids"].wait()
    loads["links"].wait()
    place = (core, xc, ylo, q, inner, outer)
    fill_pick(place, ids[...], links[...], wide, by_slot, pick)
    end_one(0)
    start_two(0)
    fill_onehots(brow[...], oh_brick)
    fill_edges(arow[...], oh_edge)
    loads["solid"].wait()
    loads["flow"].wait()
    relax_first(0, 2)
    end_one(1)
    start_two(1)
    relax_first(2, TILES)
    send_flow_halo(0, first)
    end_two(0)
    cool_bricks(1, 0, 0)
    store_faces(brick[...], faces)
    ask_bricks(2)
    start_one(2)
    end_two(1)
    heat_sides(1, 0)
    send_heat_halo(0, first)
    heat_faces(first)


    @pl.loop(0, (TILES - 2) // 2)
    def _(n):
        for u in range(2):
            for xb in range(4):
                pulled_temp(1 + 2 * n + u, xb)

    end_one(2)
    start_two(2)
    look_up(True)
    end_heat_halo(0, first)
    for t in range(TILES):
        for xb in range(4):
            if t in (0, TILES - 1) or xb in (0, 3):
                pulled_temp(t, xb)
    fill_message(3, found[...] + look_up_edges())
    start_one(3)
    end_flow_halo(0, first)
    along_sides(relax_second)
    send_flow_halo(1, second)
    end_one(3)
    start_two(3)
    inside_sides(relax_second)
    end_two(2)
    heat_sides(2, 3)
    send_heat_halo(1, second)
    heat_faces(second)
    inside_sides(hand_flow)
    for n in range(3):
        end_sends(n)
    end_flow_halo(1, second)
    along_sides(hand_flow)
    end_two(3)
    lost[...] = WALL_COEF * (msg[2] - arrived(3))
    layers[...] = ghosts(2)
    end_sends(3)
    end_heat_halo(1, second)


def hand_out_kernel(
    flow,
    second_heat,
    brick,
    lost,
    layers,
    blcol,
    oh_brick,
    flow_out,
    heat_out,
    brick_out,
    heat,
    flat,
    spread,
    sems,
):
    lane = iota((8, 128), 1)
    copies = []
    for n in range(4):
        part = pl.ds(n * 5, 5 if n < 3 else 4)
        copies.append(pltpu.make_async_copy(flow.at[part], flow_out.at[part], sems.at[3 + n]))
        copies[-1].start()
    store = Lattice(None, second_heat)

    @pl.loop(0, TILES // 4)
    def _(n):
        for u in range(4):
            t = n * 4 + u
            for xb in range(4):
                for j in range(7):
                    rows, lanes = natural(t, xb)
                    heat[j, rows, lanes] = pull(store, 19 + j, t, xb, lane)

    copies.append(pltpu.make_async_copy(heat, heat_out, sems.at[1]))
    copies[-1].start()
    fill_spread(blcol[...], lost[...], spread)
    loss = gather_spread(oh_brick, spread)
    from_rows(conduct(brick[...], layers[...], loss), flat)
    copies.append(pltpu.make_async_copy(flat, brick_out, sems.at[2]))
    copies[-1].start()
    for copy in copies:
        copy.wait()


def body(
    flow_pops,
    heat_pops,
    solid_flag,
    brick_temp,
    brick_ids,
    brick_links,
    face_cell,
    face_owner,
    face_spot,
):
    shape = jax.ShapeDtypeStruct
    dma = pltpu.SemaphoreType.DMA
    near = pl.BlockSpec(memory_space=pltpu.VMEM)
    far = pl.BlockSpec(memory_space=pltpu.HBM)
    grid = (TILES * ROWS, 128)
    inputs = (
        flow_pops,
        heat_pops,
        solid_flag,
        face_owner.reshape(1024, 128),
        face_spot.reshape(1024, 128),
        face_cell.reshape(1024, 128),
        brick_temp,
        brick_ids.reshape(2, 128),
        brick_links.T,
    )
    results = pl.pallas_call(
        steps_kernel,
        out_shape=[
            pltpu.VMEM(flow_pops.shape, F32),
            pltpu.VMEM((7, TALL, 128), F32),
            pltpu.VMEM((16, 128), F32),
            pltpu.VMEM((128, 128), F32),
            pltpu.VMEM((8, 128), F32),
            pltpu.VMEM((128, 128), I32),
            pltpu.VMEM((16, SLOTS), BF16),
        ],
        in_specs=[far] * 9,
        out_specs=[near] * 7,
        scratch_shapes=[
            pltpu.VMEM((26, TALL, 128), F32),
            pltpu.VMEM((19, TALL, 128), F32),
            pltpu.VMEM(flow_pops.shape, F32),
            pltpu.VMEM(heat_pops.shape, F32),
            pltpu.VMEM(solid_flag.shape, I32),
            pltpu.VMEM((1024, 128), I32),
            pltpu.VMEM((1024, 128), I32),
            pltpu.VMEM((8, 128), I32),
            pltpu.VMEM((2, 512), F32),
            pltpu.VMEM((2, 128), I32),
            pltpu.VMEM((6, 256), I32),
            pltpu.VMEM((8, 128, 128), F32),
            pltpu.VMEM((8, 128, 128), F32),
            pltpu.VMEM((128, 128), F32),
            pltpu.VMEM((128, 128), F32),
            pltpu.VMEM((128, 256), F32),
            pltpu.VMEM((256, 128), F32),
            pltpu.VMEM((192, 128), BF16),
            pltpu.VMEM((TILES * ROWS, SLOTS), BF16),
            pltpu.VMEM((96, SLOTS), BF16),
            pltpu.VMEM((CAP, 128), I32),
            pltpu.VMEM((CAP, 128), I32),
            pltpu.VMEM((128, 128), I32),
            pltpu.VMEM((CAP, 128), I32),
            pltpu.VMEM((CAP, 128), I32),
            pltpu.VMEM(grid, F32),
            pltpu.VMEM(grid, F32),
            pltpu.VMEM((96, 128), F32),
            pltpu.VMEM((SLOTS, 256), BF16),
            pltpu.VMEM((CAP, 128), F32),
            pltpu.VMEM((4, 128, 128), F32),
            pltpu.VMEM((8, 128), F32),
            pltpu.VMEM((4, 8 * 24, 128), F32),
            pltpu.VMEM((4, 8 * 24, 128), F32),
            pltpu.VMEM((4, 16 * 16, 128), F32),
            pltpu.VMEM((4, 16 * 16, 128), F32),
            pltpu.VMEM((2, 2, 80, 128), F32),
            pltpu.VMEM((2, 2, 80, 128), F32),
            pltpu.VMEM((2, 2, 64, 128), F32),
            pltpu.VMEM((2, 2, 64, 128), F32),
            pltpu.VMEM((2, 4, 8, 128), F32),
            pltpu.VMEM((2, 4, 8, 128), F32),
            pltpu.VMEM((2, 2, 16, 128), F32),
            pltpu.VMEM((2, 2, 16, 128), F32),
            pltpu.VMEM((2, 2, 32, 128), F32),
            pltpu.VMEM((2, 2, 32, 128), F32),
            dma((9,)),
            dma((4, 8)),
            dma((4, 8)),
            dma((4, 16)),
            dma((4, 16)),
            dma((2, 8)),
            dma((2, 8)),
            dma((2, 4)),
            dma((2, 4)),
        ],
        compiler_params=pltpu.CompilerParams(
            collective_id=0, has_side_effects=True, vmem_limit_bytes=46 << 20
        ),
    )(*(pltpu.with_memory_space_constraint(value, pltpu.HBM) for value in inputs))
    flow, heat, brick = pl.pallas_call(
        hand_out_kernel,
        out_shape=[
            shape(flow_pops.shape, F32),
            shape(heat_pops.shape, F32),
            shape(brick_temp.shape, F32),
        ],
        in_specs=[near] * 7,
        out_specs=[far] * 3,
        scratch_shapes=[
            pltpu.VMEM(heat_pops.shape, F32),
            pltpu.VMEM(brick_temp.shape, F32),
            pltpu.VMEM((SLOTS, 256), BF16),
            dma((7,)),
        ],
        compiler_params=pltpu.CompilerParams(vmem_limit_bytes=8 << 20),
    )(*results)
    return flow, heat, brick


def solution(mesh):
    return jax.shard_map(
        body,
        mesh=mesh,
        in_specs=(
            P(None, "gx", "gy"),
            P(None, "gx", "gy"),
            P("gx", "gy"),
            P(("gx", "gy"), None),
            P(),
            P(),
            P(),
            P(),
            P(),
        ),
        out_specs=(P(None, "gx", "gy"), P(None, "gx", "gy"), P(("gx", "gy"), None)),
        check_vma=False,
    )
```

```python
import functools

import jax
import jax.numpy as jnp
from jax import lax
from jax.experimental import pallas as pl
from jax.experimental.pallas import tpu as pltpu
from jax.sharding import PartitionSpec as P

MESH = pl.DeviceIdType.MESH
F32, BF16, I32 = jnp.float32, jnp.bfloat16, jnp.int32

VELOCITY = [
    (0, 0, 0),
    (1, 0, 0),
    (-1, 0, 0),
    (0, 1, 0),
    (0, -1, 0),
    (0, 0, 1),
    (0, 0, -1),
    (1, 1, 0),
    (-1, -1, 0),
    (1, -1, 0),
    (-1, 1, 0),
    (1, 0, 1),
    (-1, 0, -1),
    (1, 0, -1),
    (-1, 0, 1),
    (0, 1, 1),
    (0, -1, -1),
    (0, 1, -1),
    (0, -1, 1),
]
SIDE_SWAP = [1, 0, 3, 2, 5, 4]
WEIGHTS_HEAT = [0.25] + [0.125] * 6
TAU_FLOW, TAU_HEAT = 0.8, 0.9
BUOYANCY = 0.002
WALL_COEF = 0.1
BRICK_LOSS = 0.5
COND_BASE, COND_SLOPE = 0.04, 0.1
LATENT, MELT, MELT_WIDTH = 2.0, 4.0, 0.5

GX, GY = 16, 8
DEV = GX * GY
CAP = 16
ROWS, TILES, NZ = 32, 16, 32
PITCH = 48
TALL = (TILES + 2) * PITCH
SLOTS = CAP * DEV

ALL_VELOCITY = VELOCITY + VELOCITY[:7]
SIDES = [([9, 1, 11, 13, 7], 20), ([10, 2, 12, 14, 8], 21)]
SIDES += [([7, 3, 15, 17, 10], 22), ([8, 4, 16, 18, 9], 23)]
CORNERS = [(7, 1, 1), (8, -1, -1), (9, 1, -1), (10, -1, 1)]


def iota(shape, dim):
    return lax.broadcasted_iota(I32, shape, dim)


def lane_pick(rows, index):
    return jnp.take_along_axis(rows, index, axis=1, mode="promise_in_bounds")


def compact(get, key, val, packed):
    square = (128, 128)
    wide_row, wide_lane = iota((128, 256), 0), iota((128, 256), 1)
    prefix = jnp.where(wide_row <= wide_lane, 1.0, 0.0).astype(BF16)
    before = jnp.zeros(square, F32)
    for b in range(8):
        mask, value = get(b)
        counts = jnp.dot(
            jnp.where(mask, 1.0, 0.0).astype(BF16), prefix, preferred_element_type=F32
        )
        key[b] = jnp.where(mask, counts[:, :128] + before, 0.0)
        val[b] = value
        before = before + counts[:, 128:]

    @pl.loop(0, 4)
    def _(c):
        for u in range(4):
            rows = pl.ds(pl.multiple_of(c * 32 + u * 8, 8), 8)
            keys = [key[b, rows, :] for b in range(8)]
            vals = [val[b, rows, :] for b in range(8)]
            at = iota((8, 128), 1)
            out = jnp.zeros((8, 128), F32)
            for r in range(CAP):
                hit = jnp.zeros((8, 128), F32)
                for b in range(8):
                    hit = jnp.where(keys[b] == float(r + 1), vals[b], hit)
                out = jnp.where(at == r, jnp.sum(hit, axis=1, keepdims=True), out)
            packed[rows, :] = out

    return packed[...]


def compact_own(place, cell):
    square = (128, 128)
    wide_row, wide_lane = iota((128, 256), 0), iota((128, 256), 1)
    prefix = jnp.where(wide_row <= wide_lane, 1.0, 0.0).astype(BF16)
    device, rank = iota(square, 0), iota((CAP, 128), 0).astype(F32) + 1.0
    before = jnp.zeros(square, F32)
    masks, values = [], []
    for b in range(8):
        mask = device == place[b : b + 1, :]
        masks.append(jnp.where(mask, 1.0, 0.0).astype(BF16))
        counts = jnp.dot(masks[-1], prefix, preferred_element_type=F32)
        own = jnp.where(mask, counts[:, :128] + before, 0.0)
        before = before + counts[:, 128:]
        match = rank == jnp.sum(own, axis=0, keepdims=True)
        high = (cell[b : b + 1, :] >> 8).astype(F32)
        low = (cell[b : b + 1, :] & 255).astype(F32)
        both = [jnp.where(match, high, 0.0), jnp.where(match, low, 0.0)]
        values.append(jnp.concatenate(both, axis=0).astype(BF16))
    out = lax.dot_general(
        jnp.concatenate(values, axis=1),
        jnp.concatenate(masks, axis=1),
        (((1,), (1,)), ((), ())),
        preferred_element_type=F32,
    )
    return out[:CAP] * 256.0 + out[CAP:]


def split_cell(c):
    c = c.astype(I32) - 1
    live = c >= 0
    a = ((c >> 7) & 15) * ROWS + (c >> 11)
    return jnp.where(live, a, -1), c & 127, live


def split_spot(c):
    c = c.astype(I32) - 1
    live = c >= 0
    return jnp.where(live, c >> 6, -1), c & 63, live


def fill_onehots(row, onehot):
    count = onehot.shape[0]
    for r in range(CAP):
        for q in range(0, count, 128):
            size = min(128, count)
            part = iota((size, 128), 0) + q == row[r : r + 1, :]
            onehot[q : q + size, r * 128 : (r + 1) * 128] = jnp.where(part, 1.0, 0.0).astype(BF16)


def fill_edges(row, onehot):
    n = iota((96, 128), 0)
    last = n - 32 + (TILES - 1) * ROWS
    sides = jnp.where(n < 80, (n - 64) * ROWS, (n - 80) * ROWS + ROWS - 1)
    wanted = jnp.where(n < 32, n, jnp.where(n < 64, last, sides))
    for r in range(CAP):
        part = wanted == row[r : r + 1, :]
        onehot[:, r * 128 : (r + 1) * 128] = jnp.where(part, 1.0, 0.0).astype(BF16)


def ranked(device):
    return (((device >> 2) & 1) << 6) | ((device >> 4) << 3) | (((device >> 3) & 1) << 2) | (device & 3)


def fill_pick(spot, ids, links, wide, by_slot, pick):
    core, xc, ylo, q, inner, outer = spot
    order = jnp.concatenate([ids[0:1, :], ids[1:2, :]], axis=1)
    chosen = jnp.where(iota((256, 256), 0) == order, 1.0, 0.0).astype(BF16)
    wide[...] = jnp.zeros((128, 256), F32)
    wide[0:6, :] = jnp.dot(
        links.astype(F32).astype(BF16), chosen, preferred_element_type=F32
    )
    by_slot[0:128, :] = jnp.transpose(wide[:, 0:128])
    by_slot[128:256, :] = jnp.transpose(wide[:, 128:256])
    at, to = iota((16, 128), 1), iota((16, 128), 0)
    half = jnp.where(q >= 4, ids[1:2, :], ids[0:1, :])
    from_b, from_inner, side = at >> 6, (at >> 3) & 7, at & 7
    column = lax.rem(q, 4) * 32 + (from_inner >> 2) * 16 + ylo * 8 + (from_inner & 3) * 2 + from_b
    here = lane_pick(jnp.broadcast_to(half.astype(F32), (16, 128)), column)
    for b in range(2):
        named = jnp.concatenate(
            [
                by_slot[pl.ds((core * 8 + low * 4 + xc) * 2 + b, 8, stride=32), :]
                for low in range(2)
            ],
            axis=0,
        )
        for s in range(6):
            j = s * 2 + b
            n = named[:, s : s + 1]
            remote = (n == here) & (side == SIDE_SWAP[s])
            own = (n < 0.0) & (to == outer) & (at == b * 64 + inner * 8 + s)
            pick[j * 16 : (j + 1) * 16, :] = jnp.where(remote | own, 1.0, 0.0).astype(BF16)


def to_rows(brick):
    at = iota((1, 128), 1)
    rows = []
    for b in range(2):
        for x in range(8):
            part = brick[b : b + 1, (x // 2) * 128 : (x // 2 + 1) * 128]
            part = pltpu.roll(part, 64, 1) if x % 2 else part
            rows.append(jnp.where(at < 64, part, 0.0))
    return jnp.concatenate(rows, axis=0)


def from_rows(rows, out):
    turned = pltpu.roll(rows, 64, 1)
    at = iota((1, 128), 1)
    for b in range(2):
        for q in range(4):
            r = b * 8 + q * 2
            out[b : b + 1, q * 128 : (q + 1) * 128] = jnp.where(
                at < 64, rows[r : r + 1, :], turned[r + 1 : r + 2, :]
            )


def collide(f, g, solid):
    pairs = [(1, 2), (3, 4), (5, 6), (7, 8), (9, 10), (11, 12), (13, 14), (15, 16), (17, 18)]
    total = {a: f[a] + f[b] for a, b in pairs}
    diff = {a: f[a] - f[b] for a, b in pairs}
    density = f[0] + (
        (total[1] + total[3])
        + (total[5] + total[7])
        + (total[9] + total[11])
        + (total[13] + total[15])
        + total[17]
    )
    inverse = 1.0 / density
    ux = (diff[1] + diff[7] + diff[9] + diff[11] + diff[13]) * inverse
    uy = (diff[3] + diff[7] - diff[9] + diff[15] + diff[17]) * inverse
    uz = (diff[5] + diff[11] - diff[13] + diff[15] - diff[17]) * inverse
    temp = g[0] + ((g[1] + g[2]) + (g[3] + g[4]) + (g[5] + g[6]))
    sz = uz + (TAU_FLOW * BUOYANCY) * (temp - 1.0) * inverse
    base = 1.0 - 1.5 * (ux * ux + uy * uy + sz * sz)
    keep = 1.0 - 1.0 / TAU_FLOW
    along_of = {1: ux, 3: uy, 5: sz, 7: ux + uy, 9: ux - uy}
    along_of.update({11: ux + sz, 13: ux - sz, 15: uy + sz, 17: uy - sz})
    out_f = [None] * 19
    k0 = density * (1.0 / 3.0 / TAU_FLOW)
    out_f[0] = jnp.where(solid, f[0], keep * f[0] + k0 * base)
    scale = {1: density * (1.0 / 18.0 / TAU_FLOW), 7: density * (1.0 / 36.0 / TAU_FLOW)}
    level = {a: k * base for a, k in scale.items()}
    bend = {a: 4.5 * k for a, k in scale.items()}
    lean = {a: 3.0 * k for a, k in scale.items()}
    for a, b in pairs:
        kind = 1 if a < 7 else 7
        along = along_of[a]
        even = level[kind] + bend[kind] * (along * along)
        odd = lean[kind] * along
        out_f[a] = jnp.where(solid, f[b], (even + odd) + keep * f[a])
        out_f[b] = jnp.where(solid, f[a], (even - odd) + keep * f[b])
    keep = 1.0 - 1.0 / TAU_HEAT
    out_g = [None] * 7
    out_g[0] = jnp.where(solid, g[0], keep * g[0] + (0.25 / TAU_HEAT) * temp)
    k = (0.125 / TAU_HEAT) * temp
    for a, u in ((1, ux), (3, uy), (5, uz)):
        odd = (4.0 * k) * u
        out_g[a] = jnp.where(solid, g[a + 1], (k + odd) + keep * g[a])
        out_g[a + 1] = jnp.where(solid, g[a], (k - odd) + keep * g[a + 1])
    return out_f, out_g


class Lattice:
    def __init__(self, flow, heat):
        self.flow, self.heat = flow, heat

    def at(self, key):
        pop = key[0]
        if pop < 19:
            return self.flow, key
        return self.heat, (pop - 19,) + tuple(key[1:])

    def __getitem__(self, key):
        ref, key = self.at(key)
        return ref[key]

    def __setitem__(self, key, value):
        ref, key = self.at(key)
        ref[key] = value


def pull(store, pop, t, xb, lane):
    cx, cy, cz = ALL_VELOCITY[pop]
    at = pop

    def tile(step):
        return store[at, pl.ds((t + 1 + step) * PITCH + 8 + xb * 8 - cx, 8), :]

    here = tile(0)
    if cy == 1:
        here = jnp.where(lane >= 128 - NZ, tile(-1), here)
    if cy == -1:
        here = jnp.where(lane < NZ, tile(1), here)
    shift = (cy * NZ + cz) % 128
    if shift:
        here = pltpu.roll(here, shift, 1)
    if cz == 1:
        here = jnp.where(lane & (NZ - 1) == 0, 0.0, here)
    if cz == -1:
        here = jnp.where(lane & (NZ - 1) == NZ - 1, 0.0, here)
    return here


def own_rows(t, xb):
    return pl.ds((t + 1) * PITCH + 8 + xb * 8, 8)


def natural(t, xb):
    return pl.ds(xb * 8, 8), pl.ds(pl.multiple_of(t * 128, 128), 128)


def temp_rows(t, xb):
    return pl.ds(pl.multiple_of(t * ROWS + xb * 8, 8), 8)


def halves(value):
    high = value.astype(BF16)
    return high, (value - high.astype(F32)).astype(BF16)


def fill_spread(columns, flux, spread):
    high, low = halves(flux)
    high, low = high.astype(F32), low.astype(F32)
    at = iota((128, 128), 1)
    for r in range(CAP):
        hit = at == columns[:, r : r + 1]
        rows = slice(r * 128, (r + 1) * 128)
        spread[rows, 0:128] = jnp.where(hit, high[:, r : r + 1], 0.0).astype(BF16)
        spread[rows, 128:256] = jnp.where(hit, low[:, r : r + 1], 0.0).astype(BF16)


def gather_spread(onehot, spread):
    both = jnp.dot(onehot[...], spread[...], preferred_element_type=F32)
    return both[:, :128] + both[:, 128:]


def brick_lookup(brick, brow, blrow):
    out = jnp.zeros((CAP, 128), F32)
    for a in range(16):
        row = jnp.broadcast_to(brick[a : a + 1, :], (CAP, 128))
        out = jnp.where(brow == a, lane_pick(row, blrow), out)
    return out


def store_faces(brick, faces):
    at, row = iota((16, 128), 1), iota((16, 128), 0)
    line = iota((1, 128), 1)
    mine = ((at >> 3) & 7) == (row & 7)
    wanted = {
        2: at & 7,
        3: 56 + (at & 7),
        4: (at & 7) * 8,
        5: (at & 7) * 8 + 7,
    }
    faces[6:8, :] = jnp.zeros((2, 128), F32)
    for s in range(6):
        if s < 2:
            low, high = brick[7 * s : 7 * s + 1, :], brick[8 + 7 * s : 9 + 7 * s, :]
        else:
            got = jnp.where(mine, lane_pick(brick, wanted[s]), 0.0)
            low = jnp.sum(got[0:8], axis=0, keepdims=True)
            high = jnp.sum(got[8:16], axis=0, keepdims=True)
        faces[s : s + 1, :] = jnp.where(line < 64, low, pltpu.roll(high, 64, 1))


def conduct(brick, ghost, loss):
    at, row = iota((16, 128), 1), iota((16, 128), 0)
    x = row & 7

    other_brick = pltpu.roll(ghost, 64, 1)

    def ghost_rows(s):
        return jnp.where(row < 8, ghost[s : s + 1, :], other_brick[s : s + 1, :])

    over_z = x * 8 + (at & 7)
    over_y = x * 8 + ((at >> 3) & 7)
    beside = [
        jnp.where(x == 0, ghost_rows(0), pltpu.roll(brick, 1, 0)),
        jnp.where(x == 7, ghost_rows(1), pltpu.roll(brick, 15, 0)),
        jnp.where(at < 8, lane_pick(ghost_rows(2), over_z), pltpu.roll(brick, 8, 1)),
        jnp.where(at >= 56, lane_pick(ghost_rows(3), over_z), pltpu.roll(brick, 120, 1)),
        jnp.where((at & 7) == 0, lane_pick(ghost_rows(4), over_y), pltpu.roll(brick, 1, 1)),
        jnp.where((at & 7) == 7, lane_pick(ghost_rows(5), over_y), pltpu.roll(brick, 127, 1)),
    ]
    here = COND_BASE * (1.0 + COND_SLOPE * brick)
    spread = jnp.zeros((16, 128), F32)
    for other in beside:
        spread += 0.5 * (here + COND_BASE * (1.0 + COND_SLOPE * other)) * (other - brick)
    phase = 1.0 / (1.0 + jnp.exp(-(brick - MELT) / MELT_WIDTH))
    capacity = 1.0 + LATENT * phase * (1.0 - phase) / MELT_WIDTH
    return jnp.where(at < 64, brick + (spread - BRICK_LOSS * loss) / capacity, 0.0)


def steps_kernel(
    flow_in,
    heat_in,
    solid_in,
    owners_in,
    spots_in,
    cells_in,
    brick_in,
    ids_in,
    links_in,
    flow_out,
    second_heat,
    brick,
    lost,
    layers,
    blcol,
    oh_brick,
    first,
    second_flow,
    flow,
    heat,
    solid,
    owners,
    spots,
    cells,
    brick_flat,
    ids,
    links,
    key,
    val,
    packed,
    reordered,
    wide,
    by_slot,
    pick,
    oh_cell,
    oh_edge,
    arow,
    lrow,
    lcol,
    brow,
    blrow,
    temps,
    gain,
    edge,
    spread,
    found,
    msg,
    faces,
    s1,
    r1,
    s2,
    r2,
    xf,
    xfr,
    yf,
    yfr,
    cf,
    cfr,
    xh,
    xhr,
    yh,
    yhr,
    load_sem,
    s1_send,
    s1_recv,
    s2_send,
    s2_recv,
    flow_send,
    flow_recv,
    heat_send,
    heat_recv,
):
    x, y = lax.axis_index("gx"), lax.axis_index("gy")
    me = x * GY + y
    core, q = lax.rem(x, 2), x // 2
    xc, ylo = lax.rem(y, 4), y // 4
    inner, outer = core * 4 + xc, ylo * 8 + q

    def inner_peer(i):
        return (q * 2 + i // 4, ylo * 4 + lax.rem(i, 4))

    def outer_peer(h):
        return (lax.rem(h, 8) * 2 + core, (h // 8) * 4 + xc)

    def inner_next(k):
        return lax.rem(inner + k, 8)

    def outer_next(k):
        return lax.rem(outer + k, 16)

    def xn(k):
        return lax.rem(x + (k + GX), GX)

    def yn(k):
        return lax.rem(y + (k + GY), GY)

    second = Lattice(second_flow, second_heat)
    own_faces = pl.ds(pl.multiple_of(me * 8, 8), 8)
    loads = {}
    for n, (name, source, target) in enumerate(
        (
            ("owners", owners_in, owners),
            ("cells", cells_in.at[own_faces, :], cells),
            ("heat", heat_in, heat),
            ("spots", spots_in, spots),
            ("brick", brick_in, brick_flat),
            ("ids", ids_in, ids),
            ("links", links_in, links),
            ("solid", solid_in, solid),
            ("flow", flow_in, flow),
        )
    ):
        loads[name] = pltpu.make_async_copy(source, target, load_sem.at[n])
        if name not in ("solid", "flow"):
            loads[name].start()

    barrier = pltpu.get_barrier_semaphore()
    peers = [(xn(a), yn(b)) for a in (-1, 1) for b in (-1, 1)]
    peers += [outer_peer(outer_next(k)) for k in (10, 6, 2, 14, 9, 11, 5, 7, 1, 3, 13, 15, 8, 4, 12)]
    peers += [(xn(a), yn(b)) for a, b in ((-1, 0), (1, 0), (0, -1), (0, 1))]
    peers += [inner_peer(inner_next(k)) for k in range(1, 8)]
    for peer in peers:
        pl.semaphore_signal(barrier, inc=1, device_id=peer, device_id_type=MESH)

    lane = iota((8, 128), 1)


    def look_up_row(row, outs, u, a, low):
        line = jnp.broadcast_to(temps[pl.ds(row, 1), :], (CAP, 128))
        outs[u % 4] = jnp.where(a == row, lane_pick(line, low), outs[u % 4])

    def look_up(inner_only):
        parts = []
        for n in range(4):
            part = temps[n * 128 : (n + 1) * 128, :]
            if inner_only:
                row = iota((128, 128), 0)
                away = (row & 31 != 0) & (row & 31 != 31)
                if n == 0:
                    away = away & (row >= 32)
                if n == 3:
                    away = away & (row < 96)
                part = jnp.where(away, part, 0.0)
            parts.append(jnp.transpose(part))
        high, low = halves(jnp.concatenate(parts, axis=1))
        both = jnp.concatenate([high, low], axis=0)
        lanes = lrow[...]
        at = iota((128, 128), 0)
        for r in range(0, CAP, 2):
            got = jnp.dot(
                both, oh_cell[:, r * 128 : (r + 2) * 128], preferred_element_type=F32
            )
            got = got[:128] + got[128:]
            for u in range(2):
                hit = jnp.where(
                    at == lanes[r + u : r + u + 1, :], got[:, u * 128 : (u + 1) * 128], 0.0
                )
                found[r + u : r + u + 1, :] = jnp.sum(hit, axis=0, keepdims=True)

    def look_up_edges():
        a, low = arow[...], lrow[...]
        outs = [jnp.zeros((CAP, 128), F32)] * 4
        rows = [t * ROWS + row for t in range(1, TILES - 1) for row in (0, ROWS - 1)]
        rows += [t * ROWS + row for t in (0, TILES - 1) for row in range(ROWS)]
        for u, row in enumerate(rows):
            look_up_row(row, outs, u, a, low)
        return (outs[0] + outs[1]) + (outs[2] + outs[3])

    def fill_message(n, value):
        rest = jnp.zeros((128 - CAP, 128), F32)
        msg[n] = jnp.transpose(jnp.concatenate([value, rest], axis=0))

    def ask_bricks(n):
        fill_message(n, brick_lookup(brick[...], brow[...], blrow[...]))


    def wait_all(buffer, n, rows, sem):
        part = buffer.at[n, pl.ds(0, rows), :]
        pltpu.make_async_copy(part, part, sem.at[n]).wait()

    def one(n, to, slot):
        count = 16 if n % 2 else 24
        return pltpu.make_async_remote_copy(
            src_ref=s1.at[n, pl.ds(pl.multiple_of(to * 24, 8), count), :],
            dst_ref=r1.at[n, pl.ds(pl.multiple_of(slot * 24, 8), count), :],
            send_sem=s1_send.at[n],
            recv_sem=s1_recv.at[n],
            device_id=inner_peer(to),
            device_id_type=MESH,
        )

    def two(n, to, slot):
        count = 8 if n % 2 else 16
        return pltpu.make_async_remote_copy(
            src_ref=s2.at[n, pl.ds(pl.multiple_of(to * 16, 8), count), :],
            dst_ref=r2.at[n, pl.ds(pl.multiple_of(slot * 16, 8), count), :],
            send_sem=s2_send.at[n],
            recv_sem=s2_recv.at[n],
            device_id=outer_peer(to),
            device_id_type=MESH,
        )

    def start_one(n):
        for k in range(8):
            s1[n, k * 24 : k * 24 + 16, :] = msg[n, pl.ds(k, 16, stride=8), :]
            if n % 2 == 0:
                s1[n, k * 24 + 16 : k * 24 + 24, :] = faces[...]
        for k in range(1, 8):
            one(n, inner_next(k), inner).start()
        own = pl.ds(pl.multiple_of(inner * 24, 8), 24)
        r1[n, own, :] = s1[n, own, :]

    def end_one(n):
        wait_all(r1, n, 7 * (16 if n % 2 else 24), s1_recv)

    def start_two(n):
        if n % 2 == 0:
            every = jnp.concatenate(
                [r1[n, k * 24 + 16 : k * 24 + 24, :] for k in range(8)], axis=0
            )
            every = jnp.concatenate([every, pltpu.roll(every, 64, 1)], axis=0)
            high = every.astype(BF16)
            low = every - high.astype(F32)
            at = iota((128, 128), 1)
            both = jnp.where(at < 64, high.astype(F32), pltpu.roll(low, 64, 1)).astype(BF16)
            picked = jnp.dot(pick[...], both, preferred_element_type=F32)
            picked = picked + pltpu.roll(picked, 64, 1)
            at = iota((16, 128), 1)
            for s in range(8):
                pair = jnp.zeros((16, 128), F32)
                if s < 6:
                    top = s * 32
                    pair = jnp.where(at < 64, picked[top : top + 16], picked[top + 16 : top + 32])
                s2[n, pl.ds(8 + s, 16, stride=16), :] = pair
        for h in range(16):
            s2[n, h * 16 : h * 16 + 8, :] = r1[n, pl.ds(h, 8, stride=24), :]
        for k in range(1, 16):
            two(n, outer_next(k), outer).start()
        own = pl.ds(pl.multiple_of(outer * 16, 8), 16)
        r2[n, own, :] = s2[n, own, :]

    def end_two(n):
        wait_all(r2, n, 15 * (8 if n % 2 else 16), s2_recv)

    def end_sends(n):
        wait_all(s1, n, 7 * (16 if n % 2 else 24), s1_send)
        wait_all(s2, n, 15 * (8 if n % 2 else 16), s2_send)

    def arrived(n):
        return jnp.concatenate([r2[n, h * 16 : h * 16 + 8, :] for h in range(16)], axis=0)

    def heat_sides(bricks, fluid):
        fill_spread(lcol[...], WALL_COEF * (arrived(bricks) - msg[fluid]), spread)
        edge[...] = gather_spread(oh_edge, spread)

    def heat_faces(store):
        gain[...] = gather_spread(oh_cell, spread)

        @pl.loop(0, TILES)
        def _(t):
            for xb in range(4):
                more = gain[temp_rows(t, xb), :]
                rows = own_rows(t, xb)
                for j in range(7):
                    store[19 + j, rows, :] = store[19 + j, rows, :] + WEIGHTS_HEAT[j] * more

    def ghosts(n):
        ghost = r2[n, 8:16, :]
        for h in range(1, 16):
            ghost = ghost + r2[n, h * 16 + 8 : h * 16 + 16, :]
        return ghost

    def cool_bricks(bricks, fluid, layers):
        fill_spread(blcol[...], WALL_COEF * (msg[bricks] - arrived(fluid)), spread)
        loss = gather_spread(oh_brick, spread)
        brick[...] = conduct(brick[...], ghosts(layers), loss)


    ways = [(1, 0), (-1, 0), (0, 1), (0, -1)]
    inside = {(1, 0): x > 0, (-1, 0): x < GX - 1, (0, 1): y > 0, (0, -1): y < GY - 1}
    leave_row, leave_tile = (39, 8), (TILES, 1)
    enter_row, enter_tile = (7, 40), (0, TILES + 1)
    edge_lane = (128 - NZ, 0)

    def plan_copies(step, plan, send, recv):
        return [
            pltpu.make_async_remote_copy(
                src_ref=source,
                dst_ref=target,
                send_sem=send.at[step, n],
                recv_sem=recv.at[step, n],
                device_id=peer,
                device_id_type=MESH,
            )
            for n, (source, target, peer) in enumerate(plan)
        ]

    def flow_copies(step):
        plan = []
        for n, (dx, dy) in enumerate(ways):
            source, target = (xf, xfr) if n < 2 else (yf, yfr)
            plan.append((source.at[step, n % 2], target.at[step, n % 2], (xn(dx), yn(dy))))
        for c, (_, dx, dy) in enumerate(CORNERS):
            plan.append((cf.at[step, c], cfr.at[step, c], (xn(dx), yn(dy))))
        return plan_copies(step, plan, flow_send, flow_recv)

    def heat_copies(step):
        plan = []
        for n, (dx, dy) in enumerate(ways):
            source, target = (xh, xhr) if n < 2 else (yh, yhr)
            plan.append((source.at[step, n % 2], target.at[step, n % 2], (xn(dx), yn(dy))))
        return plan_copies(step, plan, heat_send, heat_recv)

    def send_flow_halo(step, store):
        for n in range(2):
            for k, pop in enumerate(SIDES[n][0]):
                rows = pl.ds(PITCH + leave_row[n], 16, stride=PITCH)
                xf[step, n, k * 16 : (k + 1) * 16, :] = store[pop, rows, :]
        at = iota((32, 128), 1)
        for n in range(2):
            top = leave_tile[n] * PITCH + 8
            parts = []
            for k, pop in enumerate(SIDES[2 + n][0]):
                turn = ((k % 4) * NZ - edge_lane[n]) % 128
                part = store[pop, top : top + 32, :]
                parts.append(pltpu.roll(part, turn, 1) if turn else part)
            for k in range(1, 4):
                parts[0] = jnp.where(at >= k * NZ, parts[k], parts[0])
            yf[step, n, 0:32, :] = parts[0]
            yf[step, n, 32:64, :] = parts[4]
        for c, (pop, dx, dy) in enumerate(CORNERS):
            row = leave_tile[dy < 0] * PITCH + leave_row[dx < 0]
            cf[step, c] = jnp.broadcast_to(store[pop, row : row + 1, :], (8, 128))
        for copy in flow_copies(step):
            copy.start()

    def end_flow_halo(step, store):
        for copy in flow_copies(step):
            copy.wait()
        for n in range(2):
            for k, pop in enumerate(SIDES[n][0]):
                rows = pl.ds(PITCH + enter_row[n], 16, stride=PITCH)
                store[pop, rows, :] = jnp.where(
                    inside[ways[n]], xfr[step, n, k * 16 : (k + 1) * 16, :], 0.0
                )
        for n in range(2):
            top = enter_tile[n] * PITCH + 8
            for k, pop in enumerate(SIDES[2 + n][0]):
                part = yfr[step, n, (k // 4) * 32 : (k // 4 + 1) * 32, :]
                turn = (edge_lane[n] - (k % 4) * NZ) % 128
                part = pltpu.roll(part, turn, 1) if turn else part
                store[pop, top : top + 32, :] = jnp.where(inside[ways[2 + n]], part, 0.0)
        for c, (pop, dx, dy) in enumerate(CORNERS):
            row = enter_tile[dy < 0] * PITCH + enter_row[dx < 0]
            known = inside[(dx, 0)] & inside[(0, dy)]
            store[pop, row : row + 1, :] = jnp.where(known, cfr[step, c, 0:1, :], 0.0)

    def send_heat_halo(step, store):
        for n in range(2):
            rows = pl.ds(PITCH + leave_row[n], 16, stride=PITCH)
            more = WEIGHTS_HEAT[1] * edge[80 - 16 * n : 96 - 16 * n, :]
            xh[step, n] = store[SIDES[n][1], rows, :] + more
            top = leave_tile[n] * PITCH + 8
            more = WEIGHTS_HEAT[1] * edge[32 - 32 * n : 64 - 32 * n, :]
            yh[step, n] = store[SIDES[2 + n][1], top : top + 32, :] + more
        for copy in heat_copies(step):
            copy.start()

    def end_heat_halo(step, store):
        for copy in heat_copies(step):
            copy.wait()
        for n in range(2):
            rows = pl.ds(PITCH + enter_row[n], 16, stride=PITCH)
            store[SIDES[n][1], rows, :] = jnp.where(inside[ways[n]], xhr[step, n], 0.0)
            top = enter_tile[n] * PITCH + 8
            store[SIDES[2 + n][1], top : top + 32, :] = jnp.where(
                inside[ways[2 + n]], yhr[step, n], 0.0
            )


    def store_relaxed(store, t, xb, f, g):
        out_f, out_g = collide(f, g, solid[natural(t, xb)] == 1)
        rows = own_rows(t, xb)
        for i, value in enumerate(out_f + out_g):
            store[i, rows, :] = value

    def relax_first(low, high):
        @pl.loop(low, high)
        def _(t):
            for xb in range(4):
                rows, lanes = natural(t, xb)
                f = [flow[i, rows, lanes] for i in range(19)]
                g = [heat[j, rows, lanes] for j in range(7)]
                store_relaxed(first, t, xb, f, g)

    def relax_second(t, xb):
        f = [pull(first, i, t, xb, lane) for i in range(19)]
        g = [pull(first, 19 + j, t, xb, lane) for j in range(7)]
        store_relaxed(second, t, xb, f, g)

    def hand_flow(t, xb):
        rows, lanes = natural(t, xb)
        for i in range(19):
            flow_out[i, rows, lanes] = pull(second, i, t, xb, lane)

    def along_sides(act):
        @pl.loop(0, (TILES - 2) // 2)
        def _(n):
            for u in range(2):
                for xb in (0, 3):
                    act(1 + 2 * n + u, xb)

        @pl.loop(0, 2)
        def _(n):
            for xb in range(4):
                act(n * (TILES - 1), xb)

    def inside_sides(act):
        @pl.loop(0, (TILES - 2) // 2)
        def _(n):
            for u in range(2):
                for xb in (1, 2):
                    act(1 + 2 * n + u, xb)

    def sum_heat(g):
        return g[0] + ((g[1] + g[2]) + (g[3] + g[4]) + (g[5] + g[6]))

    def pulled_temp(t, xb):
        temps[temp_rows(t, xb), :] = sum_heat([pull(first, 19 + j, t, xb, lane) for j in range(7)])


    loads["owners"].wait()
    loads["cells"].wait()
    by_rank = compact_own(ranked(owners[own_faces, :]), cells[...] + 1)
    table = jnp.transpose(
        jnp.concatenate([by_rank, jnp.zeros((128 - CAP, 128), F32)], axis=0)
    )
    _, low, live = split_cell(table)
    lcol[...] = jnp.where(live, low, -1)
    a, low, live = split_cell(by_rank)
    arow[...] = a
    lrow[...] = jnp.where(live, low, 0)


    loads["heat"].wait()
    loads["solid"].start()
    loads["flow"].start()

    @pl.loop(0, TILES // 2)
    def _(n):
        for u in range(2):
            for xb in range(4):
                rows, lanes = natural(n * 2 + u, xb)
                temps[temp_rows(n * 2 + u, xb), :] = sum_heat(
                    [heat[j, rows, lanes] for j in range(7)]
                )

    fill_onehots(arow[...], oh_cell)
    look_up(False)
    fill_message(0, found[...])
    loads["brick"].wait()
    brick[...] = to_rows(brick_flat[...])
    store_faces(brick[...], faces)
    pl.semaphore_wait(barrier, len(peers))
    start_one(0)

    loads["spots"].wait()

    def from_device(b):
        rows = pl.ds(b, 128, stride=8)
        return owners[rows, :] == me, spots[rows, :].astype(F32) + 1.0

    table = compact(from_device, key, val, packed)
    for n in range(32):
        source = ((n >> 1) & 7) * 16 + (n & 1) * 8 + (n >> 4) * 4
        reordered[n * 4 : n * 4 + 4, :] = packed[source : source + 4, :]
    table = reordered[...]
    _, low, live = split_spot(table)
    blcol[...] = jnp.where(live, low, -1)
    a, low, live = split_spot(jnp.transpose(table)[:CAP, :])
    brow[...] = a
    blrow[...] = jnp.where(live, low, 0)

    ask_bricks(1)
    start_one(1)
    loads["ids"].wait()
    loads["links"].wait()
    place = (core, xc, ylo, q, inner, outer)
    fill_pick(place, ids[...], links[...], wide, by_slot, pick)
    end_one(0)
    start_two(0)
    fill_onehots(brow[...], oh_brick)
    fill_edges(arow[...], oh_edge)
    loads["solid"].wait()
    loads["flow"].wait()
    relax_first(0, 2)
    end_one(1)
    start_two(1)
    relax_first(2, TILES)
    send_flow_halo(0, first)
    end_two(0)
    cool_bricks(1, 0, 0)
    store_faces(brick[...], faces)
    ask_bricks(2)
    start_one(2)
    end_two(1)
    heat_sides(1, 0)
    send_heat_halo(0, first)
    heat_faces(first)


    @pl.loop(0, (TILES - 2) // 2)
    def _(n):
        for u in range(2):
            for xb in range(4):
                pulled_temp(1 + 2 * n + u, xb)

    end_one(2)
    start_two(2)
    look_up(True)
    end_heat_halo(0, first)
    for t in range(TILES):
        for xb in range(4):
            if t in (0, TILES - 1) or xb in (0, 3):
                pulled_temp(t, xb)
    fill_message(3, found[...] + look_up_edges())
    start_one(3)
    end_flow_halo(0, first)
    along_sides(relax_second)
    end_one(3)
    start_two(3)
    send_flow_halo(1, second)
    inside_sides(relax_second)
    end_two(2)
    heat_sides(2, 3)
    send_heat_halo(1, second)
    heat_faces(second)
    inside_sides(hand_flow)
    for n in range(3):
        end_sends(n)
    end_flow_halo(1, second)
    along_sides(hand_flow)
    layers[...] = ghosts(2)
    end_two(3)
    lost[...] = WALL_COEF * (msg[2] - arrived(3))
    end_sends(3)
    end_heat_halo(1, second)


def hand_out_kernel(
    flow,
    second_heat,
    brick,
    lost,
    layers,
    blcol,
    oh_brick,
    flow_out,
    heat_out,
    brick_out,
    heat,
    flat,
    spread,
    sems,
):
    lane = iota((8, 128), 1)
    copies = []
    for n in range(4):
        part = pl.ds(n * 5, 5 if n < 3 else 4)
        copies.append(pltpu.make_async_copy(flow.at[part], flow_out.at[part], sems.at[3 + n]))
        copies[-1].start()
    store = Lattice(None, second_heat)

    @pl.loop(0, TILES // 4)
    def _(n):
        for u in range(4):
            t = n * 4 + u
            for xb in range(4):
                for j in range(7):
                    rows, lanes = natural(t, xb)
                    heat[j, rows, lanes] = pull(store, 19 + j, t, xb, lane)

    copies.append(pltpu.make_async_copy(heat, heat_out, sems.at[1]))
    copies[-1].start()
    fill_spread(blcol[...], lost[...], spread)
    loss = gather_spread(oh_brick, spread)
    from_rows(conduct(brick[...], layers[...], loss), flat)
    copies.append(pltpu.make_async_copy(flat, brick_out, sems.at[2]))
    copies[-1].start()
    for copy in copies:
        copy.wait()


def body(
    flow_pops,
    heat_pops,
    solid_flag,
    brick_temp,
    brick_ids,
    brick_links,
    face_cell,
    face_owner,
    face_spot,
):
    shape = jax.ShapeDtypeStruct
    dma = pltpu.SemaphoreType.DMA
    near = pl.BlockSpec(memory_space=pltpu.VMEM)
    far = pl.BlockSpec(memory_space=pltpu.HBM)
    grid = (TILES * ROWS, 128)
    inputs = (
        flow_pops,
        heat_pops,
        solid_flag,
        face_owner.reshape(1024, 128),
        face_spot.reshape(1024, 128),
        face_cell.reshape(1024, 128),
        brick_temp,
        brick_ids.reshape(2, 128),
        brick_links.T,
    )
    results = pl.pallas_call(
        steps_kernel,
        out_shape=[
            pltpu.VMEM(flow_pops.shape, F32),
            pltpu.VMEM((7, TALL, 128), F32),
            pltpu.VMEM((16, 128), F32),
            pltpu.VMEM((128, 128), F32),
            pltpu.VMEM((8, 128), F32),
            pltpu.VMEM((128, 128), I32),
            pltpu.VMEM((16, SLOTS), BF16),
        ],
        in_specs=[far] * 9,
        out_specs=[near] * 7,
        scratch_shapes=[
            pltpu.VMEM((26, TALL, 128), F32),
            pltpu.VMEM((19, TALL, 128), F32),
            pltpu.VMEM(flow_pops.shape, F32),
            pltpu.VMEM(heat_pops.shape, F32),
            pltpu.VMEM(solid_flag.shape, I32),
            pltpu.VMEM((1024, 128), I32),
            pltpu.VMEM((1024, 128), I32),
            pltpu.VMEM((8, 128), I32),
            pltpu.VMEM((2, 512), F32),
            pltpu.VMEM((2, 128), I32),
            pltpu.VMEM((6, 256), I32),
            pltpu.VMEM((8, 128, 128), F32),
            pltpu.VMEM((8, 128, 128), F32),
            pltpu.VMEM((128, 128), F32),
            pltpu.VMEM((128, 128), F32),
            pltpu.VMEM((128, 256), F32),
            pltpu.VMEM((256, 128), F32),
            pltpu.VMEM((192, 128), BF16),
            pltpu.VMEM((TILES * ROWS, SLOTS), BF16),
            pltpu.VMEM((96, SLOTS), BF16),
            pltpu.VMEM((CAP, 128), I32),
            pltpu.VMEM((CAP, 128), I32),
            pltpu.VMEM((128, 128), I32),
            pltpu.VMEM((CAP, 128), I32),
            pltpu.VMEM((CAP, 128), I32),
            pltpu.VMEM(grid, F32),
            pltpu.VMEM(grid, F32),
            pltpu.VMEM((96, 128), F32),
            pltpu.VMEM((SLOTS, 256), BF16),
            pltpu.VMEM((CAP, 128), F32),
            pltpu.VMEM((4, 128, 128), F32),
            pltpu.VMEM((8, 128), F32),
            pltpu.VMEM((4, 8 * 24, 128), F32),
            pltpu.VMEM((4, 8 * 24, 128), F32),
            pltpu.VMEM((4, 16 * 16, 128), F32),
            pltpu.VMEM((4, 16 * 16, 128), F32),
            pltpu.VMEM((2, 2, 80, 128), F32),
            pltpu.VMEM((2, 2, 80, 128), F32),
            pltpu.VMEM((2, 2, 64, 128), F32),
            pltpu.VMEM((2, 2, 64, 128), F32),
            pltpu.VMEM((2, 4, 8, 128), F32),
            pltpu.VMEM((2, 4, 8, 128), F32),
            pltpu.VMEM((2, 2, 16, 128), F32),
            pltpu.VMEM((2, 2, 16, 128), F32),
            pltpu.VMEM((2, 2, 32, 128), F32),
            pltpu.VMEM((2, 2, 32, 128), F32),
            dma((9,)),
            dma((4,)),
            dma((4,)),
            dma((4,)),
            dma((4,)),
            dma((2, 8)),
            dma((2, 8)),
            dma((2, 4)),
            dma((2, 4)),
        ],
        compiler_params=pltpu.CompilerParams(
            collective_id=0, has_side_effects=True, vmem_limit_bytes=46 << 20
        ),
    )(*(pltpu.with_memory_space_constraint(value, pltpu.HBM) for value in inputs))
    flow, heat, brick = pl.pallas_call(
        hand_out_kernel,
        out_shape=[
            shape(flow_pops.shape, F32),
            shape(heat_pops.shape, F32),
            shape(brick_temp.shape, F32),
        ],
        in_specs=[near] * 7,
        out_specs=[far] * 3,
        scratch_shapes=[
            pltpu.VMEM(heat_pops.shape, F32),
            pltpu.VMEM(brick_temp.shape, F32),
            pltpu.VMEM((SLOTS, 256), BF16),
            dma((7,)),
        ],
        compiler_params=pltpu.CompilerParams(vmem_limit_bytes=8 << 20),
    )(*results)
    return flow, heat, brick


def solution(mesh):
    return jax.shard_map(
        body,
        mesh=mesh,
        in_specs=(
            P(None, "gx", "gy"),
            P(None, "gx", "gy"),
            P("gx", "gy"),
            P(("gx", "gy"), None),
            P(),
            P(),
            P(),
            P(),
            P(),
        ),
        out_specs=(P(None, "gx", "gy"), P(None, "gx", "gy"), P(("gx", "gy"), None)),
        check_vma=False,
    )
```

```python
import functools

import jax
import jax.numpy as jnp
from jax import lax
from jax.experimental import pallas as pl
from jax.experimental.pallas import tpu as pltpu
from jax.sharding import PartitionSpec as P

MESH = pl.DeviceIdType.MESH
F32, BF16, I32 = jnp.float32, jnp.bfloat16, jnp.int32

VELOCITY = [
    (0, 0, 0),
    (1, 0, 0),
    (-1, 0, 0),
    (0, 1, 0),
    (0, -1, 0),
    (0, 0, 1),
    (0, 0, -1),
    (1, 1, 0),
    (-1, -1, 0),
    (1, -1, 0),
    (-1, 1, 0),
    (1, 0, 1),
    (-1, 0, -1),
    (1, 0, -1),
    (-1, 0, 1),
    (0, 1, 1),
    (0, -1, -1),
    (0, 1, -1),
    (0, -1, 1),
]
SIDE_SWAP = [1, 0, 3, 2, 5, 4]
WEIGHTS_HEAT = [0.25] + [0.125] * 6
TAU_FLOW, TAU_HEAT = 0.8, 0.9
BUOYANCY = 0.002
WALL_COEF = 0.1
BRICK_LOSS = 0.5
COND_BASE, COND_SLOPE = 0.04, 0.1
LATENT, MELT, MELT_WIDTH = 2.0, 4.0, 0.5

GX, GY = 16, 8
DEV = GX * GY
CAP = 16
ROWS, TILES, NZ = 32, 16, 32
PITCH = 48
TALL = (TILES + 2) * PITCH
SLOTS = CAP * DEV

ALL_VELOCITY = VELOCITY + VELOCITY[:7]
SIDES = [([9, 1, 11, 13, 7], 20), ([10, 2, 12, 14, 8], 21)]
SIDES += [([7, 3, 15, 17, 10], 22), ([8, 4, 16, 18, 9], 23)]
CORNERS = [(7, 1, 1), (8, -1, -1), (9, 1, -1), (10, -1, 1)]


def iota(shape, dim):
    return lax.broadcasted_iota(I32, shape, dim)


def lane_pick(rows, index):
    return jnp.take_along_axis(rows, index, axis=1, mode="promise_in_bounds")


def compact(get, key, val, packed):
    square = (128, 128)
    wide_row, wide_lane = iota((128, 256), 0), iota((128, 256), 1)
    prefix = jnp.where(wide_row <= wide_lane, 1.0, 0.0).astype(BF16)
    before = jnp.zeros(square, F32)
    for b in range(8):
        mask, value = get(b)
        counts = jnp.dot(
            jnp.where(mask, 1.0, 0.0).astype(BF16), prefix, preferred_element_type=F32
        )
        key[b] = jnp.where(mask, counts[:, :128] + before, 0.0)
        val[b] = value
        before = before + counts[:, 128:]

    @pl.loop(0, 4)
    def _(c):
        for u in range(4):
            rows = pl.ds(pl.multiple_of(c * 32 + u * 8, 8), 8)
            keys = [key[b, rows, :] for b in range(8)]
            vals = [val[b, rows, :] for b in range(8)]
            at = iota((8, 128), 1)
            out = jnp.zeros((8, 128), F32)
            for r in range(CAP):
                hit = jnp.zeros((8, 128), F32)
                for b in range(8):
                    hit = jnp.where(keys[b] == float(r + 1), vals[b], hit)
                out = jnp.where(at == r, jnp.sum(hit, axis=1, keepdims=True), out)
            packed[rows, :] = out

    return packed[...]


def compact_own(place, cell):
    square = (128, 128)
    wide_row, wide_lane = iota((128, 256), 0), iota((128, 256), 1)
    prefix = jnp.where(wide_row <= wide_lane, 1.0, 0.0).astype(BF16)
    device, rank = iota(square, 0), iota((CAP, 128), 0).astype(F32) + 1.0
    before = jnp.zeros(square, F32)
    masks, values = [], []
    for b in range(8):
        mask = device == place[b : b + 1, :]
        masks.append(jnp.where(mask, 1.0, 0.0).astype(BF16))
        counts = jnp.dot(masks[-1], prefix, preferred_element_type=F32)
        own = jnp.where(mask, counts[:, :128] + before, 0.0)
        before = before + counts[:, 128:]
        match = rank == jnp.sum(own, axis=0, keepdims=True)
        high = (cell[b : b + 1, :] >> 8).astype(F32)
        low = (cell[b : b + 1, :] & 255).astype(F32)
        both = [jnp.where(match, high, 0.0), jnp.where(match, low, 0.0)]
        values.append(jnp.concatenate(both, axis=0).astype(BF16))
    out = lax.dot_general(
        jnp.concatenate(values, axis=1),
        jnp.concatenate(masks, axis=1),
        (((1,), (1,)), ((), ())),
        preferred_element_type=F32,
    )
    return out[:CAP] * 256.0 + out[CAP:]


def split_cell(c):
    c = c.astype(I32) - 1
    live = c >= 0
    a = ((c >> 7) & 15) * ROWS + (c >> 11)
    return jnp.where(live, a, -1), c & 127, live


def split_spot(c):
    c = c.astype(I32) - 1
    live = c >= 0
    return jnp.where(live, c >> 6, -1), c & 63, live


def fill_onehots(row, onehot):
    count = onehot.shape[0]
    for r in range(CAP):
        for q in range(0, count, 128):
            size = min(128, count)
            part = iota((size, 128), 0) + q == row[r : r + 1, :]
            onehot[q : q + size, r * 128 : (r + 1) * 128] = jnp.where(part, 1.0, 0.0).astype(BF16)


def fill_edges(row, onehot):
    n = iota((96, 128), 0)
    last = n - 32 + (TILES - 1) * ROWS
    sides = jnp.where(n < 80, (n - 64) * ROWS, (n - 80) * ROWS + ROWS - 1)
    wanted = jnp.where(n < 32, n, jnp.where(n < 64, last, sides))
    for r in range(CAP):
        part = wanted == row[r : r + 1, :]
        onehot[:, r * 128 : (r + 1) * 128] = jnp.where(part, 1.0, 0.0).astype(BF16)


def ranked(device):
    return (((device >> 2) & 1) << 6) | ((device >> 4) << 3) | (((device >> 3) & 1) << 2) | (device & 3)


def fill_pick(spot, ids, links, wide, by_slot, pick):
    core, xc, ylo, q, inner, outer = spot
    order = jnp.concatenate([ids[0:1, :], ids[1:2, :]], axis=1)
    chosen = jnp.where(iota((256, 256), 0) == order, 1.0, 0.0).astype(BF16)
    wide[...] = jnp.zeros((128, 256), F32)
    wide[0:6, :] = jnp.dot(
        links.astype(F32).astype(BF16), chosen, preferred_element_type=F32
    )
    by_slot[0:128, :] = jnp.transpose(wide[:, 0:128])
    by_slot[128:256, :] = jnp.transpose(wide[:, 128:256])
    at, to = iota((16, 128), 1), iota((16, 128), 0)
    half = jnp.where(q >= 4, ids[1:2, :], ids[0:1, :])
    from_b, from_inner, side = at >> 6, (at >> 3) & 7, at & 7
    column = lax.rem(q, 4) * 32 + (from_inner >> 2) * 16 + ylo * 8 + (from_inner & 3) * 2 + from_b
    here = lane_pick(jnp.broadcast_to(half.astype(F32), (16, 128)), column)
    for b in range(2):
        named = jnp.concatenate(
            [
                by_slot[pl.ds((core * 8 + low * 4 + xc) * 2 + b, 8, stride=32), :]
                for low in range(2)
            ],
            axis=0,
        )
        for s in range(6):
            j = s * 2 + b
            n = named[:, s : s + 1]
            remote = (n == here) & (side == SIDE_SWAP[s])
            own = (n < 0.0) & (to == outer) & (at == b * 64 + inner * 8 + s)
            pick[j * 16 : (j + 1) * 16, :] = jnp.where(remote | own, 1.0, 0.0).astype(BF16)


def to_rows(brick):
    at = iota((1, 128), 1)
    rows = []
    for b in range(2):
        for x in range(8):
            part = brick[b : b + 1, (x // 2) * 128 : (x // 2 + 1) * 128]
            part = pltpu.roll(part, 64, 1) if x % 2 else part
            rows.append(jnp.where(at < 64, part, 0.0))
    return jnp.concatenate(rows, axis=0)


def from_rows(rows, out):
    turned = pltpu.roll(rows, 64, 1)
    at = iota((1, 128), 1)
    for b in range(2):
        for q in range(4):
            r = b * 8 + q * 2
            out[b : b + 1, q * 128 : (q + 1) * 128] = jnp.where(
                at < 64, rows[r : r + 1, :], turned[r + 1 : r + 2, :]
            )


def collide(f, g, solid):
    pairs = [(1, 2), (3, 4), (5, 6), (7, 8), (9, 10), (11, 12), (13, 14), (15, 16), (17, 18)]
    total = {a: f[a] + f[b] for a, b in pairs}
    diff = {a: f[a] - f[b] for a, b in pairs}
    density = f[0] + (
        (total[1] + total[3])
        + (total[5] + total[7])
        + (total[9] + total[11])
        + (total[13] + total[15])
        + total[17]
    )
    inverse = 1.0 / density
    ux = (diff[1] + diff[7] + diff[9] + diff[11] + diff[13]) * inverse
    uy = (diff[3] + diff[7] - diff[9] + diff[15] + diff[17]) * inverse
    uz = (diff[5] + diff[11] - diff[13] + diff[15] - diff[17]) * inverse
    temp = g[0] + ((g[1] + g[2]) + (g[3] + g[4]) + (g[5] + g[6]))
    sz = uz + (TAU_FLOW * BUOYANCY) * (temp - 1.0) * inverse
    base = 1.0 - 1.5 * (ux * ux + uy * uy + sz * sz)
    keep = 1.0 - 1.0 / TAU_FLOW
    along_of = {1: ux, 3: uy, 5: sz, 7: ux + uy, 9: ux - uy}
    along_of.update({11: ux + sz, 13: ux - sz, 15: uy + sz, 17: uy - sz})
    out_f = [None] * 19
    k0 = density * (1.0 / 3.0 / TAU_FLOW)
    out_f[0] = jnp.where(solid, f[0], keep * f[0] + k0 * base)
    scale = {1: density * (1.0 / 18.0 / TAU_FLOW), 7: density * (1.0 / 36.0 / TAU_FLOW)}
    level = {a: k * base for a, k in scale.items()}
    bend = {a: 4.5 * k for a, k in scale.items()}
    lean = {a: 3.0 * k for a, k in scale.items()}
    for a, b in pairs:
        kind = 1 if a < 7 else 7
        along = along_of[a]
        even = level[kind] + bend[kind] * (along * along)
        odd = lean[kind] * along
        out_f[a] = jnp.where(solid, f[b], (even + odd) + keep * f[a])
        out_f[b] = jnp.where(solid, f[a], (even - odd) + keep * f[b])
    keep = 1.0 - 1.0 / TAU_HEAT
    out_g = [None] * 7
    out_g[0] = jnp.where(solid, g[0], keep * g[0] + (0.25 / TAU_HEAT) * temp)
    k = (0.125 / TAU_HEAT) * temp
    for a, u in ((1, ux), (3, uy), (5, uz)):
        odd = (4.0 * k) * u
        out_g[a] = jnp.where(solid, g[a + 1], (k + odd) + keep * g[a])
        out_g[a + 1] = jnp.where(solid, g[a], (k - odd) + keep * g[a + 1])
    return out_f, out_g


class Lattice:
    def __init__(self, flow, heat):
        self.flow, self.heat = flow, heat

    def at(self, key):
        pop = key[0]
        if pop < 19:
            return self.flow, key
        return self.heat, (pop - 19,) + tuple(key[1:])

    def __getitem__(self, key):
        ref, key = self.at(key)
        return ref[key]

    def __setitem__(self, key, value):
        ref, key = self.at(key)
        ref[key] = value


def pull(store, pop, t, xb, lane):
    cx, cy, cz = ALL_VELOCITY[pop]
    at = pop

    def tile(step):
        return store[at, pl.ds((t + 1 + step) * PITCH + 8 + xb * 8 - cx, 8), :]

    here = tile(0)
    if cy == 1:
        here = jnp.where(lane >= 128 - NZ, tile(-1), here)
    if cy == -1:
        here = jnp.where(lane < NZ, tile(1), here)
    shift = (cy * NZ + cz) % 128
    if shift:
        here = pltpu.roll(here, shift, 1)
    if cz == 1:
        here = jnp.where(lane & (NZ - 1) == 0, 0.0, here)
    if cz == -1:
        here = jnp.where(lane & (NZ - 1) == NZ - 1, 0.0, here)
    return here


def own_rows(t, xb):
    return pl.ds((t + 1) * PITCH + 8 + xb * 8, 8)


def natural(t, xb):
    return pl.ds(xb * 8, 8), pl.ds(pl.multiple_of(t * 128, 128), 128)


def temp_rows(t, xb):
    return pl.ds(pl.multiple_of(t * ROWS + xb * 8, 8), 8)


def halves(value):
    high = value.astype(BF16)
    return high, (value - high.astype(F32)).astype(BF16)


def fill_spread(columns, flux, spread):
    high, low = halves(flux)
    high, low = high.astype(F32), low.astype(F32)
    at = iota((128, 128), 1)
    for r in range(CAP):
        hit = at == columns[:, r : r + 1]
        rows = slice(r * 128, (r + 1) * 128)
        spread[rows, 0:128] = jnp.where(hit, high[:, r : r + 1], 0.0).astype(BF16)
        spread[rows, 128:256] = jnp.where(hit, low[:, r : r + 1], 0.0).astype(BF16)


def gather_spread(onehot, spread):
    both = jnp.dot(onehot[...], spread[...], preferred_element_type=F32)
    return both[:, :128] + both[:, 128:]


def brick_lookup(brick, brow, blrow):
    out = jnp.zeros((CAP, 128), F32)
    for a in range(16):
        row = jnp.broadcast_to(brick[a : a + 1, :], (CAP, 128))
        out = jnp.where(brow == a, lane_pick(row, blrow), out)
    return out


def store_faces(brick, faces):
    at, row = iota((16, 128), 1), iota((16, 128), 0)
    line = iota((1, 128), 1)
    mine = ((at >> 3) & 7) == (row & 7)
    wanted = {
        2: at & 7,
        3: 56 + (at & 7),
        4: (at & 7) * 8,
        5: (at & 7) * 8 + 7,
    }
    faces[6:8, :] = jnp.zeros((2, 128), F32)
    for s in range(6):
        if s < 2:
            low, high = brick[7 * s : 7 * s + 1, :], brick[8 + 7 * s : 9 + 7 * s, :]
        else:
            got = jnp.where(mine, lane_pick(brick, wanted[s]), 0.0)
            low = jnp.sum(got[0:8], axis=0, keepdims=True)
            high = jnp.sum(got[8:16], axis=0, keepdims=True)
        faces[s : s + 1, :] = jnp.where(line < 64, low, pltpu.roll(high, 64, 1))


def conduct(brick, ghost, loss):
    at, row = iota((16, 128), 1), iota((16, 128), 0)
    x = row & 7

    other_brick = pltpu.roll(ghost, 64, 1)

    def ghost_rows(s):
        return jnp.where(row < 8, ghost[s : s + 1, :], other_brick[s : s + 1, :])

    over_z = x * 8 + (at & 7)
    over_y = x * 8 + ((at >> 3) & 7)
    beside = [
        jnp.where(x == 0, ghost_rows(0), pltpu.roll(brick, 1, 0)),
        jnp.where(x == 7, ghost_rows(1), pltpu.roll(brick, 15, 0)),
        jnp.where(at < 8, lane_pick(ghost_rows(2), over_z), pltpu.roll(brick, 8, 1)),
        jnp.where(at >= 56, lane_pick(ghost_rows(3), over_z), pltpu.roll(brick, 120, 1)),
        jnp.where((at & 7) == 0, lane_pick(ghost_rows(4), over_y), pltpu.roll(brick, 1, 1)),
        jnp.where((at & 7) == 7, lane_pick(ghost_rows(5), over_y), pltpu.roll(brick, 127, 1)),
    ]
    here = COND_BASE * (1.0 + COND_SLOPE * brick)
    spread = jnp.zeros((16, 128), F32)
    for other in beside:
        spread += 0.5 * (here + COND_BASE * (1.0 + COND_SLOPE * other)) * (other - brick)
    phase = 1.0 / (1.0 + jnp.exp(-(brick - MELT) / MELT_WIDTH))
    capacity = 1.0 + LATENT * phase * (1.0 - phase) / MELT_WIDTH
    return jnp.where(at < 64, brick + (spread - BRICK_LOSS * loss) / capacity, 0.0)


def steps_kernel(
    flow_in,
    heat_in,
    solid_in,
    owners_in,
    spots_in,
    cells_in,
    brick_in,
    ids_in,
    links_in,
    flow_out,
    second_heat,
    brick,
    lost,
    layers,
    blcol,
    oh_brick,
    first,
    second_flow,
    flow,
    heat,
    solid,
    owners,
    spots,
    cells,
    own_owners,
    brick_flat,
    ids,
    links,
    key,
    val,
    packed,
    reordered,
    wide,
    by_slot,
    pick,
    oh_cell,
    oh_edge,
    arow,
    lrow,
    lcol,
    brow,
    blrow,
    temps,
    gain,
    edge,
    spread,
    found,
    msg,
    faces,
    s1,
    r1,
    s2,
    r2,
    xf,
    xfr,
    yf,
    yfr,
    cf,
    cfr,
    xh,
    xhr,
    yh,
    yhr,
    load_sem,
    s1_send,
    s1_recv,
    s2_send,
    s2_recv,
    flow_send,
    flow_recv,
    heat_send,
    heat_recv,
):
    x, y = lax.axis_index("gx"), lax.axis_index("gy")
    me = x * GY + y
    core, q = lax.rem(x, 2), x // 2
    xc, ylo = lax.rem(y, 4), y // 4
    inner, outer = core * 4 + xc, ylo * 8 + q

    def inner_peer(i):
        return (q * 2 + i // 4, ylo * 4 + lax.rem(i, 4))

    def outer_peer(h):
        return (lax.rem(h, 8) * 2 + core, (h // 8) * 4 + xc)

    def inner_next(k):
        return lax.rem(inner + k, 8)

    def outer_next(k):
        return lax.rem(outer + k, 16)

    def xn(k):
        return lax.rem(x + (k + GX), GX)

    def yn(k):
        return lax.rem(y + (k + GY), GY)

    second = Lattice(second_flow, second_heat)
    own_faces = pl.ds(pl.multiple_of(me * 8, 8), 8)
    loads = {}
    for n, (name, source, target) in enumerate(
        (
            ("own", owners_in.at[own_faces, :], own_owners),
            ("cells", cells_in.at[own_faces, :], cells),
            ("heat", heat_in, heat),
            ("owners", owners_in, owners),
            ("spots", spots_in, spots),
            ("brick", brick_in, brick_flat),
            ("ids", ids_in, ids),
            ("links", links_in, links),
            ("solid", solid_in, solid),
            ("flow", flow_in, flow),
        )
    ):
        loads[name] = pltpu.make_async_copy(source, target, load_sem.at[n])
        if name not in ("solid", "flow"):
            loads[name].start()

    barrier = pltpu.get_barrier_semaphore()
    peers = [(xn(a), yn(b)) for a in (-1, 1) for b in (-1, 1)]
    peers += [outer_peer(outer_next(k)) for k in (10, 6, 2, 14, 9, 11, 5, 7, 1, 3, 13, 15, 8, 4, 12)]
    peers += [(xn(a), yn(b)) for a, b in ((-1, 0), (1, 0), (0, -1), (0, 1))]
    peers += [inner_peer(inner_next(k)) for k in range(1, 8)]
    for peer in peers:
        pl.semaphore_signal(barrier, inc=1, device_id=peer, device_id_type=MESH)

    lane = iota((8, 128), 1)


    def look_up_row(row, outs, u, a, low):
        line = jnp.broadcast_to(temps[pl.ds(row, 1), :], (CAP, 128))
        outs[u % 4] = jnp.where(a == row, lane_pick(line, low), outs[u % 4])

    def look_up(inner_only):
        parts = []
        for n in range(4):
            part = temps[n * 128 : (n + 1) * 128, :]
            if inner_only:
                row = iota((128, 128), 0)
                away = (row & 31 != 0) & (row & 31 != 31)
                if n == 0:
                    away = away & (row >= 32)
                if n == 3:
                    away = away & (row < 96)
                part = jnp.where(away, part, 0.0)
            parts.append(jnp.transpose(part))
        high, low = halves(jnp.concatenate(parts, axis=1))
        both = jnp.concatenate([high, low], axis=0)
        lanes = lrow[...]
        at = iota((128, 128), 0)
        for r in range(0, CAP, 2):
            got = jnp.dot(
                both, oh_cell[:, r * 128 : (r + 2) * 128], preferred_element_type=F32
            )
            got = got[:128] + got[128:]
            for u in range(2):
                hit = jnp.where(
                    at == lanes[r + u : r + u + 1, :], got[:, u * 128 : (u + 1) * 128], 0.0
                )
                found[r + u : r + u + 1, :] = jnp.sum(hit, axis=0, keepdims=True)

    def look_up_edges():
        a, low = arow[...], lrow[...]
        outs = [jnp.zeros((CAP, 128), F32)] * 4
        rows = [t * ROWS + row for t in range(1, TILES - 1) for row in (0, ROWS - 1)]
        rows += [t * ROWS + row for t in (0, TILES - 1) for row in range(ROWS)]
        for u, row in enumerate(rows):
            look_up_row(row, outs, u, a, low)
        return (outs[0] + outs[1]) + (outs[2] + outs[3])

    def fill_message(n, value):
        rest = jnp.zeros((128 - CAP, 128), F32)
        msg[n] = jnp.transpose(jnp.concatenate([value, rest], axis=0))

    def ask_bricks(n):
        fill_message(n, brick_lookup(brick[...], brow[...], blrow[...]))


    def wait_all(buffer, n, rows, sem):
        part = buffer.at[n, pl.ds(0, rows), :]
        pltpu.make_async_copy(part, part, sem.at[n]).wait()

    def one(n, to, slot):
        count = 16 if n % 2 else 24
        return pltpu.make_async_remote_copy(
            src_ref=s1.at[n, pl.ds(pl.multiple_of(to * 24, 8), count), :],
            dst_ref=r1.at[n, pl.ds(pl.multiple_of(slot * 24, 8), count), :],
            send_sem=s1_send.at[n],
            recv_sem=s1_recv.at[n],
            device_id=inner_peer(to),
            device_id_type=MESH,
        )

    def two(n, to, slot):
        count = 8 if n % 2 else 16
        return pltpu.make_async_remote_copy(
            src_ref=s2.at[n, pl.ds(pl.multiple_of(to * 16, 8), count), :],
            dst_ref=r2.at[n, pl.ds(pl.multiple_of(slot * 16, 8), count), :],
            send_sem=s2_send.at[n],
            recv_sem=s2_recv.at[n],
            device_id=outer_peer(to),
            device_id_type=MESH,
        )

    def start_one(n):
        for k in range(8):
            s1[n, k * 24 : k * 24 + 16, :] = msg[n, pl.ds(k, 16, stride=8), :]
            if n % 2 == 0:
                s1[n, k * 24 + 16 : k * 24 + 24, :] = faces[...]
        for k in range(1, 8):
            one(n, inner_next(k), inner).start()
        own = pl.ds(pl.multiple_of(inner * 24, 8), 24)
        r1[n, own, :] = s1[n, own, :]

    def end_one(n):
        wait_all(r1, n, 7 * (16 if n % 2 else 24), s1_recv)

    def start_two(n):
        if n % 2 == 0:
            every = jnp.concatenate(
                [r1[n, k * 24 + 16 : k * 24 + 24, :] for k in range(8)], axis=0
            )
            every = jnp.concatenate([every, pltpu.roll(every, 64, 1)], axis=0)
            high = every.astype(BF16)
            low = every - high.astype(F32)
            at = iota((128, 128), 1)
            both = jnp.where(at < 64, high.astype(F32), pltpu.roll(low, 64, 1)).astype(BF16)
            picked = jnp.dot(pick[...], both, preferred_element_type=F32)
            picked = picked + pltpu.roll(picked, 64, 1)
            at = iota((16, 128), 1)
            for s in range(8):
                pair = jnp.zeros((16, 128), F32)
                if s < 6:
                    top = s * 32
                    pair = jnp.where(at < 64, picked[top : top + 16], picked[top + 16 : top + 32])
                s2[n, pl.ds(8 + s, 16, stride=16), :] = pair
        for h in range(16):
            s2[n, h * 16 : h * 16 + 8, :] = r1[n, pl.ds(h, 8, stride=24), :]
        for k in range(1, 16):
            two(n, outer_next(k), outer).start()
        own = pl.ds(pl.multiple_of(outer * 16, 8), 16)
        r2[n, own, :] = s2[n, own, :]

    def end_two(n):
        wait_all(r2, n, 15 * (8 if n % 2 else 16), s2_recv)

    def end_sends(n):
        wait_all(s1, n, 7 * (16 if n % 2 else 24), s1_send)
        wait_all(s2, n, 15 * (8 if n % 2 else 16), s2_send)

    def arrived(n):
        return jnp.concatenate([r2[n, h * 16 : h * 16 + 8, :] for h in range(16)], axis=0)

    def heat_sides(bricks, fluid):
        fill_spread(lcol[...], WALL_COEF * (arrived(bricks) - msg[fluid]), spread)
        edge[...] = gather_spread(oh_edge, spread)

    def heat_faces(store):
        gain[...] = gather_spread(oh_cell, spread)

        @pl.loop(0, TILES)
        def _(t):
            for xb in range(4):
                more = gain[temp_rows(t, xb), :]
                rows = own_rows(t, xb)
                for j in range(7):
                    store[19 + j, rows, :] = store[19 + j, rows, :] + WEIGHTS_HEAT[j] * more

    def ghosts(n):
        ghost = r2[n, 8:16, :]
        for h in range(1, 16):
            ghost = ghost + r2[n, h * 16 + 8 : h * 16 + 16, :]
        return ghost

    def cool_bricks(bricks, fluid, layers):
        fill_spread(blcol[...], WALL_COEF * (msg[bricks] - arrived(fluid)), spread)
        loss = gather_spread(oh_brick, spread)
        brick[...] = conduct(brick[...], ghosts(layers), loss)


    ways = [(1, 0), (-1, 0), (0, 1), (0, -1)]
    inside = {(1, 0): x > 0, (-1, 0): x < GX - 1, (0, 1): y > 0, (0, -1): y < GY - 1}
    leave_row, leave_tile = (39, 8), (TILES, 1)
    enter_row, enter_tile = (7, 40), (0, TILES + 1)
    edge_lane = (128 - NZ, 0)

    def plan_copies(step, plan, send, recv):
        return [
            pltpu.make_async_remote_copy(
                src_ref=source,
                dst_ref=target,
                send_sem=send.at[step, n],
                recv_sem=recv.at[step, n],
                device_id=peer,
                device_id_type=MESH,
            )
            for n, (source, target, peer) in enumerate(plan)
        ]

    def flow_copies(step):
        plan = []
        for n, (dx, dy) in enumerate(ways):
            source, target = (xf, xfr) if n < 2 else (yf, yfr)
            plan.append((source.at[step, n % 2], target.at[step, n % 2], (xn(dx), yn(dy))))
        for c, (_, dx, dy) in enumerate(CORNERS):
            plan.append((cf.at[step, c], cfr.at[step, c], (xn(dx), yn(dy))))
        return plan_copies(step, plan, flow_send, flow_recv)

    def heat_copies(step):
        plan = []
        for n, (dx, dy) in enumerate(ways):
            source, target = (xh, xhr) if n < 2 else (yh, yhr)
            plan.append((source.at[step, n % 2], target.at[step, n % 2], (xn(dx), yn(dy))))
        return plan_copies(step, plan, heat_send, heat_recv)

    def send_flow_halo(step, store):
        for n in range(2):
            for k, pop in enumerate(SIDES[n][0]):
                rows = pl.ds(PITCH + leave_row[n], 16, stride=PITCH)
                xf[step, n, k * 16 : (k + 1) * 16, :] = store[pop, rows, :]
        at = iota((32, 128), 1)
        for n in range(2):
            top = leave_tile[n] * PITCH + 8
            parts = []
            for k, pop in enumerate(SIDES[2 + n][0]):
                turn = ((k % 4) * NZ - edge_lane[n]) % 128
                part = store[pop, top : top + 32, :]
                parts.append(pltpu.roll(part, turn, 1) if turn else part)
            for k in range(1, 4):
                parts[0] = jnp.where(at >= k * NZ, parts[k], parts[0])
            yf[step, n, 0:32, :] = parts[0]
            yf[step, n, 32:64, :] = parts[4]
        for c, (pop, dx, dy) in enumerate(CORNERS):
            row = leave_tile[dy < 0] * PITCH + leave_row[dx < 0]
            cf[step, c] = jnp.broadcast_to(store[pop, row : row + 1, :], (8, 128))
        for copy in flow_copies(step):
            copy.start()

    def end_flow_halo(step, store):
        for copy in flow_copies(step):
            copy.wait()
        for n in range(2):
            for k, pop in enumerate(SIDES[n][0]):
                rows = pl.ds(PITCH + enter_row[n], 16, stride=PITCH)
                store[pop, rows, :] = jnp.where(
                    inside[ways[n]], xfr[step, n, k * 16 : (k + 1) * 16, :], 0.0
                )
        for n in range(2):
            top = enter_tile[n] * PITCH + 8
            for k, pop in enumerate(SIDES[2 + n][0]):
                part = yfr[step, n, (k // 4) * 32 : (k // 4 + 1) * 32, :]
                turn = (edge_lane[n] - (k % 4) * NZ) % 128
                part = pltpu.roll(part, turn, 1) if turn else part
                store[pop, top : top + 32, :] = jnp.where(inside[ways[2 + n]], part, 0.0)
        for c, (pop, dx, dy) in enumerate(CORNERS):
            row = enter_tile[dy < 0] * PITCH + enter_row[dx < 0]
            known = inside[(dx, 0)] & inside[(0, dy)]
            store[pop, row : row + 1, :] = jnp.where(known, cfr[step, c, 0:1, :], 0.0)

    def send_heat_halo(step, store):
        for n in range(2):
            rows = pl.ds(PITCH + leave_row[n], 16, stride=PITCH)
            more = WEIGHTS_HEAT[1] * edge[80 - 16 * n : 96 - 16 * n, :]
            xh[step, n] = store[SIDES[n][1], rows, :] + more
            top = leave_tile[n] * PITCH + 8
            more = WEIGHTS_HEAT[1] * edge[32 - 32 * n : 64 - 32 * n, :]
            yh[step, n] = store[SIDES[2 + n][1], top : top + 32, :] + more
        for copy in heat_copies(step):
            copy.start()

    def end_heat_halo(step, store):
        for copy in heat_copies(step):
            copy.wait()
        for n in range(2):
            rows = pl.ds(PITCH + enter_row[n], 16, stride=PITCH)
            store[SIDES[n][1], rows, :] = jnp.where(inside[ways[n]], xhr[step, n], 0.0)
            top = enter_tile[n] * PITCH + 8
            store[SIDES[2 + n][1], top : top + 32, :] = jnp.where(
                inside[ways[2 + n]], yhr[step, n], 0.0
            )


    def store_relaxed(store, t, xb, f, g):
        out_f, out_g = collide(f, g, solid[natural(t, xb)] == 1)
        rows = own_rows(t, xb)
        for i, value in enumerate(out_f + out_g):
            store[i, rows, :] = value

    def relax_first(low, high):
        @pl.loop(low, high)
        def _(t):
            for xb in range(4):
                rows, lanes = natural(t, xb)
                f = [flow[i, rows, lanes] for i in range(19)]
                g = [heat[j, rows, lanes] for j in range(7)]
                store_relaxed(first, t, xb, f, g)

    def relax_second(t, xb):
        f = [pull(first, i, t, xb, lane) for i in range(19)]
        g = [pull(first, 19 + j, t, xb, lane) for j in range(7)]
        store_relaxed(second, t, xb, f, g)

    def hand_flow(t, xb):
        rows, lanes = natural(t, xb)
        for i in range(19):
            flow_out[i, rows, lanes] = pull(second, i, t, xb, lane)

    def along_sides(act):
        @pl.loop(0, (TILES - 2) // 2)
        def _(n):
            for u in range(2):
                for xb in (0, 3):
                    act(1 + 2 * n + u, xb)

        @pl.loop(0, 2)
        def _(n):
            for xb in range(4):
                act(n * (TILES - 1), xb)

    def inside_sides(act):
        @pl.loop(0, (TILES - 2) // 2)
        def _(n):
            for u in range(2):
                for xb in (1, 2):
                    act(1 + 2 * n + u, xb)

    def sum_heat(g):
        return g[0] + ((g[1] + g[2]) + (g[3] + g[4]) + (g[5] + g[6]))

    def pulled_temp(t, xb):
        temps[temp_rows(t, xb), :] = sum_heat([pull(first, 19 + j, t, xb, lane) for j in range(7)])


    loads["own"].wait()
    loads["cells"].wait()
    by_rank = compact_own(ranked(own_owners[...]), cells[...] + 1)
    table = jnp.transpose(
        jnp.concatenate([by_rank, jnp.zeros((128 - CAP, 128), F32)], axis=0)
    )
    _, low, live = split_cell(table)
    lcol[...] = jnp.where(live, low, -1)
    a, low, live = split_cell(by_rank)
    arow[...] = a
    lrow[...] = jnp.where(live, low, 0)


    loads["heat"].wait()
    loads["solid"].start()
    loads["flow"].start()

    @pl.loop(0, TILES // 2)
    def _(n):
        for u in range(2):
            for xb in range(4):
                rows, lanes = natural(n * 2 + u, xb)
                temps[temp_rows(n * 2 + u, xb), :] = sum_heat(
                    [heat[j, rows, lanes] for j in range(7)]
                )

    fill_onehots(arow[...], oh_cell)
    look_up(False)
    fill_message(0, found[...])
    loads["brick"].wait()
    brick[...] = to_rows(brick_flat[...])
    store_faces(brick[...], faces)
    pl.semaphore_wait(barrier, len(peers))
    start_one(0)

    loads["owners"].wait()
    loads["spots"].wait()

    def from_device(b):
        rows = pl.ds(b, 128, stride=8)
        return owners[rows, :] == me, spots[rows, :].astype(F32) + 1.0

    table = compact(from_device, key, val, packed)
    for n in range(32):
        source = ((n >> 1) & 7) * 16 + (n & 1) * 8 + (n >> 4) * 4
        reordered[n * 4 : n * 4 + 4, :] = packed[source : source + 4, :]
    table = reordered[...]
    _, low, live = split_spot(table)
    blcol[...] = jnp.where(live, low, -1)
    a, low, live = split_spot(jnp.transpose(table)[:CAP, :])
    brow[...] = a
    blrow[...] = jnp.where(live, low, 0)

    ask_bricks(1)
    start_one(1)
    loads["ids"].wait()
    loads["links"].wait()
    place = (core, xc, ylo, q, inner, outer)
    fill_pick(place, ids[...], links[...], wide, by_slot, pick)
    end_one(0)
    start_two(0)
    fill_onehots(brow[...], oh_brick)
    fill_edges(arow[...], oh_edge)
    loads["solid"].wait()
    loads["flow"].wait()
    relax_first(0, 2)
    end_one(1)
    start_two(1)
    relax_first(2, TILES)
    send_flow_halo(0, first)
    end_two(0)
    cool_bricks(1, 0, 0)
    store_faces(brick[...], faces)
    ask_bricks(2)
    start_one(2)
    end_two(1)
    heat_sides(1, 0)
    send_heat_halo(0, first)
    heat_faces(first)


    @pl.loop(0, (TILES - 2) // 2)
    def _(n):
        for u in range(2):
            for xb in range(4):
                pulled_temp(1 + 2 * n + u, xb)

    end_one(2)
    start_two(2)
    look_up(True)
    end_heat_halo(0, first)
    for t in range(TILES):
        for xb in range(4):
            if t in (0, TILES - 1) or xb in (0, 3):
                pulled_temp(t, xb)
    fill_message(3, found[...] + look_up_edges())
    start_one(3)
    end_flow_halo(0, first)
    along_sides(relax_second)
    end_one(3)
    start_two(3)
    send_flow_halo(1, second)
    inside_sides(relax_second)
    end_two(2)
    heat_sides(2, 3)
    send_heat_halo(1, second)
    heat_faces(second)
    inside_sides(hand_flow)
    for n in range(3):
        end_sends(n)
    end_flow_halo(1, second)
    along_sides(hand_flow)
    layers[...] = ghosts(2)
    end_two(3)
    lost[...] = WALL_COEF * (msg[2] - arrived(3))
    end_sends(3)
    end_heat_halo(1, second)


def hand_out_kernel(
    flow,
    second_heat,
    brick,
    lost,
    layers,
    blcol,
    oh_brick,
    flow_out,
    heat_out,
    brick_out,
    heat,
    flat,
    spread,
    sems,
):
    lane = iota((8, 128), 1)
    copies = []
    for n in range(4):
        part = pl.ds(n * 5, 5 if n < 3 else 4)
        copies.append(pltpu.make_async_copy(flow.at[part], flow_out.at[part], sems.at[3 + n]))
        copies[-1].start()
    store = Lattice(None, second_heat)

    @pl.loop(0, TILES // 4)
    def _(n):
        for u in range(4):
            t = n * 4 + u
            for xb in range(4):
                for j in range(7):
                    rows, lanes = natural(t, xb)
                    heat[j, rows, lanes] = pull(store, 19 + j, t, xb, lane)

    copies.append(pltpu.make_async_copy(heat, heat_out, sems.at[1]))
    copies[-1].start()
    fill_spread(blcol[...], lost[...], spread)
    loss = gather_spread(oh_brick, spread)
    from_rows(conduct(brick[...], layers[...], loss), flat)
    copies.append(pltpu.make_async_copy(flat, brick_out, sems.at[2]))
    copies[-1].start()
    for copy in copies:
        copy.wait()


def body(
    flow_pops,
    heat_pops,
    solid_flag,
    brick_temp,
    brick_ids,
    brick_links,
    face_cell,
    face_owner,
    face_spot,
):
    shape = jax.ShapeDtypeStruct
    dma = pltpu.SemaphoreType.DMA
    near = pl.BlockSpec(memory_space=pltpu.VMEM)
    far = pl.BlockSpec(memory_space=pltpu.HBM)
    grid = (TILES * ROWS, 128)
    inputs = (
        flow_pops,
        heat_pops,
        solid_flag,
        face_owner.reshape(1024, 128),
        face_spot.reshape(1024, 128),
        face_cell.reshape(1024, 128),
        brick_temp,
        brick_ids.reshape(2, 128),
        brick_links.T,
    )
    results = pl.pallas_call(
        steps_kernel,
        out_shape=[
            pltpu.VMEM(flow_pops.shape, F32),
            pltpu.VMEM((7, TALL, 128), F32),
            pltpu.VMEM((16, 128), F32),
            pltpu.VMEM((128, 128), F32),
            pltpu.VMEM((8, 128), F32),
            pltpu.VMEM((128, 128), I32),
            pltpu.VMEM((16, SLOTS), BF16),
        ],
        in_specs=[far] * 9,
        out_specs=[near] * 7,
        scratch_shapes=[
            pltpu.VMEM((26, TALL, 128), F32),
            pltpu.VMEM((19, TALL, 128), F32),
            pltpu.VMEM(flow_pops.shape, F32),
            pltpu.VMEM(heat_pops.shape, F32),
            pltpu.VMEM(solid_flag.shape, I32),
            pltpu.VMEM((1024, 128), I32),
            pltpu.VMEM((1024, 128), I32),
            pltpu.VMEM((8, 128), I32),
            pltpu.VMEM((8, 128), I32),
            pltpu.VMEM((2, 512), F32),
            pltpu.VMEM((2, 128), I32),
            pltpu.VMEM((6, 256), I32),
            pltpu.VMEM((8, 128, 128), F32),
            pltpu.VMEM((8, 128, 128), F32),
            pltpu.VMEM((128, 128), F32),
            pltpu.VMEM((128, 128), F32),
            pltpu.VMEM((128, 256), F32),
            pltpu.VMEM((256, 128), F32),
            pltpu.VMEM((192, 128), BF16),
            pltpu.VMEM((TILES * ROWS, SLOTS), BF16),
            pltpu.VMEM((96, SLOTS), BF16),
            pltpu.VMEM((CAP, 128), I32),
            pltpu.VMEM((CAP, 128), I32),
            pltpu.VMEM((128, 128), I32),
            pltpu.VMEM((CAP, 128), I32),
            pltpu.VMEM((CAP, 128), I32),
            pltpu.VMEM(grid, F32),
            pltpu.VMEM(grid, F32),
            pltpu.VMEM((96, 128), F32),
            pltpu.VMEM((SLOTS, 256), BF16),
            pltpu.VMEM((CAP, 128), F32),
            pltpu.VMEM((4, 128, 128), F32),
            pltpu.VMEM((8, 128), F32),
            pltpu.VMEM((4, 8 * 24, 128), F32),
            pltpu.VMEM((4, 8 * 24, 128), F32),
            pltpu.VMEM((4, 16 * 16, 128), F32),
            pltpu.VMEM((4, 16 * 16, 128), F32),
            pltpu.VMEM((2, 2, 80, 128), F32),
            pltpu.VMEM((2, 2, 80, 128), F32),
            pltpu.VMEM((2, 2, 64, 128), F32),
            pltpu.VMEM((2, 2, 64, 128), F32),
            pltpu.VMEM((2, 4, 8, 128), F32),
            pltpu.VMEM((2, 4, 8, 128), F32),
            pltpu.VMEM((2, 2, 16, 128), F32),
            pltpu.VMEM((2, 2, 16, 128), F32),
            pltpu.VMEM((2, 2, 32, 128), F32),
            pltpu.VMEM((2, 2, 32, 128), F32),
            dma((10,)),
            dma((4,)),
            dma((4,)),
            dma((4,)),
            dma((4,)),
            dma((2, 8)),
            dma((2, 8)),
            dma((2, 4)),
            dma((2, 4)),
        ],
        compiler_params=pltpu.CompilerParams(
            collective_id=0, has_side_effects=True, vmem_limit_bytes=46 << 20
        ),
    )(*(pltpu.with_memory_space_constraint(value, pltpu.HBM) for value in inputs))
    flow, heat, brick = pl.pallas_call(
        hand_out_kernel,
        out_shape=[
            shape(flow_pops.shape, F32),
            shape(heat_pops.shape, F32),
            shape(brick_temp.shape, F32),
        ],
        in_specs=[near] * 7,
        out_specs=[far] * 3,
        scratch_shapes=[
            pltpu.VMEM(heat_pops.shape, F32),
            pltpu.VMEM(brick_temp.shape, F32),
            pltpu.VMEM((SLOTS, 256), BF16),
            dma((7,)),
        ],
        compiler_params=pltpu.CompilerParams(vmem_limit_bytes=8 << 20),
    )(*results)
    return flow, heat, brick


def solution(mesh):
    return jax.shard_map(
        body,
        mesh=mesh,
        in_specs=(
            P(None, "gx", "gy"),
            P(None, "gx", "gy"),
            P("gx", "gy"),
            P(("gx", "gy"), None),
            P(),
            P(),
            P(),
            P(),
            P(),
        ),
        out_specs=(P(None, "gx", "gy"), P(None, "gx", "gy"), P(("gx", "gy"), None)),
        check_vma=False,
    )
```
